32 devices in a mesh: seq: 8 (over z, x), tp: 4 (over y, core).
Axes of the slice: x: 2, y: 2, z: 4, core: 2. Of those that a mesh axis runs over, the one named last changes fastest.
Arguments:
- tokens: bfloat16 [4, 1024, 768], P('tp', 'seq'), may hold values from -6 to 6
- norm_gain: float32 [768], replicated, may hold values from 0.5 to 1.5
- query_weight: bfloat16 [768, 768], replicated, may hold values from -0.21875 to 0.21875
- key_weight: bfloat16 [768, 768], replicated, may hold values from -0.21875 to 0.21875
- value_weight: bfloat16 [768, 768], replicated, may hold values from -0.21875 to 0.21875
- rate_weight: bfloat16 [768, 12], replicated, may hold values from -0.21875 to 0.21875
- rate_bias: float32 [12], P('tp'), may hold values from -2 to 1
- first_weight: float32 [12, 64, 256], P('tp'), may hold values from -0.75 to 0.75
- first_bias: float32 [12, 256], P('tp'), may hold values from -3 to 3
- second_weight: float32 [12, 256, 64], P('tp'), may hold values from -0.375 to 0.375
- second_bias: float32 [12, 64], P('tp'), may hold values from -3 to 3
- inner_gain: float32 [12, 64], P('tp'), may hold values from 0.25 to 1.75
- inner_bias: float32 [12, 64], P('tp'), may hold values from -3 to 3
- branch_gate: bfloat16 [768, 768], replicated, may hold values from -0.21875 to 0.21875
- output_weight: bfloat16 [768, 768], replicated, may hold values from -0.4375 to 0.4375
- post_gain: float32 [768], replicated, may hold values from 0.5 to 1.5
- post_bias: float32 [768], replicated, may hold values from -3 to 3
- feed_gain: float32 [768], replicated, may hold values from 0.5 to 1.5
- feed_gate: bfloat16 [768, 2048], P(None, 'tp'), may hold values from -0.21875 to 0.21875
- feed_linear: bfloat16 [768, 2048], P(None, 'tp'), may hold values from -0.21875 to 0.21875
- feed_down: bfloat16 [2048, 768], P('tp'), may hold values from -0.25 to 0.25
- cotangent: bfloat16 [4, 1024, 768], P('tp', 'seq'), may hold values from -6 to 6
Outputs:
- result: bfloat16 [4, 1024, 768], P('tp', 'seq')
- tokens_grad: float32 [4, 1024, 768], P('tp', 'seq')
- norm_gain_grad: float32 [768], replicated
- query_weight_grad: float32 [768, 768], replicated
- key_weight_grad: float32 [768, 768], replicated
- value_weight_grad: float32 [768, 768], replicated
- rate_weight_grad: float32 [768, 12], replicated
- rate_bias_grad: float32 [12], P('tp')
- first_weight_grad: float32 [12, 64, 256], P('tp')
- first_bias_grad: float32 [12, 256], P('tp')
- second_weight_grad: float32 [12, 256, 64], P('tp')
- second_bias_grad: float32 [12, 64], P('tp')
- inner_gain_grad: float32 [12, 64], P('tp')
- inner_bias_grad: float32 [12, 64], P('tp')
- branch_gate_grad: float32 [768, 768], replicated
- output_weight_grad: float32 [768, 768], replicated
- post_gain_grad: float32 [768], replicated
- post_bias_grad: float32 [768], replicated
- feed_gain_grad: float32 [768], replicated
- feed_gate_grad: float32 [768, 2048], P(None, 'tp')
- feed_linear_grad: float32 [768, 2048], P(None, 'tp')
- feed_down_grad: float32 [2048, 768], P('tp')
The draws below stay inside these ranges and needn't reach their ends.
All inputs are finite; a program needn't handle non-finite values.
Results may differ from the reference program's by a relative error of at most 0.028.
Values may be sent and summed in bfloat16 or wider, within the bound.
No kernel may reach another device: no remote copies, remote signals or barrier semaphores. Data moves between devices by JAX's collectives and lax.ppermute only.
A program may use at most 128 MiB of HBM per device.

```python
from functools import partial
import jax
import jax.numpy as jnp
from jax import lax

D = 768
HEADS = 12
HEAD = 64
INNER = 256
FF = 2048
MINI = 16
SEQS = 4
LENGTH = 1024


def block_scale(own_key, shape, split, least, largest):
    def one(position, shards_of):
        heights = jax.random.uniform(jax.random.fold_in(jax.random.fold_in(own_key, 6), position), (shards_of,), jnp.float32, least / len(split), largest / len(split))
        return jnp.repeat(jnp.exp(heights), shape[position] // shards_of).reshape((-1,) + (1,) * (len(shape) - position - 1))

    factor_of = one(*split[0])
    for cut in split[1:]:
        factor_of = factor_of * one(*cut)
    return factor_of


def centred(key, extent, spread, limit, shards=(), held_as=jnp.bfloat16):
    values = jax.random.normal(key, extent, jnp.float32) * spread
    if len(shards) > 0:
        values = block_scale(key, extent, shards, -0.22, 0.18) * values
    return jnp.clip(values, min=-limit, max=limit).astype(held_as)


def setup_inputs(seed: int = 0) -> dict:
    key_list = jax.random.split(jax.random.key(seed), 23)
    return {
        "tokens": centred(key_list[0], (SEQS, LENGTH, D), 1.0, 6.0, ((0, 4), (1, 8))),
        "norm_gain": jnp.clip(1.0 + 0.1 * jax.random.normal(key_list[1], (D,), jnp.float32), 0.5, 1.5),
        "query_weight": centred(key_list[2], (D, D), D ** -0.5, 0.21875),
        "key_weight": centred(key_list[3], (D, D), D ** -0.5, 0.21875),
        "value_weight": centred(key_list[4], (D, D), D ** -0.5, 0.21875),
        "rate_weight": centred(key_list[5], (D, HEADS), D ** -0.5, 0.21875),
        "rate_bias": jnp.clip(-2.0 + 3.0 * jax.random.uniform(key_list[6], (HEADS,), jnp.float32) ** block_scale(key_list[6], (HEADS,), ((0, 4),), -0.2, 0.2), -2.0, 1.0),
        "first_weight": centred(key_list[7], (HEADS, HEAD, INNER), HEAD ** -0.5, 0.75, ((0, 4),), jnp.float32),
        "first_bias": centred(key_list[8], (HEADS, INNER), 0.3, 3.0, ((0, 4),), jnp.float32),
        "second_weight": centred(key_list[9], (HEADS, INNER, HEAD), INNER ** -0.5, 0.375, ((0, 4),), jnp.float32),
        "second_bias": centred(key_list[10], (HEADS, HEAD), 0.3, 3.0, ((0, 4),), jnp.float32),
        "inner_gain": jnp.clip(1.0 + 0.15 * jax.random.normal(key_list[11], (HEADS, HEAD), jnp.float32), 0.25, 1.75),
        "inner_bias": centred(key_list[12], (HEADS, HEAD), 0.3, 3.0, ((0, 4),), jnp.float32),
        "branch_gate": centred(key_list[13], (D, D), D ** -0.5, 0.21875),
        "output_weight": centred(key_list[14], (D, D), (D // 4) ** -0.5, 0.4375),
        "post_gain": jnp.clip(1.0 + 0.1 * jax.random.normal(key_list[15], (D,), jnp.float32), 0.5, 1.5),
        "post_bias": centred(key_list[16], (D,), 0.3, 3.0, (), jnp.float32),
        "feed_gain": jnp.clip(1.0 + 0.1 * jax.random.normal(key_list[17], (D,), jnp.float32), 0.5, 1.5),
        "feed_gate": centred(key_list[18], (D, FF), D ** -0.5, 0.21875, ((1, 4),)),
        "feed_linear": centred(key_list[19], (D, FF), D ** -0.5, 0.21875, ((1, 4),)),
        "feed_down": centred(key_list[20], (FF, D), (FF // 4) ** -0.5, 0.25, ((0, 4),)),
        "cotangent": centred(key_list[21], (SEQS, LENGTH, D), 1.0, 6.0, ((0, 4), (1, 8))),
    }


@jax.custom_vjp
def low(v):
    return lax.optimization_barrier(v.astype(jnp.bfloat16)).astype(jnp.float32)

@jax.custom_vjp
def low_back(v):
    return v

def low_keep(v):
    return (low(v), None)

def low_pass(kept, grad):
    return (grad,)

def back_keep(v):
    return (v, None)

def back_low(kept, grad):
    return (low(grad),)
low.defvjp(low_keep, low_pass)
low_back.defvjp(back_keep, back_low)
RATE_SCALE = 0.25
INNER_EPS = 1e-06
NORM_EPS = 1e-05
SLOPE_C = 0.7978845608028654
CUBIC = 0.044715

def smooth_act(value):
    return 0.5 * value * (1.0 + jnp.tanh(SLOPE_C * (value + CUBIC * value * value * value)))

def smooth_slope(value):
    tangent = jnp.tanh(SLOPE_C * (value + CUBIC * value * value * value))
    return 0.5 * (1.0 + tangent) + 0.5 * value * (1.0 - tangent * tangent) * SLOPE_C * (1.0 + 3.0 * CUBIC * value * value)

def product(spec, left, right):
    return jnp.einsum(spec, left, right, precision=lax.Precision.HIGHEST)

def row_norm(value):
    centre = value - lax.optimization_barrier(jnp.mean(value, -1, keepdims=True))
    scale = lax.rsqrt(lax.optimization_barrier(jnp.mean(centre * centre, -1, keepdims=True)) + INNER_EPS)
    return (centre * scale, scale)

def inner_step(gain, bias, state, block):
    first_w, first_b, second_w, second_b = state
    query, keys, values, rate = block
    size = keys.shape[-2]
    causal = jnp.tril(jnp.ones((size, size), jnp.float32))
    gain_row = gain[..., None, :]
    bias_row = bias[..., None, :]
    first_pre = product('...bp,...pi->...bi', keys, first_w) + first_b[..., None, :]
    first_act = smooth_act(first_pre)
    second_pre = product('...bi,...ip->...bp', first_act, second_w) + second_b[..., None, :]
    normed, scale = row_norm(second_pre)
    error = normed * gain_row + bias_row + keys - values
    grad_norm = error * gain_row
    second_grad = scale * (grad_norm - lax.optimization_barrier(jnp.mean(grad_norm, -1, keepdims=True)) - normed * lax.optimization_barrier(jnp.mean(grad_norm * normed, -1, keepdims=True)))
    first_grad = product('...bp,...ip->...bi', second_grad, second_w) * smooth_slope(first_pre)
    rate_cols = rate[..., None, :]
    weights_one = (product('...bp,...cp->...bc', query, keys) + 1.0) * causal * rate_cols
    query_first = product('...bp,...pi->...bi', query, first_w) + first_b[..., None, :] - product('...bc,...ci->...bi', weights_one, first_grad)
    query_act = smooth_act(query_first)
    weights_two = (product('...bi,...ci->...bc', query_act, first_act) + 1.0) * causal * rate_cols
    query_second = product('...bi,...ip->...bp', query_act, second_w) + second_b[..., None, :] - product('...bc,...cp->...bp', weights_two, second_grad)
    query_normed, unused = row_norm(query_second)
    outputs = query + query_normed * gain_row + bias_row
    scaled_first = first_grad * rate[..., None]
    scaled_second = second_grad * rate[..., None]
    first_w = first_w - product('...bp,...bi->...pi', keys, scaled_first)
    first_b = first_b - lax.optimization_barrier(jnp.sum(scaled_first, -2))
    second_w = second_w - product('...bi,...bp->...ip', first_act, scaled_second)
    second_b = second_b - lax.optimization_barrier(jnp.sum(scaled_second, -2))
    return ((first_w, first_b, second_w, second_b), outputs)

def blocks_of(array, lead, count, block):
    shaped = array.reshape(lead + (count, block) + array.shape[len(lead) + 1:])
    return jnp.moveaxis(shaped, len(lead), 0)

def inner_group(state, query, keys, values, rate, gain, bias, block):
    lead = query.shape[:-2]
    length = query.shape[-2]
    width = query.shape[-1]
    count = length // block
    stepper = jax.checkpoint(partial(inner_step, gain, bias))
    pieces = (blocks_of(query, lead, count, block), blocks_of(keys, lead, count, block), blocks_of(values, lead, count, block), blocks_of(rate, lead, count, block))
    state, outputs = lax.scan(stepper, state, pieces)
    outputs = jnp.moveaxis(outputs, 0, len(lead)).reshape(lead + (length, width))
    return (state, outputs)

def root_norm(value, gain):
    return value * lax.rsqrt(lax.optimization_barrier(jnp.mean(value * value, -1, keepdims=True)) + NORM_EPS) * gain

def layer_norm(value, gain, bias):
    centre = value - lax.optimization_barrier(jnp.mean(value, -1, keepdims=True))
    return centre * lax.rsqrt(lax.optimization_barrier(jnp.mean(centre * centre, -1, keepdims=True)) + NORM_EPS) * gain + bias

def project(value, weight):
    return jnp.einsum('...d,de->...e', value, weight, precision=lax.Precision.HIGHEST)

def one_sequence(params, tokens):
    norm_gain, query_weight, key_weight, value_weight, rate_weight, rate_bias, first_weight, first_bias, second_weight, second_bias, inner_gain, inner_bias, branch_gate, output_weight, post_gain, post_bias, feed_gain, feed_gate, feed_linear, feed_down = params
    length = tokens.shape[0]
    normed = low(root_norm(tokens, norm_gain))
    query = low_back(low(project(normed, query_weight)))
    keys = low_back(low(project(normed, key_weight)))
    values = low_back(low(project(normed, value_weight)))
    logits = low_back(low(project(normed, rate_weight)))
    gate_pre = low_back(project(normed, branch_gate))

    def heads(array):
        return array.reshape(length, HEADS, HEAD).transpose(1, 0, 2)
    rate = jnp.transpose(jax.nn.sigmoid(logits + rate_bias)) * (RATE_SCALE / HEAD)
    state = (first_weight, first_bias, second_weight, second_bias)
    unused, inner_out = inner_group(state, heads(query), heads(keys), heads(values), rate, inner_gain, inner_bias, MINI)
    mixed = low_back(low(inner_out.transpose(1, 0, 2).reshape(length, D)))
    branch_in = low(layer_norm(mixed, post_gain, post_bias) * smooth_act(gate_pre))
    middle = tokens + low_back(project(branch_in, output_weight))
    feed_in = low(root_norm(middle, feed_gain))
    gate_val = low_back(project(feed_in, feed_gate))
    linear_val = low_back(project(feed_in, feed_linear))
    hidden = low(jax.nn.silu(gate_val) * linear_val)
    return middle + low_back(project(hidden, feed_down))

def forward(tokens, *params):
    return lax.map(jax.checkpoint(partial(one_sequence, params)), tokens)

def reference(tokens, norm_gain, query_weight, key_weight, value_weight, rate_weight, rate_bias, first_weight, first_bias, second_weight, second_bias, inner_gain, inner_bias, branch_gate, output_weight, post_gain, post_bias, feed_gain, feed_gate, feed_linear, feed_down, cotangent):
    floats = [array.astype(jnp.float32) for array in (tokens, norm_gain, query_weight, key_weight, value_weight, rate_weight, rate_bias, first_weight, first_bias, second_weight, second_bias, inner_gain, inner_bias, branch_gate, output_weight, post_gain, post_bias, feed_gain, feed_gate, feed_linear, feed_down)]
    output, pull = jax.vjp(forward, *floats)
    grads = pull(cotangent.astype(jnp.float32))
    return (output.astype(jnp.bfloat16), grads[0], grads[1], grads[2], grads[3], grads[4], grads[5], grads[6], grads[7], grads[8], grads[9], grads[10], grads[11], grads[12], grads[13], grads[14], grads[15], grads[16], grads[17], grads[18], grads[19], grads[20])
```

```python
from functools import partial

import jax
import jax.numpy as jnp
from jax import lax
from jax.sharding import PartitionSpec as P
from jax.experimental import pallas as pl
from jax.experimental.pallas import tpu as pltpu
C0=0.7978845608028654;C1=0.044715
EPS=1e-6
B=16
CH=128
LOW=jnp.bfloat16
F=jnp.float32
def nn(a,b): return lax.dot_general(a.astype(LOW),b.astype(LOW),(((1,),(0,)),((),())),preferred_element_type=F)
def nt(a,b): return lax.dot_general(a.astype(LOW),b.astype(LOW),(((1,),(1,)),((),())),preferred_element_type=F)
def tn(a,b): return lax.dot_general(a.astype(LOW),b.astype(LOW),(((0,),(0,)),((),())),preferred_element_type=F)
def mean(x): return jnp.sum(x,-1,keepdims=True)*(1.0/x.shape[-1])
def gelu2(z):
    z2=z*z
    t=jnp.tanh(z*(C0+(C0*C1)*z2))
    h=0.5+0.5*t
    x=z*h
    g1=h+x*(1-t)*(C0+(3*C0*C1)*z2)
    return x,g1
def gelu1(z):
    z2=z*z
    return z*(0.5+0.5*jnp.tanh(z*(C0+(C0*C1)*z2)))
def iotas():
    r=lax.broadcasted_iota(jnp.int32,(CH,CH),0); c=lax.broadcasted_iota(jnp.int32,(CH,CH),1)
    return r,c

def fwd_kernel(C,q_ref,k_ref,v_ref,r_ref,w1_ref,b1_ref,u_ref,b2_ref,gam_ref,bet_ref,
               o_ref,z1_ref,p_ref,zc_ref,z1q_ref,zq_ref,us_ref,w1s_ref,
               W1,B1,U,B2,S1,S2,X2,KK,BASE,T):
    @pl.when(pl.program_id(0)==0)
    def _():
        W1[...]=w1_ref[...]; B1[...]=b1_ref[...]; U[...]=u_ref[...]; B2[...]=b2_ref[...]
        S1[...]=jnp.zeros_like(S1)
    H=64
    ri,ci=iotas()
    blk=(ci//B)<(ri//B)
    tri=ci<=ri
    K=[k_ref[:,H*c:H*c+H] for c in range(C)]
    Q=[q_ref[:,H*c:H*c+H] for c in range(C)]
    gam=[gam_ref[c] for c in range(C)]; bet=[bet_ref[c] for c in range(C)]
    R=[r_ref[:,c:c+1] for c in range(C)]
    w1b=[W1[c].astype(LOW) for c in range(C)]
    b1=[B1[c] for c in range(C)]
    u0=[U[c].astype(LOW) for c in range(C)]
    b20=[B2[c] for c in range(C)]
    g2=[gam[c]*gam[c] for c in range(C)]
    g2m=[mean(g2[c]) for c in range(C)]
    for c in range(C):
        w1s_ref[0,c]=w1b[c]
        KK[c]=jnp.where(blk,nt(K[c],K[c])+1.0,0.0).astype(LOW)
        BASE[c]=nn(K[c],w1b[c])+b1[c]
        T[c]=(bet[c]+K[c].astype(F)-v_ref[:,H*c:H*c+H].astype(F))*gam[c]
    ub=list(u0); uf=[U[c] for c in range(C)]; b2=list(b20)
    for j in range(CH//B):
        sl=slice(B*j,B*j+B)
        for c in range(C):
            z1=BASE[c,sl]
            if j>0: z1=z1-nn(KK[c,sl],S1[c])
            x2,g1=gelu2(z1)
            x2b=x2.astype(LOW)
            zc=nt(x2b,ub[c])+b2[c]
            mu=mean(zc); zz=zc*zc; t=T[c,sl]
            var=mean(zz)-mu*mu
            s=lax.rsqrt(var+EPS)
            zc=zc-mu
            y=zc*s
            G=y*g2[c]+t
            m1=mean(G); m2=mean(G*y)
            d2=s*(G-m1-y*m2)
            P=nn(d2,ub[c])
            rr=R[c][sl]
            s1=P*(g1*rr)
            s2=d2*rr
            s2b=s2.astype(LOW)
            S1[c,sl]=s1.astype(LOW); S2[c,sl]=s2b; X2[c,sl]=x2b
            z1_ref[c,sl]=z1; p_ref[c,sl]=P; zc_ref[c,sl]=zc
            us_ref[0,c,j]=ub[c]
            uf[c]=uf[c]-tn(s2b,x2b); ub[c]=uf[c].astype(LOW)
            b2[c]=b2[c]-jnp.sum(s2,0,keepdims=True)
    for c in range(C):
        U[c]=uf[c]; B2[c]=b2[c]
        W1[c]=W1[c]-tn(K[c],S1[c])
        B1[c]=B1[c]-jnp.sum(S1[c].astype(F),0,keepdims=True)
        A1=jnp.where(tri,nt(Q[c],K[c])+1.0,0.0)
        z1q=nn(Q[c],w1b[c])+b1[c]-nn(A1,S1[c])
        x2q=gelu1(z1q).astype(LOW)
        A2=jnp.where(tri,nt(x2q,X2[c])+1.0,0.0)
        zq=nt(x2q,u0[c])+b20[c]-nn(A2,S2[c])
        zq=zq-mean(zq)
        yq=zq*lax.rsqrt(mean(zq*zq)+EPS)
        o_ref[:,H*c:H*c+H]=(Q[c].astype(F)+yq*gam[c]+bet[c]).astype(LOW)
        z1q_ref[c]=z1q; zq_ref[c]=zq

def fwd_scan(q,k,v,r,w1,b1,u,b2,gam,bet):
    L=q.shape[0]; C=w1.shape[0]; I=w1.shape[2]; H=w1.shape[1]; n=L//CH
    row=lambda w,dt=None: pl.BlockSpec((CH,w),lambda i:(i,0))
    full=lambda *s: pl.BlockSpec(s,lambda i:(0,)*len(s))
    big=lambda w: pl.BlockSpec((C,CH,w),lambda i:(0,i,0))
    sd=jax.ShapeDtypeStruct
    return pl.pallas_call(partial(fwd_kernel,C),grid=(n,),
        in_specs=[row(C*H)]*3+[row(C),full(C,H,I),full(C,1,I),full(C,H,I),full(C,1,H),full(C,1,H),full(C,1,H)],
        out_specs=[row(C*H),big(I),big(I),big(H),big(I),big(H),pl.BlockSpec((1,C,CH//B,H,I),lambda i:(i,0,0,0,0)),pl.BlockSpec((1,C,H,I),lambda i:(i,0,0,0))],
        out_shape=[sd((L,C*H),LOW),sd((C,L,I),F),sd((C,L,I),F),sd((C,L,H),F),sd((C,L,I),F),sd((C,L,H),F),sd((n,C,CH//B,H,I),LOW),sd((n,C,H,I),LOW)],
        scratch_shapes=[pltpu.VMEM((C,H,I),F),pltpu.VMEM((C,1,I),F),pltpu.VMEM((C,H,I),F),pltpu.VMEM((C,1,H),F),
            pltpu.VMEM((C,CH,I),LOW),pltpu.VMEM((C,CH,H),LOW),pltpu.VMEM((C,CH,I),LOW),pltpu.VMEM((C,CH,CH),LOW),pltpu.VMEM((C,CH,I),F),pltpu.VMEM((C,CH,H),F)],
        compiler_params=pltpu.CompilerParams(vmem_limit_bytes=48*1024*1024),
    )(q,k,v,r,w1,b1,u,b2,gam,bet)

def gelu3(z):
    z2=z*z
    t=jnp.tanh(z*(C0+(C0*C1)*z2))
    u1=C0+(3*C0*C1)*z2
    h=0.5+0.5*t
    h1=h*(1-t)*u1
    x=z*h
    g1=h+z*h1
    g2=2*h1+z*(h*(1-t)*(6*C0*C1)*z-2*t*u1*h1)
    return x,g1,g2

def bwd_kernel(C,n,q_ref,k_ref,v_ref,r_ref,do_ref,z1_ref,p_ref,zc_ref,z1q_ref,zq_ref,us_ref,w1s_ref,gam_ref,bet_ref,
               dq_ref,dk_ref,dv_ref,dr_ref,H1,h1,HU,h2,dgam_ref,dbet_ref,
               BASE,DX2,X2,RG1,RPG2,DS2Q,KK,DZ1,DS1,DS2,DG,YB,GB,DB,SB,S2B,G1):
    @pl.when(pl.program_id(0)==0)
    def _():
        for ref in (H1,h1,HU,h2,dgam_ref,dbet_ref,DZ1): ref[...]=jnp.zeros_like(ref)
    H=64
    ri,ci=iotas()
    blk=(ci//B)<(ri//B)
    blkT=(ci//B)>(ri//B)
    tri=ci<=ri
    K=[k_ref[:,H*c:H*c+H] for c in range(C)]
    Q=[q_ref[:,H*c:H*c+H] for c in range(C)]
    gam=[gam_ref[c] for c in range(C)]; bet=[bet_ref[c] for c in range(C)]
    R=[r_ref[:,c:c+1] for c in range(C)]
    g2=[gam[c]*gam[c] for c in range(C)]
    hu=[HU[c] for c in range(C)]; hh2=[h2[c] for c in range(C)]
    keep=[]
    for c in range(C):
        dO=do_ref[:,H*c:H*c+H].astype(F)
        x2q,g1q=gelu2(z1q_ref[c]); x2q=x2q.astype(LOW)
        zq=zq_ref[c]; sq=lax.rsqrt(mean(zq*zq)+EPS); yq=zq*sq
        x2,g1,gg2=gelu3(z1_ref[c]); x2=x2.astype(LOW)
        X2[c]=x2
        P=p_ref[c]
        r=R[c]
        RG1[c]=r*g1; G1[c]=g1
        RPG2[c]=r*(P*gg2)
        s1=(P*g1*r).astype(LOW)
        zc=zc_ref[c]
        s=lax.rsqrt(mean(zc*zc)+EPS)
        y=zc*s
        t0=bet[c]+K[c].astype(F)-v_ref[:,H*c:H*c+H].astype(F)
        G=y*g2[c]+t0*gam[c]
        m1=mean(G); m2=mean(G*y)
        d2=s*(G-m1-y*m2)
        s2=(d2*r).astype(LOW)
        YB[c]=y; GB[c]=G; DB[c]=d2; S2B[c]=s2
        SB[c,:,0:1]=s; SB[c,:,1:2]=m2
        u0=us_ref[0,c,0]
        w1=w1s_ref[0,c]
        dgam_ref[c]=dgam_ref[c]+jnp.sum(dO*yq,0,keepdims=True)
        dbet_ref[c]=dbet_ref[c]+jnp.sum(dO,0,keepdims=True)
        dyq=dO*gam[c]
        dzq=sq*(dyq-mean(dyq)-yq*mean(dyq*yq))
        dzqb=dzq.astype(LOW)
        A2=jnp.where(tri,nt(x2q,x2)+1.0,0.0)
        dA2=jnp.where(tri,nt(dzqb,s2),0.0).astype(LOW)
        dx2q=nn(dzqb,u0)-nn(dA2,x2)
        DX2[c]=-tn(dA2,x2q)
        DS2Q[c]=-tn(A2,dzqb)
        dz1q=dx2q*g1q
        dz1qb=dz1q.astype(LOW)
        A1=jnp.where(tri,nt(Q[c],K[c])+1.0,0.0)
        dA1=jnp.where(tri,nt(dz1qb,s1),0.0).astype(LOW)
        dq_ref[:,H*c:H*c+H]=(dO+nt(dz1qb,w1)-nn(dA1,K[c])).astype(LOW)
        h1b=H1[c].astype(LOW)
        dk=nt(s1,h1b)+tn(dA1,Q[c])
        KK[c]=jnp.where(blkT,nt(K[c],K[c])+1.0,0.0).astype(LOW)
        BASE[c]=-tn(A1,dz1qb)-nn(K[c],h1b)-h1[c]
        h1n=h1[c]+jnp.sum(dz1q,0,keepdims=True)
        H1n=H1[c]+tn(Q[c],dz1qb)
        keep.append((s1,t0,dzqb,x2q,dk,H1n,h1n,w1,P*g1))
    for j in reversed(range(CH//B)):
        sl=slice(B*j,B*j+B)
        for c in range(C):
            ub=us_ref[0,c,j]
            rr=R[c][sl]
            hub=hu[c].astype(LOW)
            ds1=BASE[c,sl]
            if j<CH//B-1: ds1=ds1-nn(KK[c,sl],DZ1[c])
            x2=X2[c,sl]
            ds2=DS2Q[c,sl]-nt(x2,hub)-hh2[c]
            dx2=DX2[c,sl]-nn(S2B[c,sl],hub)
            dP=ds1*RG1[c,sl]
            dPb=dP.astype(LOW)
            e=rr*ds2+nt(dPb,ub)
            s=SB[c,sl,0:1]; m2=SB[c,sl,1:2]; y=YB[c,sl]; g_=GB[c,sl]; d2=DB[c,sl]
            a=mean(e); b=mean(e*y); cc=mean(e*d2)
            dG=s*(e-a-y*b)
            dY=g2[c]*dG-s*(m2*e+g_*b)
            dZc=s*(dY-mean(dY)-y*(cc+mean(dY*y)))
            dZcb=dZc.astype(LOW)
            dx2=dx2+nn(dZcb,ub)
            dz1=dx2*G1[c,sl]+ds1*RPG2[c,sl]
            DZ1[c,sl]=dz1.astype(LOW)
            DS1[c,sl]=ds1; DS2[c,sl]=ds2; DG[c,sl]=dG
            hu[c]=hu[c]+tn(jnp.concatenate([d2.astype(LOW),dZcb],0),jnp.concatenate([dPb,x2],0))
            hh2[c]=hh2[c]+jnp.sum(dZc,0,keepdims=True)
    for c in range(C):
        s1,t0,dzqb,x2q,dk,H1n,h1n,w1,D1=keep[c]
        dz1=DZ1[c]
        M=jnp.where(blk,nt(dz1,s1),0.0).astype(LOW)
        dG=DG[c]; dGg=dG*gam[c]
        dk=-dk-nn(M,K[c])-tn(M,K[c])+nt(dz1,w1)+dGg
        dk_ref[:,H*c:H*c+H]=dk.astype(LOW)
        dv_ref[:,H*c:H*c+H]=(-dGg).astype(LOW)
        dr_ref[:,c:c+1]=jnp.sum(DS1[c]*D1,-1,keepdims=True)+jnp.sum(DS2[c]*DB[c],-1,keepdims=True)
        dgam_ref[c]=dgam_ref[c]+jnp.sum(dG*(2*YB[c]*gam[c]+t0),0,keepdims=True)
        dbet_ref[c]=dbet_ref[c]+jnp.sum(dGg,0,keepdims=True)
        H1[c]=H1n+tn(K[c],dz1)
        h1[c]=h1n+jnp.sum(dz1.astype(F),0,keepdims=True)
        HU[c]=hu[c]+tn(dzqb,x2q)
        h2[c]=hh2[c]+jnp.sum(dzqb.astype(F),0,keepdims=True)

def bwd_scan(q,k,v,r,do,z1,p,zc,z1q,zq,us,w1s,gam,bet):
    L=q.shape[0]; C,_,I=z1.shape; H=zc.shape[2]; n=L//CH
    row=lambda w,dt=None: pl.BlockSpec((CH,w),lambda i:(n-1-i,0))
    full=lambda *s: pl.BlockSpec(s,lambda i:(0,)*len(s))
    big=lambda w: pl.BlockSpec((C,CH,w),lambda i:(0,n-1-i,0))
    sd=jax.ShapeDtypeStruct
    V=pltpu.VMEM
    return pl.pallas_call(partial(bwd_kernel,C,n),grid=(n,),
        in_specs=[row(C*H)]*3+[row(C),row(C*H),big(I),big(I),big(H),big(I),big(H),pl.BlockSpec((1,C,CH//B,H,I),lambda i:(n-1-i,0,0,0,0)),pl.BlockSpec((1,C,H,I),lambda i:(n-1-i,0,0,0)),full(C,1,H),full(C,1,H)],
        out_specs=[row(C*H)]*3+[row(C),full(C,H,I),full(C,1,I),full(C,H,I),full(C,1,H),full(C,1,H),full(C,1,H)],
        out_shape=[sd((L,C*H),LOW)]*3+[sd((L,C),F),sd((C,H,I),F),sd((C,1,I),F),sd((C,H,I),F),sd((C,1,H),F),sd((C,1,H),F),sd((C,1,H),F)],
        scratch_shapes=[V((C,CH,I),F),V((C,CH,I),F),V((C,CH,I),LOW),V((C,CH,I),F),V((C,CH,I),F),V((C,CH,H),F),V((C,CH,CH),LOW),V((C,CH,I),LOW),V((C,CH,I),F),V((C,CH,H),F),V((C,CH,H),F),
            V((C,CH,H),F),V((C,CH,H),F),V((C,CH,H),F),V((C,CH,2),F),V((C,CH,H),LOW),V((C,CH,I),F)],
        compiler_params=pltpu.CompilerParams(vmem_limit_bytes=48*1024*1024),
    )(q,k,v,r,do,z1,p,zc,z1q,zq,us,w1s,gam,bet)

RATE_SCALE = 0.25
NORM_EPS = 1e-05


def smooth_act(value):
    return 0.5 * value * (1.0 + jnp.tanh(C0 * (value + C1 * value * value * value)))


def root_norm(value, gain):
    return value * lax.rsqrt(jnp.mean(value * value, -1, keepdims=True) + NORM_EPS) * gain


def layer_norm(value, gain, bias):
    centre = value - jnp.mean(value, -1, keepdims=True)
    return centre * lax.rsqrt(jnp.mean(centre * centre, -1, keepdims=True) + NORM_EPS) * gain + bias


def gated_branch(mixed, gate_pre, gain, bias):
    return layer_norm(mixed, gain, bias) * smooth_act(gate_pre)


def swish_product(gate_val, linear_val):
    return jax.nn.silu(gate_val) * linear_val


def matmul(left, right):
    return jnp.dot(left, right, preferred_element_type=F)


def on_device(
    tokens, norm_gain, query_weight, key_weight, value_weight, rate_weight, rate_bias,
    first_weight, first_bias, second_weight, second_bias, inner_gain, inner_bias,
    branch_gate, output_weight, post_gain, post_bias, feed_gain, feed_gate, feed_linear,
    feed_down, cotangent,
):
    seqs = lax.axis_size("seq")
    rank = lax.axis_index("seq")
    heads = rate_weight.shape[1]
    local_heads, head, inner = first_weight.shape
    rows = tokens.shape[1]
    width = tokens.shape[2]
    each = -(-heads // seqs)
    span = each * head
    length = seqs * rows
    extra = -(-each // 16) * 16

    def to_chains(array):
        padded = jnp.pad(array, ((0, 0), (0, seqs * span - array.shape[1])))
        return padded.reshape(rows, seqs, span).transpose(1, 0, 2)

    def from_chains(array):
        return array.transpose(1, 0, 2).reshape(rows, seqs * span)[:, :width]

    def swap(array):
        return lax.all_to_all(array, "seq", split_axis=0, concat_axis=0, tiled=True)

    first_pack = jnp.concatenate([first_weight, first_bias[:, None, :]], 1)
    centred = jnp.swapaxes(second_weight, 1, 2)
    centred = centred - jnp.mean(centred, 1, keepdims=True)
    tail = jnp.concatenate(
        [
            second_bias - jnp.mean(second_bias, -1, keepdims=True),
            inner_gain,
            inner_bias,
            jnp.pad(rate_bias[:, None], ((0, 0), (0, inner - 3 * head - 1))),
        ],
        -1,
    )
    second_pack = jnp.concatenate([centred, tail[:, None, :]], 1)
    packed = jnp.pad(jnp.stack([first_pack, second_pack], 1), ((0, 0), (0, 0), (0, 7), (0, 0)))
    every = lax.all_gather(packed, "tp", axis=0, tiled=True)
    own = jnp.stack(
        [
            lax.dynamic_index_in_dim(every, jnp.minimum(rank * each + c, heads - 1), 0, keepdims=False)
            for c in range(each)
        ]
    )
    chain_first = own[:, 0, :head]
    chain_first_bias = own[:, 0, head : head + 1]
    chain_second = own[:, 1, :head]
    chain_tail = own[:, 1, head : head + 1]
    chain_second_bias = chain_tail[..., :head]
    chain_gain = chain_tail[..., head : 2 * head]
    chain_shift = chain_tail[..., 2 * head : 3 * head]
    chain_rate_bias = chain_tail[:, 0, 3 * head]

    residual = tokens[0].astype(F)
    normed_val, norm_pull = jax.vjp(root_norm, residual, norm_gain)
    normed = normed_val.astype(LOW)
    query_tok = matmul(normed, query_weight).astype(LOW)
    keys_tok = matmul(normed, key_weight).astype(LOW)
    values_tok = matmul(normed, value_weight).astype(LOW)
    logits_tok = matmul(normed, rate_weight).astype(LOW)
    gate_pre = matmul(normed, branch_gate)

    logit_rows = jnp.pad(logits_tok.T, ((0, seqs * each - heads), (0, 0))).reshape(seqs, each, rows)
    logit_rows = jnp.pad(logit_rows, ((0, 0), (0, extra - each), (0, 3 * span - rows)))
    sent = jnp.concatenate(
        [jnp.concatenate([to_chains(query_tok), to_chains(keys_tok), to_chains(values_tok)], -1), logit_rows],
        1,
    )
    got = swap(sent)
    chain_qkv = got[:, :rows].reshape(length, 3 * span)
    query_c = chain_qkv[:, :span]
    keys_c = chain_qkv[:, span : 2 * span]
    values_c = chain_qkv[:, 2 * span :]
    logit_c = got[:, rows : rows + each, :rows].transpose(0, 2, 1).reshape(length, each).astype(F)
    gate_c = jax.nn.sigmoid(logit_c + chain_rate_bias)
    rate_c = gate_c * (RATE_SCALE / head)

    outs, *kept = fwd_scan(
        query_c, keys_c, values_c, rate_c, chain_first, chain_first_bias, chain_second,
        chain_second_bias, chain_gain, chain_shift,
    )
    mixed_tok = from_chains(swap(outs.reshape(seqs, rows, span))).astype(F)

    branch_val, branch_pull = jax.vjp(gated_branch, mixed_tok, gate_pre, post_gain, post_bias)
    branch_in = branch_val.astype(LOW)
    middle = residual + matmul(branch_in, output_weight)
    feed_val, feed_pull = jax.vjp(root_norm, middle, feed_gain)
    feed_in = feed_val.astype(LOW)
    down_grad = cotangent[0]
    grad_out = down_grad.astype(F)
    every_grad = lax.all_gather(down_grad, "tp", axis=0, tiled=True)
    every_in = lax.all_gather(feed_in, "tp", axis=0, tiled=True)
    gate_val = matmul(every_in, feed_gate)
    linear_val = matmul(every_in, feed_linear)
    act_val, act_pull = jax.vjp(swish_product, gate_val, linear_val)
    hidden = act_val.astype(LOW)

    def sum_over_tp(array):
        parts = array.astype(LOW).reshape(lax.axis_size("tp"), rows, width)
        parts = lax.all_to_all(parts, "tp", split_axis=0, concat_axis=0, tiled=True)
        return jnp.sum(parts.astype(F), 0)

    hidden_grad = jnp.einsum("td,fd->tf", every_grad, feed_down, preferred_element_type=F)
    gate_grad, linear_grad = act_pull(hidden_grad)
    gate_low = gate_grad.astype(LOW)
    linear_low = linear_grad.astype(LOW)
    input_part = jnp.einsum("tf,df->td", gate_low, feed_gate, preferred_element_type=F) + jnp.einsum(
        "tf,df->td", linear_low, feed_linear, preferred_element_type=F
    )
    feed_in_grad = sum_over_tp(input_part)
    middle_part, feed_gain_grad = feed_pull(feed_in_grad)
    middle_grad = grad_out + middle_part
    out_low = middle_grad.astype(LOW)
    branch_grad = jnp.einsum("te,de->td", out_low, output_weight, preferred_element_type=F)
    mixed_grad, gate_pre_grad, post_gain_grad, post_bias_grad = branch_pull(branch_grad)
    out_grad_c = swap(to_chains(mixed_grad.astype(LOW))).reshape(length, span)

    second_out = sum_over_tp(matmul(hidden, feed_down))
    result = (middle + second_out).astype(LOW)[None]

    feed_down_grad = jnp.einsum("tf,td->fd", hidden, every_grad, preferred_element_type=F)
    feed_gate_grad = jnp.einsum("td,tf->df", every_in, gate_low, preferred_element_type=F)
    feed_linear_grad = jnp.einsum("td,tf->df", every_in, linear_low, preferred_element_type=F)
    output_weight_grad = jnp.einsum("td,te->de", branch_in, out_low, preferred_element_type=F)
    gate_low_pre = gate_pre_grad.astype(LOW)
    branch_gate_grad = jnp.einsum("td,te->de", normed, gate_low_pre, preferred_element_type=F)
    fed = [
        array.astype(F)
        for array in lax.psum(
            (feed_gate_grad.astype(LOW), feed_linear_grad.astype(LOW), feed_down_grad.astype(LOW)), "seq"
        )
    ]
    early = [
        array.astype(F)
        for array in lax.psum((output_weight_grad.astype(LOW), branch_gate_grad.astype(LOW)), ("seq", "tp"))
    ]

    (
        query_g, keys_g, values_g, rate_g, first_g, first_bias_g, second_g, second_bias_g, gain_g, shift_g,
    ) = bwd_scan(query_c, keys_c, values_c, rate_c, out_grad_c, *kept, chain_gain, chain_shift)
    logit_g = rate_g * (RATE_SCALE / head) * gate_c * (1.0 - gate_c)
    second_g = second_g - jnp.mean(second_g, 1, keepdims=True)
    second_bias_g = second_bias_g - jnp.mean(second_bias_g, -1, keepdims=True)
    bias_g = jnp.sum(logit_g, 0)

    logit_back = logit_g.astype(LOW).reshape(seqs, rows, each).transpose(0, 2, 1)
    logit_back = jnp.pad(logit_back, ((0, 0), (0, extra - each), (0, 3 * span - rows)))
    qkv_back = jnp.concatenate([query_g, keys_g, values_g], -1).reshape(seqs, rows, 3 * span)
    back = swap(jnp.concatenate([qkv_back, logit_back], 1))
    query_low = from_chains(back[:, :rows, :span])
    keys_low = from_chains(back[:, :rows, span : 2 * span])
    values_low = from_chains(back[:, :rows, 2 * span :])
    logit_low = back[:, rows : rows + each, :rows].reshape(seqs * each, rows)[:heads].T

    query_weight_grad = jnp.einsum("td,te->de", normed, query_low, preferred_element_type=F)
    key_weight_grad = jnp.einsum("td,te->de", normed, keys_low, preferred_element_type=F)
    value_weight_grad = jnp.einsum("td,te->de", normed, values_low, preferred_element_type=F)
    rate_weight_grad = jnp.einsum("td,te->de", normed, logit_low, preferred_element_type=F)
    late_in = (query_weight_grad.astype(LOW), key_weight_grad.astype(LOW), value_weight_grad.astype(LOW))
    late_in, early = lax.optimization_barrier((late_in, early))
    late = [array.astype(F) for array in lax.psum(late_in, ("seq", "tp"))]
    normed_grad = (
        jnp.einsum("te,de->td", query_low, query_weight, preferred_element_type=F)
        + jnp.einsum("te,de->td", keys_low, key_weight, preferred_element_type=F)
        + jnp.einsum("te,de->td", values_low, value_weight, preferred_element_type=F)
        + jnp.einsum("te,de->td", logit_low, rate_weight, preferred_element_type=F)
        + jnp.einsum("te,de->td", gate_low_pre, branch_gate, preferred_element_type=F)
    )
    residual_part, norm_gain_grad = norm_pull(normed_grad)
    tokens_grad = (middle_grad + residual_part)[None]
    small = lax.psum(
        (norm_gain_grad, rate_weight_grad, post_gain_grad, post_bias_grad, feed_gain_grad), ("seq", "tp")
    )

    tail_g = jnp.concatenate(
        [
            second_bias_g[:, 0],
            gain_g[:, 0],
            shift_g[:, 0],
            jnp.pad(bias_g[:, None], ((0, 0), (0, inner - 3 * head - 1))),
        ],
        -1,
    )
    chain_g = jnp.stack(
        [
            jnp.concatenate([first_g, first_bias_g], 1),
            jnp.concatenate([second_g, tail_g[:, None, :]], 1),
        ],
        1,
    )
    chain_g = jnp.pad(chain_g, ((0, 0), (0, 0), (0, 7), (0, 0))).astype(LOW)
    all_g = lax.all_gather(chain_g, "seq", axis=0, tiled=True)[:heads]
    head_g = lax.psum_scatter(all_g, "tp", scatter_dimension=0, tiled=True).astype(F)
    tail_sum = head_g[:, 1, head]
    return (
        result,
        tokens_grad,
        small[0],
        late[0],
        late[1],
        late[2],
        small[1],
        tail_sum[:, 3 * head],
        head_g[:, 0, :head],
        head_g[:, 0, head],
        jnp.swapaxes(head_g[:, 1, :head], 1, 2),
        tail_sum[:, :head],
        tail_sum[:, head : 2 * head],
        tail_sum[:, 2 * head : 3 * head],
        early[1],
        early[0],
        small[2],
        small[3],
        small[4],
        fed[0],
        fed[1],
        fed[2],
    )


def solution(mesh):
    in_specs = (
        P("tp", "seq", None),
        P(),
        P(),
        P(),
        P(),
        P(),
        P("tp"),
        P("tp", None, None),
        P("tp", None),
        P("tp", None, None),
        P("tp", None),
        P("tp", None),
        P("tp", None),
        P(),
        P(),
        P(),
        P(),
        P(),
        P(None, "tp"),
        P(None, "tp"),
        P("tp", None),
        P("tp", "seq", None),
    )
    out_specs = (
        P("tp", "seq", None),
        P("tp", "seq", None),
        P(),
        P(),
        P(),
        P(),
        P(),
        P("tp"),
        P("tp", None, None),
        P("tp", None),
        P("tp", None, None),
        P("tp", None),
        P("tp", None),
        P("tp", None),
        P(),
        P(),
        P(),
        P(),
        P(),
        P(None, "tp"),
        P(None, "tp"),
        P("tp", None),
    )
    return jax.shard_map(
        on_device, mesh=mesh, in_specs=in_specs, out_specs=out_specs, check_vma=False
    )
```

```python
from functools import partial

import jax
import jax.numpy as jnp
from jax import lax
from jax.sharding import PartitionSpec as P
from jax.experimental import pallas as pl
from jax.experimental.pallas import tpu as pltpu
C0=0.7978845608028654;C1=0.044715
EPS=1e-6
B=16
CH=128
LOW=jnp.bfloat16
F=jnp.float32
def nn(a,b): return lax.dot_general(a.astype(LOW),b.astype(LOW),(((1,),(0,)),((),())),preferred_element_type=F)
def nt(a,b): return lax.dot_general(a.astype(LOW),b.astype(LOW),(((1,),(1,)),((),())),preferred_element_type=F)
def tn(a,b): return lax.dot_general(a.astype(LOW),b.astype(LOW),(((0,),(0,)),((),())),preferred_element_type=F)
def mean(x): return jnp.sum(x,-1,keepdims=True)*(1.0/x.shape[-1])
def gelu2(z):
    z2=z*z
    t=jnp.tanh(z*(C0+(C0*C1)*z2))
    h=0.5+0.5*t
    x=z*h
    g1=h+x*(1-t)*(C0+(3*C0*C1)*z2)
    return x,g1
def gelu1(z):
    z2=z*z
    return z*(0.5+0.5*jnp.tanh(z*(C0+(C0*C1)*z2)))
def iotas():
    r=lax.broadcasted_iota(jnp.int32,(CH,CH),0); c=lax.broadcasted_iota(jnp.int32,(CH,CH),1)
    return r,c

def fwd_kernel(C,x_ref,r_ref,w1_ref,b1_ref,u_ref,b2_ref,gam_ref,bet_ref,
               o_ref,z1_ref,p_ref,zc_ref,z1q_ref,zq_ref,us_ref,w1s_ref,
               W1,B1,U,B2,S1,S2,X2,KK,BASE,T):
    @pl.when(pl.program_id(0)==0)
    def _():
        W1[...]=w1_ref[...]; B1[...]=b1_ref[...]; U[...]=u_ref[...]; B2[...]=b2_ref[...]
        S1[...]=jnp.zeros_like(S1)
    H=64
    ri,ci=iotas()
    blk=(ci//B)<(ri//B)
    tri=ci<=ri
    K=[x_ref[:,H*(C+c):H*(C+c)+H] for c in range(C)]
    Q=[x_ref[:,H*c:H*c+H] for c in range(C)]
    gam=[gam_ref[c] for c in range(C)]; bet=[bet_ref[c] for c in range(C)]
    R=[r_ref[:,c:c+1] for c in range(C)]
    w1b=[W1[c].astype(LOW) for c in range(C)]
    b1=[B1[c] for c in range(C)]
    u0=[U[c].astype(LOW) for c in range(C)]
    b20=[B2[c] for c in range(C)]
    g2=[gam[c]*gam[c] for c in range(C)]
    g2m=[mean(g2[c]) for c in range(C)]
    for c in range(C):
        w1s_ref[0,c]=w1b[c]
        KK[c]=jnp.where(blk,nt(K[c],K[c])+1.0,0.0).astype(LOW)
        BASE[c]=nn(K[c],w1b[c])+b1[c]
        T[c]=(bet[c]+K[c].astype(F)-x_ref[:,H*(2*C+c):H*(2*C+c)+H].astype(F))*gam[c]
    ub=list(u0); uf=[U[c] for c in range(C)]; b2=list(b20)
    for j in range(CH//B):
        sl=slice(B*j,B*j+B)
        for c in range(C):
            z1=BASE[c,sl]
            if j>0: z1=z1-nn(KK[c,sl],S1[c])
            x2,g1=gelu2(z1)
            x2b=x2.astype(LOW)
            zc=nt(x2b,ub[c])+b2[c]
            mu=mean(zc); zz=zc*zc; t=T[c,sl]
            var=mean(zz)-mu*mu
            s=lax.rsqrt(var+EPS)
            zc=zc-mu
            y=zc*s
            G=y*g2[c]+t
            m1=mean(G); m2=mean(G*y)
            d2=s*(G-m1-y*m2)
            P=nn(d2,ub[c])
            rr=R[c][sl]
            s1=P*(g1*rr)
            s2=d2*rr
            s2b=s2.astype(LOW)
            S1[c,sl]=s1.astype(LOW); S2[c,sl]=s2b; X2[c,sl]=x2b
            z1_ref[c,sl]=z1; p_ref[c,sl]=P; zc_ref[c,sl]=zc
            us_ref[0,c,j]=ub[c]
            uf[c]=uf[c]-tn(s2b,x2b); ub[c]=uf[c].astype(LOW)
            b2[c]=b2[c]-jnp.sum(s2,0,keepdims=True)
    for c in range(C):
        U[c]=uf[c]; B2[c]=b2[c]
        W1[c]=W1[c]-tn(K[c],S1[c])
        B1[c]=B1[c]-jnp.sum(S1[c].astype(F),0,keepdims=True)
        A1=jnp.where(tri,nt(Q[c],K[c])+1.0,0.0)
        z1q=nn(Q[c],w1b[c])+b1[c]-nn(A1,S1[c])
        x2q=gelu1(z1q).astype(LOW)
        A2=jnp.where(tri,nt(x2q,X2[c])+1.0,0.0)
        zq=nt(x2q,u0[c])+b20[c]-nn(A2,S2[c])
        zq=zq-mean(zq)
        yq=zq*lax.rsqrt(mean(zq*zq)+EPS)
        o_ref[:,H*c:H*c+H]=(Q[c].astype(F)+yq*gam[c]+bet[c]).astype(LOW)
        z1q_ref[c]=z1q; zq_ref[c]=zq

def fwd_scan(x,r,w1,b1,u,b2,gam,bet):
    L=x.shape[0]; C=w1.shape[0]; I=w1.shape[2]; H=w1.shape[1]; n=L//CH
    row=lambda w,dt=None: pl.BlockSpec((CH,w),lambda i:(i,0))
    full=lambda *s: pl.BlockSpec(s,lambda i:(0,)*len(s))
    big=lambda w: pl.BlockSpec((C,CH,w),lambda i:(0,i,0))
    sd=jax.ShapeDtypeStruct
    return pl.pallas_call(partial(fwd_kernel,C),grid=(n,),
        in_specs=[row(3*C*H),row(C),full(C,H,I),full(C,1,I),full(C,H,I),full(C,1,H),full(C,1,H),full(C,1,H)],
        out_specs=[row(C*H),big(I),big(I),big(H),big(I),big(H),pl.BlockSpec((1,C,CH//B,H,I),lambda i:(i,0,0,0,0)),pl.BlockSpec((1,C,H,I),lambda i:(i,0,0,0))],
        out_shape=[sd((L,C*H),LOW),sd((C,L,I),F),sd((C,L,I),F),sd((C,L,H),F),sd((C,L,I),F),sd((C,L,H),F),sd((n,C,CH//B,H,I),LOW),sd((n,C,H,I),LOW)],
        scratch_shapes=[pltpu.VMEM((C,H,I),F),pltpu.VMEM((C,1,I),F),pltpu.VMEM((C,H,I),F),pltpu.VMEM((C,1,H),F),
            pltpu.VMEM((C,CH,I),LOW),pltpu.VMEM((C,CH,H),LOW),pltpu.VMEM((C,CH,I),LOW),pltpu.VMEM((C,CH,CH),LOW),pltpu.VMEM((C,CH,I),F),pltpu.VMEM((C,CH,H),F)],
        compiler_params=pltpu.CompilerParams(vmem_limit_bytes=48*1024*1024),
    )(x,r,w1,b1,u,b2,gam,bet)

def gelu3(z):
    z2=z*z
    t=jnp.tanh(z*(C0+(C0*C1)*z2))
    u1=C0+(3*C0*C1)*z2
    h=0.5+0.5*t
    h1=h*(1-t)*u1
    x=z*h
    g1=h+z*h1
    g2=2*h1+z*(h*(1-t)*(6*C0*C1)*z-2*t*u1*h1)
    return x,g1,g2

def bwd_kernel(C,n,x_ref,r_ref,do_ref,z1_ref,p_ref,zc_ref,z1q_ref,zq_ref,us_ref,w1s_ref,gam_ref,bet_ref,
               dx_ref,dr_ref,H1,h1,HU,h2,dgam_ref,dbet_ref,
               BASE,DX2,X2,RG1,RPG2,DS2Q,KK,DZ1,DS1,DS2,DG,YB,GB,DB,SB,S2B,G1):
    @pl.when(pl.program_id(0)==0)
    def _():
        for ref in (H1,h1,HU,h2,dgam_ref,dbet_ref,DZ1): ref[...]=jnp.zeros_like(ref)
    H=64
    ri,ci=iotas()
    blk=(ci//B)<(ri//B)
    blkT=(ci//B)>(ri//B)
    tri=ci<=ri
    K=[x_ref[:,H*(C+c):H*(C+c)+H] for c in range(C)]
    Q=[x_ref[:,H*c:H*c+H] for c in range(C)]
    gam=[gam_ref[c] for c in range(C)]; bet=[bet_ref[c] for c in range(C)]
    R=[r_ref[:,c:c+1] for c in range(C)]
    g2=[gam[c]*gam[c] for c in range(C)]
    hu=[HU[c] for c in range(C)]; hh2=[h2[c] for c in range(C)]
    keep=[]
    for c in range(C):
        dO=do_ref[:,H*c:H*c+H].astype(F)
        x2q,g1q=gelu2(z1q_ref[c]); x2q=x2q.astype(LOW)
        zq=zq_ref[c]; sq=lax.rsqrt(mean(zq*zq)+EPS); yq=zq*sq
        x2,g1,gg2=gelu3(z1_ref[c]); x2=x2.astype(LOW)
        X2[c]=x2
        P=p_ref[c]
        r=R[c]
        RG1[c]=r*g1; G1[c]=g1
        RPG2[c]=r*(P*gg2)
        s1=(P*g1*r).astype(LOW)
        zc=zc_ref[c]
        s=lax.rsqrt(mean(zc*zc)+EPS)
        y=zc*s
        t0=bet[c]+K[c].astype(F)-x_ref[:,H*(2*C+c):H*(2*C+c)+H].astype(F)
        G=y*g2[c]+t0*gam[c]
        m1=mean(G); m2=mean(G*y)
        d2=s*(G-m1-y*m2)
        s2=(d2*r).astype(LOW)
        YB[c]=y; GB[c]=G; DB[c]=d2; S2B[c]=s2
        SB[c,:,0:1]=s; SB[c,:,1:2]=m2
        u0=us_ref[0,c,0]
        w1=w1s_ref[0,c]
        dgam_ref[c]=dgam_ref[c]+jnp.sum(dO*yq,0,keepdims=True)
        dbet_ref[c]=dbet_ref[c]+jnp.sum(dO,0,keepdims=True)
        dyq=dO*gam[c]
        dzq=sq*(dyq-mean(dyq)-yq*mean(dyq*yq))
        dzqb=dzq.astype(LOW)
        A2=jnp.where(tri,nt(x2q,x2)+1.0,0.0)
        dA2=jnp.where(tri,nt(dzqb,s2),0.0).astype(LOW)
        dx2q=nn(dzqb,u0)-nn(dA2,x2)
        DX2[c]=-tn(dA2,x2q)
        DS2Q[c]=-tn(A2,dzqb)
        dz1q=dx2q*g1q
        dz1qb=dz1q.astype(LOW)
        A1=jnp.where(tri,nt(Q[c],K[c])+1.0,0.0)
        dA1=jnp.where(tri,nt(dz1qb,s1),0.0).astype(LOW)
        dx_ref[:,H*c:H*c+H]=(dO+nt(dz1qb,w1)-nn(dA1,K[c])).astype(LOW)
        h1b=H1[c].astype(LOW)
        dk=nt(s1,h1b)+tn(dA1,Q[c])
        KK[c]=jnp.where(blkT,nt(K[c],K[c])+1.0,0.0).astype(LOW)
        BASE[c]=-tn(A1,dz1qb)-nn(K[c],h1b)-h1[c]
        h1n=h1[c]+jnp.sum(dz1q,0,keepdims=True)
        H1n=H1[c]+tn(Q[c],dz1qb)
        keep.append((s1,t0,dzqb,x2q,dk,H1n,h1n,w1,P*g1))
    for j in reversed(range(CH//B)):
        sl=slice(B*j,B*j+B)
        for c in range(C):
            ub=us_ref[0,c,j]
            rr=R[c][sl]
            hub=hu[c].astype(LOW)
            ds1=BASE[c,sl]
            if j<CH//B-1: ds1=ds1-nn(KK[c,sl],DZ1[c])
            x2=X2[c,sl]
            ds2=DS2Q[c,sl]-nt(x2,hub)-hh2[c]
            dx2=DX2[c,sl]-nn(S2B[c,sl],hub)
            dP=ds1*RG1[c,sl]
            dPb=dP.astype(LOW)
            e=rr*ds2+nt(dPb,ub)
            s=SB[c,sl,0:1]; m2=SB[c,sl,1:2]; y=YB[c,sl]; g_=GB[c,sl]; d2=DB[c,sl]
            a=mean(e); b=mean(e*y); cc=mean(e*d2)
            dG=s*(e-a-y*b)
            dY=g2[c]*dG-s*(m2*e+g_*b)
            dZc=s*(dY-mean(dY)-y*(cc+mean(dY*y)))
            dZcb=dZc.astype(LOW)
            dx2=dx2+nn(dZcb,ub)
            dz1=dx2*G1[c,sl]+ds1*RPG2[c,sl]
            DZ1[c,sl]=dz1.astype(LOW)
            DS1[c,sl]=ds1; DS2[c,sl]=ds2; DG[c,sl]=dG
            hu[c]=hu[c]+tn(jnp.concatenate([d2.astype(LOW),dZcb],0),jnp.concatenate([dPb,x2],0))
            hh2[c]=hh2[c]+jnp.sum(dZc,0,keepdims=True)
    for c in range(C):
        s1,t0,dzqb,x2q,dk,H1n,h1n,w1,D1=keep[c]
        dz1=DZ1[c]
        M=jnp.where(blk,nt(dz1,s1),0.0).astype(LOW)
        dG=DG[c]; dGg=dG*gam[c]
        dk=-dk-nn(M,K[c])-tn(M,K[c])+nt(dz1,w1)+dGg
        dx_ref[:,H*(C+c):H*(C+c)+H]=dk.astype(LOW)
        dx_ref[:,H*(2*C+c):H*(2*C+c)+H]=(-dGg).astype(LOW)
        dr_ref[:,c:c+1]=jnp.sum(DS1[c]*D1,-1,keepdims=True)+jnp.sum(DS2[c]*DB[c],-1,keepdims=True)
        dgam_ref[c]=dgam_ref[c]+jnp.sum(dG*(2*YB[c]*gam[c]+t0),0,keepdims=True)
        dbet_ref[c]=dbet_ref[c]+jnp.sum(dGg,0,keepdims=True)
        H1[c]=H1n+tn(K[c],dz1)
        h1[c]=h1n+jnp.sum(dz1.astype(F),0,keepdims=True)
        HU[c]=hu[c]+tn(dzqb,x2q)
        h2[c]=hh2[c]+jnp.sum(dzqb.astype(F),0,keepdims=True)

def bwd_scan(x,r,do,z1,p,zc,z1q,zq,us,w1s,gam,bet):
    L=x.shape[0]; C,_,I=z1.shape; H=zc.shape[2]; n=L//CH
    row=lambda w,dt=None: pl.BlockSpec((CH,w),lambda i:(n-1-i,0))
    full=lambda *s: pl.BlockSpec(s,lambda i:(0,)*len(s))
    big=lambda w: pl.BlockSpec((C,CH,w),lambda i:(0,n-1-i,0))
    sd=jax.ShapeDtypeStruct
    V=pltpu.VMEM
    return pl.pallas_call(partial(bwd_kernel,C,n),grid=(n,),
        in_specs=[row(3*C*H),row(C),row(C*H),big(I),big(I),big(H),big(I),big(H),pl.BlockSpec((1,C,CH//B,H,I),lambda i:(n-1-i,0,0,0,0)),pl.BlockSpec((1,C,H,I),lambda i:(n-1-i,0,0,0)),full(C,1,H),full(C,1,H)],
        out_specs=[row(3*C*H),row(C),full(C,H,I),full(C,1,I),full(C,H,I),full(C,1,H),full(C,1,H),full(C,1,H)],
        out_shape=[sd((L,3*C*H),LOW),sd((L,C),F),sd((C,H,I),F),sd((C,1,I),F),sd((C,H,I),F),sd((C,1,H),F),sd((C,1,H),F),sd((C,1,H),F)],
        scratch_shapes=[V((C,CH,I),F),V((C,CH,I),F),V((C,CH,I),LOW),V((C,CH,I),F),V((C,CH,I),F),V((C,CH,H),F),V((C,CH,CH),LOW),V((C,CH,I),LOW),V((C,CH,I),F),V((C,CH,H),F),V((C,CH,H),F),
            V((C,CH,H),F),V((C,CH,H),F),V((C,CH,H),F),V((C,CH,2),F),V((C,CH,H),LOW),V((C,CH,I),F)],
        compiler_params=pltpu.CompilerParams(vmem_limit_bytes=48*1024*1024),
    )(x,r,do,z1,p,zc,z1q,zq,us,w1s,gam,bet)

RATE_SCALE = 0.25
NORM_EPS = 1e-05


def smooth_act(value):
    return 0.5 * value * (1.0 + jnp.tanh(C0 * (value + C1 * value * value * value)))


def root_norm(value, gain):
    return value * lax.rsqrt(jnp.mean(value * value, -1, keepdims=True) + NORM_EPS) * gain


def layer_norm(value, gain, bias):
    centre = value - jnp.mean(value, -1, keepdims=True)
    return centre * lax.rsqrt(jnp.mean(centre * centre, -1, keepdims=True) + NORM_EPS) * gain + bias


def gated_branch(mixed, gate_pre, gain, bias):
    return layer_norm(mixed, gain, bias) * smooth_act(gate_pre)


def swish_product(gate_val, linear_val):
    return jax.nn.silu(gate_val) * linear_val


def matmul(left, right):
    return jnp.dot(left, right, preferred_element_type=F)


def flip(array, axis, mask):
    peers = lax.axis_size(axis)
    return lax.ppermute(array, axis, [(i, i ^ mask) for i in range(peers)])


def masks_of(axis):
    masks = []
    while 1 << len(masks) < lax.axis_size(axis):
        masks.append(1 << len(masks))
    return masks


def side(axis, mask):
    return (lax.axis_index(axis) // mask) % 2


def gather_near(array, axis):
    for mask in reversed(masks_of(axis)):
        array = jnp.concatenate([array, flip(array, axis, mask)], 0)
    return array


def scatter_near(array, axis):
    for mask in masks_of(axis):
        half = array.shape[0] // 2
        array = array[:half].astype(F) + flip(array[half:].astype(LOW), axis, mask).astype(F)
    return array


def halve(array, axis, mask, dim):
    bit = side(axis, mask)
    mine = lax.dynamic_index_in_dim(array, bit, dim, keepdims=False)
    other = lax.dynamic_index_in_dim(array, 1 - bit, dim, keepdims=False)
    return mine.astype(F) + flip(other.astype(LOW), axis, mask).astype(F)


def double(array, axis, mask):
    got = flip(array, axis, mask)
    upper = side(axis, mask) == 1
    return jnp.stack([jnp.where(upper, got, array), jnp.where(upper, array, got)])


def share_rows(columns, chain_g, rate_column, vectors, early, heads, local_heads, weights_in):
    seqs, tps = lax.axis_size("seq"), lax.axis_size("tp")
    width, lanes = columns.shape
    span = lanes // 3
    each, _, head, inner = chain_g[0].shape
    states = jnp.concatenate([chain_g[0], chain_g[1][:, :, None], jnp.zeros((each, 2, 7, inner), F)], 2)
    state_rows = states.size // lanes // tps
    rate_rows = rate_column.size // lanes // tps
    vectors = jnp.concatenate([vectors, jnp.zeros_like(vectors[:1])], 0)
    vector_rows = vectors.size // lanes // tps
    rest = jnp.concatenate(
        [rate_column.reshape(tps, rate_rows, lanes), vectors.reshape(tps, vector_rows, lanes)], 1
    )
    late = jnp.concatenate(
        [
            columns.reshape(tps, width // tps, lanes),
            states.reshape(tps, state_rows, lanes),
            jnp.pad(rest, ((0, 0), (0, 16 - rate_rows - vector_rows), (0, 0))),
        ],
        1,
    )
    late = lax.psum_scatter(late.astype(LOW), "tp", scatter_dimension=0, tiled=True)
    late = lax.all_gather(late, ("seq", "tp"), axis=0, tiled=True).reshape((seqs, tps) + late.shape[1:])
    weights = late[:, :, : width // tps].reshape(seqs, tps, width // tps, 3, span)
    weights = weights.transpose(3, 1, 2, 0, 4).reshape(3, width, seqs * span)[:, :, :width].astype(F)
    states = late[:, :, width // tps : width // tps + state_rows].reshape(seqs * each, 2, head + 8, inner)[:heads]
    states = lax.dynamic_slice_in_dim(states, lax.axis_index("tp") * local_heads, local_heads, 0).astype(F)
    rest = late[:, :, width // tps + state_rows :]
    rate_weight_grad = rest[:, :, :rate_rows].reshape(seqs * each, width)[:heads].T.astype(F)
    vectors = rest[:, :, rate_rows : rate_rows + vector_rows].reshape(seqs, 4, width)
    vectors = jnp.sum(vectors.astype(F), 0)
    norm_gain_grad = early[1] * weights_in[3].astype(F)
    for i in range(3):
        norm_gain_grad = norm_gain_grad + weights[i] * weights_in[i].astype(F)
    return weights, states[:, :, :head], states[:, :, head], rate_weight_grad, vectors, jnp.sum(norm_gain_grad, -1)


def last_kernel(seqs, each, heads, local_heads, me_ref, a_ref, b_ref, wq_ref, wk_ref, wv_ref, wg_ref, gg_ref,
                q_ref, k_ref, v_ref, n_ref, s_ref, r_ref):
    cut = a_ref.shape[3]
    span = a_ref.shape[4] // 3
    below = q_ref.shape[0] - cut
    total = gg_ref[0] * wg_ref[...].astype(F)
    for s in range(seqs):
        if s * each >= heads:
            continue
        x, q = s % 2, ((s >> 1) & 1) * 2 + (s >> 2)
        for i, o_ref in enumerate((q_ref, k_ref, v_ref)):
            o_ref[:cut, span * s : span * s + span] = a_ref[0, 0, 4 * x + q, :, span * i : span * i + span].astype(F)
            o_ref[cut:, span * s : span * s + span] = b_ref[0, x, 0, q, :below, span * i : span * i + span].astype(F)
    for o_ref, w_ref in ((q_ref, wq_ref), (k_ref, wk_ref), (v_ref, wv_ref)):
        total = total + o_ref[...] * w_ref[...].astype(F)
    n_ref[...] = jnp.sum(total, -1, keepdims=True)

    def tile(x, q, n):
        return b_ref[0, x, 0, q, below + 16 * (n // 3) : below + 16 * (n // 3) + 16, 128 * (n % 3) : 128 * (n % 3) + 128]

    for i in range(local_heads):
        h = me_ref[0] * local_heads + i
        s = h // each
        upper = lax.rem(h, each) == 1
        x = lax.rem(s, 2)
        q = lax.rem(s // 2, 2) * 2 + s // 4
        for k in range(2):
            for j in range(2):
                low = tile(x, q, k * 2 + j).astype(F)
                high = tile(x, q, 4 + k * 2 + j).astype(F)
                s_ref[i, k, :, 128 * j : 128 * j + 128] = jnp.where(upper, high, low)
    for s in range(seqs):
        r_ref[0, s] = tile(s % 2, ((s >> 1) & 1) * 2 + (s >> 2), 8).astype(F)


def share_tiles(columns, chain_g, rate_column, vectors, other_fed, early, heads, local_heads, weights_in):
    seqs, tps = lax.axis_size("seq"), lax.axis_size("tp")
    width, lanes = columns.shape
    each, _, head, inner = chain_g[0].shape
    here = width // tps
    states = chain_g[0].reshape(each * 2, tps, head // tps, 2, 128).transpose(1, 0, 3, 2, 4)
    states = states.reshape(tps, each * 4, head // tps, 128)
    tails = chain_g[1].reshape(tps, -1, 128)
    rates = rate_column.reshape(tps, -1, 128)
    vector_rows = -(-vectors.size // 128 // tps)
    small = jnp.pad(vectors.reshape(-1, 128), ((0, vector_rows * tps - vectors.size // 128), (0, 0)))
    small = jnp.concatenate([tails, rates, small.reshape(tps, vector_rows, 128)], 1)
    small = jnp.pad(small, ((0, 0), (0, 16 - small.shape[1]), (0, 0)))
    tiles = jnp.concatenate([states, small[:, None]], 1).reshape(tps, 3, 3, 16, 128)
    tiles = tiles.transpose(0, 1, 3, 2, 4).reshape(tps, 48, lanes)
    late = jnp.concatenate([columns.reshape(tps, here, lanes), tiles], 1)
    share = late.shape[1]
    late = late.reshape(2, 2, share, lanes)
    late = halve(late, "tp", 1, 1)
    late = halve(late, "tp", 2, 0).astype(LOW)
    late = double(late, "seq", 4)
    late = double(late, "seq", 2)
    cut = 128
    part_a, part_b = late[:, :, :cut], late[:, :, cut:]
    part_a, part_b = double(part_a, "seq", 1), double(part_b, "tp", 2)
    part_a, part_b = double(part_a, "tp", 2), double(part_b, "seq", 1)
    part_a, part_b = double(part_a, "tp", 1), double(part_b, "tp", 1)
    part_a = part_a.reshape(2, 2, seqs, cut, lanes)
    part_b = part_b.reshape(2, 2, 2, seqs // 2, share - cut, lanes)
    me = lax.axis_index("tp").astype(jnp.int32).reshape(1)
    square = pl.BlockSpec((here, width), lambda t: (t, 0))
    sd = jax.ShapeDtypeStruct
    *weights, norm_gain_grad, head_w, small = pl.pallas_call(
        partial(last_kernel, seqs, each, heads, local_heads),
        grid=(tps,),
        in_specs=[
            pl.BlockSpec(memory_space=pltpu.SMEM),
            pl.BlockSpec((1, 1, seqs, cut, lanes), lambda t: (t % 2, t // 2, 0, 0, 0)),
            pl.BlockSpec((1, 2, 1, seqs // 2, share - cut, lanes), lambda t: (t % 2, 0, t // 2, 0, 0, 0)),
            square, square, square, square,
            pl.BlockSpec((1, here, width), lambda t: (1, t, 0)),
        ],
        out_specs=[
            square, square, square,
            pl.BlockSpec((here, 1), lambda t: (t, 0)),
            pl.BlockSpec((local_heads, 2, head // tps, inner), lambda t: (0, 0, t, 0)),
            pl.BlockSpec((1, seqs, 16, 128), lambda t: (t, 0, 0, 0)),
        ],
        out_shape=[sd((width, width), F)] * 3
        + [sd((width, 1), F), sd((local_heads, 2, head, inner), F), sd((tps, seqs, 16, 128), F)],
        compiler_params=pltpu.CompilerParams(vmem_limit_bytes=48 * 1024 * 1024),
    )(me, part_a, part_b, *weights_in, early)
    edge = tails.shape[1]
    edge_r = edge + rates.shape[1]
    head_t = small[:, :, :edge].transpose(1, 0, 2, 3).reshape(seqs * each, 2, inner)
    head_t = lax.dynamic_slice_in_dim(head_t, me[0] * local_heads, local_heads, 0)
    rate_weight_grad = small[:, :, edge:edge_r].transpose(1, 0, 2, 3).reshape(seqs * each, width)[:heads].T
    vectors = jnp.sum(small[:, :, edge_r : edge_r + vector_rows], 1).reshape(-1)[: 3 * width].reshape(3, width)
    return weights, head_w, head_t, rate_weight_grad, vectors, other_fed, norm_gain_grad[:, 0]


def on_device(
    tokens, norm_gain, query_weight, key_weight, value_weight, rate_weight, rate_bias,
    first_weight, first_bias, second_weight, second_bias, inner_gain, inner_bias,
    branch_gate, output_weight, post_gain, post_bias, feed_gain, feed_gate, feed_linear,
    feed_down, cotangent,
):
    seqs = lax.axis_size("seq")
    rank = lax.axis_index("seq")
    heads = rate_weight.shape[1]
    local_heads, head, inner = first_weight.shape
    rows = tokens.shape[1]
    width = tokens.shape[2]
    each = -(-heads // seqs)
    span = each * head
    length = seqs * rows
    extra = -(-each // 16) * 16

    def to_chains(array):
        padded = jnp.pad(array, ((0, 0), (0, seqs * span - array.shape[1])))
        return padded.reshape(rows, seqs, span).transpose(1, 0, 2)

    def from_chains(array):
        return array.transpose(1, 0, 2).reshape(rows, seqs * span)[:, :width]

    def swap(array):
        return lax.all_to_all(array, "seq", split_axis=0, concat_axis=0, tiled=True)

    first_pack = jnp.concatenate([first_weight, first_bias[:, None, :]], 1)
    centred = jnp.swapaxes(second_weight, 1, 2)
    centred = centred - jnp.mean(centred, 1, keepdims=True)
    tail = jnp.concatenate(
        [
            second_bias - jnp.mean(second_bias, -1, keepdims=True),
            inner_gain,
            inner_bias,
            jnp.pad(rate_bias[:, None], ((0, 0), (0, inner - 3 * head - 1))),
        ],
        -1,
    )
    second_pack = jnp.concatenate([centred, tail[:, None, :]], 1)
    packed = jnp.pad(jnp.stack([first_pack, second_pack], 1), ((0, 0), (0, 0), (0, 7), (0, 0)))
    every = lax.all_gather(packed, "tp", axis=0, tiled=True)
    own = jnp.stack(
        [
            lax.dynamic_index_in_dim(every, jnp.minimum(rank * each + c, heads - 1), 0, keepdims=False)
            for c in range(each)
        ]
    )
    chain_first = own[:, 0, :head]
    chain_first_bias = own[:, 0, head : head + 1]
    chain_second = own[:, 1, :head]
    chain_tail = own[:, 1, head : head + 1]
    chain_second_bias = chain_tail[..., :head]
    chain_gain = chain_tail[..., head : 2 * head]
    chain_shift = chain_tail[..., 2 * head : 3 * head]
    chain_rate_bias = chain_tail[:, 0, 3 * head]

    residual = tokens[0].astype(F)
    normed_val, norm_pull = jax.vjp(root_norm, residual, norm_gain)
    normed = normed_val.astype(LOW)
    down_grad = cotangent[0]
    grad_out = down_grad.astype(F)
    every_grad = gather_near(down_grad, "tp")
    query_tok = matmul(normed, query_weight).astype(LOW)
    keys_tok = matmul(normed, key_weight).astype(LOW)
    values_tok = matmul(normed, value_weight).astype(LOW)
    logits_tok = matmul(normed, rate_weight).astype(LOW)
    gate_pre = matmul(normed, branch_gate)

    logit_rows = jnp.pad(logits_tok.T, ((0, seqs * each - heads), (0, 0))).reshape(seqs, each, rows)
    logit_rows = jnp.pad(logit_rows, ((0, 0), (0, extra - each), (0, 3 * span - rows)))
    sent = jnp.concatenate(
        [jnp.concatenate([to_chains(query_tok), to_chains(keys_tok), to_chains(values_tok)], -1), logit_rows],
        1,
    )
    got = swap(sent)
    chain_qkv = got[:, :rows].reshape(length, 3 * span)
    logit_c = got[:, rows : rows + each, :rows].transpose(0, 2, 1).reshape(length, each).astype(F)
    gate_c = jax.nn.sigmoid(logit_c + chain_rate_bias)
    rate_c = gate_c * (RATE_SCALE / head)

    every_normed = lax.all_gather(normed, "seq", axis=0, tiled=True)
    outs, *kept = fwd_scan(
        chain_qkv, rate_c, chain_first, chain_first_bias, chain_second,
        chain_second_bias, chain_gain, chain_shift,
    )
    outs, every_normed = lax.optimization_barrier((outs, every_normed))
    mixed_tok = from_chains(swap(outs.reshape(seqs, rows, span))).astype(F)

    branch_val, branch_pull = jax.vjp(gated_branch, mixed_tok, gate_pre, post_gain, post_bias)
    branch_in = branch_val.astype(LOW)
    middle = residual + matmul(branch_in, output_weight)
    feed_val, feed_pull = jax.vjp(root_norm, middle, feed_gain)
    feed_in = feed_val.astype(LOW)
    every_in = gather_near(feed_in, "tp")
    gate_val = matmul(every_in, feed_gate)
    linear_val = matmul(every_in, feed_linear)
    act_val, act_pull = jax.vjp(swish_product, gate_val, linear_val)
    hidden = act_val.astype(LOW)

    hidden_grad = jnp.einsum("td,fd->tf", every_grad, feed_down, preferred_element_type=F)
    gate_grad, linear_grad = act_pull(hidden_grad)
    gate_low = gate_grad.astype(LOW)
    linear_low = linear_grad.astype(LOW)
    input_part = jnp.einsum("tf,df->td", gate_low, feed_gate, preferred_element_type=F) + jnp.einsum(
        "tf,df->td", linear_low, feed_linear, preferred_element_type=F
    )
    feed_in_grad = scatter_near(input_part, "tp")
    middle_part, feed_gain_grad = feed_pull(feed_in_grad)
    middle_grad = grad_out + middle_part
    out_low = middle_grad.astype(LOW)
    branch_grad = jnp.einsum("te,de->td", out_low, output_weight, preferred_element_type=F)
    mixed_grad, gate_pre_grad, post_gain_grad, post_bias_grad = branch_pull(branch_grad)
    out_grad_c = swap(to_chains(mixed_grad.astype(LOW))).reshape(length, span)

    second_part = matmul(hidden, feed_down).astype(LOW)
    second_part, out_grad_c = lax.optimization_barrier((second_part, out_grad_c))
    second_out = scatter_near(second_part, "tp")
    result = (middle + second_out).astype(LOW)[None]

    feed_down_grad = jnp.einsum("tf,td->fd", hidden, every_grad, preferred_element_type=F)
    feed_gate_grad = jnp.einsum("td,tf->df", every_in, gate_low, preferred_element_type=F)
    feed_linear_grad = jnp.einsum("tf,td->fd", linear_low, every_in, preferred_element_type=F)
    output_weight_grad = jnp.einsum("td,te->de", branch_in, out_low, preferred_element_type=F)
    gate_low_pre = gate_pre_grad.astype(LOW)
    branch_gate_grad = jnp.einsum("td,te->de", normed, gate_low_pre, preferred_element_type=F)
    tps = lax.axis_size("tp")
    early = jnp.concatenate([output_weight_grad, branch_gate_grad], 0).reshape((2,) * len(masks_of("tp")) + (-1, width))
    for mask in masks_of("tp"):
        early = halve(early, "tp", mask, len(masks_of("tp")) - 1 - masks_of("tp").index(mask))
    fed_parts = jnp.concatenate(
        [
            feed_linear_grad.astype(LOW).reshape(seqs, -1, width),
            feed_down_grad.astype(LOW).reshape(seqs, -1, width),
        ],
        1,
    )
    fed_parts, out_grad_c = lax.optimization_barrier((fed_parts, out_grad_c))
    fed_parts = swap(fed_parts)
    early, first_fed = lax.psum((early.astype(LOW), feed_gate_grad.astype(LOW)), "seq")

    (
        qkv_g, rate_g, first_g, first_bias_g, second_g, second_bias_g, gain_g, shift_g,
    ) = bwd_scan(chain_qkv, rate_c, out_grad_c, *kept, chain_gain, chain_shift)
    early, first_fed, fed_parts, qkv_g, rate_g = lax.optimization_barrier(
        (early, first_fed, fed_parts, qkv_g, rate_g)
    )
    fed = jnp.sum(fed_parts.astype(F), 0).astype(LOW)
    levels = masks_of("seq")
    for mask in reversed(levels):
        fed = double(fed, "seq", mask)
    fed = fed.transpose(list(range(len(levels)))[::-1] + [len(levels), len(levels) + 1])
    fed = fed.reshape(seqs, 2, -1, width)
    other_fed = [fed[:, 0].reshape(-1, width).astype(F).T, fed[:, 1].reshape(-1, width).astype(F)]
    for mask in reversed(masks_of("tp")):
        early = double(early, "tp", mask)
    early = jnp.transpose(early, list(range(len(masks_of("tp"))))[::-1] + [len(masks_of("tp")), len(masks_of("tp")) + 1])
    early = early.reshape(2, width, width).astype(F)
    logit_g = rate_g * (RATE_SCALE / head) * gate_c * (1.0 - gate_c)
    second_g = second_g - jnp.mean(second_g, 1, keepdims=True)
    second_bias_g = second_bias_g - jnp.mean(second_bias_g, -1, keepdims=True)
    bias_g = jnp.sum(logit_g, 0)

    logit_back = logit_g.astype(LOW).reshape(seqs, rows, each).transpose(0, 2, 1)
    logit_back = jnp.pad(logit_back, ((0, 0), (0, extra - each), (0, 3 * span - rows)))
    qkv_back = qkv_g.reshape(seqs, rows, 3 * span)
    back = swap(jnp.concatenate([qkv_back, logit_back], 1))
    query_low = from_chains(back[:, :rows, :span])
    keys_low = from_chains(back[:, :rows, span : 2 * span])
    values_low = from_chains(back[:, :rows, 2 * span :])
    logit_low = back[:, rows : rows + each, :rows].reshape(seqs * each, rows)[:heads].T

    normed_grad = (
        jnp.einsum("te,de->td", query_low, query_weight, preferred_element_type=F)
        + jnp.einsum("te,de->td", keys_low, key_weight, preferred_element_type=F)
        + jnp.einsum("te,de->td", values_low, value_weight, preferred_element_type=F)
        + jnp.einsum("te,de->td", logit_low, rate_weight, preferred_element_type=F)
        + jnp.einsum("te,de->td", gate_low_pre, branch_gate, preferred_element_type=F)
    )
    residual_part, unused = norm_pull(normed_grad)
    tokens_grad = (middle_grad + residual_part)[None]
    tail_g = jnp.concatenate(
        [
            second_bias_g[:, 0],
            gain_g[:, 0],
            shift_g[:, 0],
            jnp.pad(bias_g[:, None], ((0, 0), (0, inner - 3 * head - 1))),
        ],
        -1,
    )
    chain_g = (jnp.stack([first_g, second_g], 1), jnp.stack([first_bias_g[:, 0], tail_g], 1))
    columns = jnp.einsum("ld,le->de", every_normed, qkv_g, preferred_element_type=F)
    rate_column = jnp.einsum("ld,le->ed", every_normed, logit_g.astype(LOW), preferred_element_type=F)
    vectors = jnp.stack([post_gain_grad, post_bias_grad, feed_gain_grad])
    if each == 2 and tps == 4 and seqs == 8:
        weights, head_w, head_t, rate_weight_grad, vectors, other_fed, norm_gain_grad = share_tiles(
            columns, chain_g, rate_column, vectors, other_fed, early, heads, local_heads,
            (query_weight, key_weight, value_weight, branch_gate),
        )
    else:
        weights, head_w, head_t, rate_weight_grad, vectors, norm_gain_grad = share_rows(
            columns, chain_g, rate_column, vectors, early, heads, local_heads,
            (query_weight, key_weight, value_weight, branch_gate),
        )
    norm_gain_grad = norm_gain_grad + jnp.sum(rate_weight_grad * rate_weight.astype(F), -1)
    norm_gain_grad = norm_gain_grad / norm_gain
    tail_sum = head_t[:, 1]
    return (
        result,
        tokens_grad,
        norm_gain_grad,
        weights[0],
        weights[1],
        weights[2],
        rate_weight_grad,
        tail_sum[:, 3 * head],
        head_w[:, 0],
        head_t[:, 0],
        jnp.swapaxes(head_w[:, 1], 1, 2),
        tail_sum[:, :head],
        tail_sum[:, head : 2 * head],
        tail_sum[:, 2 * head : 3 * head],
        early[1],
        early[0],
        vectors[0],
        vectors[1],
        vectors[2],
        first_fed.astype(F),
        other_fed[0].astype(F),
        other_fed[1].astype(F),
    )


def solution(mesh):
    in_specs = (
        P("tp", "seq", None),
        P(),
        P(),
        P(),
        P(),
        P(),
        P("tp"),
        P("tp", None, None),
        P("tp", None),
        P("tp", None, None),
        P("tp", None),
        P("tp", None),
        P("tp", None),
        P(),
        P(),
        P(),
        P(),
        P(),
        P(None, "tp"),
        P(None, "tp"),
        P("tp", None),
        P("tp", "seq", None),
    )
    out_specs = (
        P("tp", "seq", None),
        P("tp", "seq", None),
        P(),
        P(),
        P(),
        P(),
        P(),
        P("tp"),
        P("tp", None, None),
        P("tp", None),
        P("tp", None, None),
        P("tp", None),
        P("tp", None),
        P("tp", None),
        P(),
        P(),
        P(),
        P(),
        P(),
        P(None, "tp"),
        P(None, "tp"),
        P("tp", None),
    )
    return jax.shard_map(
        on_device, mesh=mesh, in_specs=in_specs, out_specs=out_specs, check_vma=False
    )
```

```python
from functools import partial

import jax
import jax.numpy as jnp
from jax import lax
from jax.sharding import PartitionSpec as P
from jax.experimental import pallas as pl
from jax.experimental.pallas import tpu as pltpu
C0=0.7978845608028654
C1=0.044715
EPS=1e-6
RATE_SCALE=0.25
B=16
CH=128
NB=CH//B
LOW=jnp.bfloat16
F=jnp.float32
def nn(a,b): return lax.dot_general(a.astype(LOW),b.astype(LOW),(((1,),(0,)),((),())),preferred_element_type=F)
def nt(a,b): return lax.dot_general(a.astype(LOW),b.astype(LOW),(((1,),(1,)),((),())),preferred_element_type=F)
def tn(a,b): return lax.dot_general(a.astype(LOW),b.astype(LOW),(((0,),(0,)),((),())),preferred_element_type=F)
def gelu1(z):
    return z*(0.5+0.5*jnp.tanh(z*(C0+(C0*C1)*(z*z))))
def gelu2(z):
    z2=z*z
    t=jnp.tanh(z*(C0+(C0*C1)*z2))
    h=0.5+0.5*t
    x=z*h
    return x,h+x*(1-t)*(C0+(3*C0*C1)*z2)
def gelu3(z):
    z2=z*z
    t=jnp.tanh(z*(C0+(C0*C1)*z2))
    u1=C0+(3*C0*C1)*z2
    h=0.5+0.5*t
    h1=h*(1-t)*u1
    x=z*h
    return x,h+z*h1,2*h1+z*(h*(1-t)*(6*C0*C1)*z-2*t*u1*h1)
def lane_masks(C,H,R):
    lane=lax.broadcasted_iota(jnp.int32,(R,C*H),1)
    return [(lane>=H*c)&(lane<H*c+H) for c in range(C)]
def expand(C,x,masks):
    if C==1: return x
    zero=jnp.zeros((B,x.shape[1]),x.dtype)
    return jnp.concatenate([jnp.where(masks[c],x[B*j:B*j+B],zero) for j in range(x.shape[0]//B) for c in range(C)],0)
def collapse(C,x,masks):
    if C==1: return x
    rows=[]
    for j in range(x.shape[0]//(B*C)):
        y=x[B*C*j:B*C*j+B]
        for c in range(1,C): y=jnp.where(masks[c],x[B*(C*j+c):B*(C*j+c)+B],y)
        rows.append(y)
    return jnp.concatenate(rows,0) if len(rows)>1 else rows[0]
def tile_rows(C,x,n):
    t=jnp.concatenate([jnp.broadcast_to(x[c:c+1],(B,x.shape[1])) for c in range(C)],0)
    return jnp.concatenate([t]*n,0) if n>1 else t
def fill_masks(C,TRI,BLK,back):
    n=CH*C
    r=lax.broadcasted_iota(jnp.int32,(n,n),0); c=lax.broadcasted_iota(jnp.int32,(n,n),1)
    rs,cs=r//(B*C),c//(B*C)
    same=((r//B)%C)==((c//B)%C)
    tri=same&((cs<rs)|((cs==rs)&((c%B)<=(r%B))))
    TRI[...]=jnp.where(tri,1.0,0.0)
    BLK[...]=jnp.where(same&(cs<rs),1.0,0.0)
    if back is not None: back[...]=jnp.where(same&(cs>rs),1.0,0.0)
def ones_of(C,H):
    r=lax.broadcasted_iota(jnp.int32,(C*H,C*H),0); c=lax.broadcasted_iota(jnp.int32,(C*H,C*H),1)
    return jnp.where((r//H)==(c//H),1.0/H,0.0).astype(LOW)
def sums_of(C):
    r=lax.broadcasted_iota(jnp.int32,(C,CH*C),0); c=lax.broadcasted_iota(jnp.int32,(C,CH*C),1)
    return jnp.where(((c//B)%C)==r,1.0,0.0).astype(LOW)
def stack_col(C,r):
    return jnp.concatenate([r[B*j:B*j+B,c:c+1] for j in range(r.shape[0]//B) for c in range(C)],0)
def pair_cols(C,H,r,masks):
    y=jnp.broadcast_to(r[:,0:1],(r.shape[0],C*H))
    for c in range(1,C): y=jnp.where(masks[c],r[:,c:c+1],y)
    return y

def rates(C,x_ref,own_ref,H):
    rows=[x_ref[0,CH+c:CH+c+1,:CH].astype(F)+own_ref[c,2*H+1:2*H+2,3*H:3*H+1] for c in range(C)]
    rows=jnp.concatenate(rows+[jnp.zeros((CH-C,CH),F)],0)
    return (jax.nn.sigmoid(rows)*(RATE_SCALE/H)).T

def pair_row(C,H,own_ref,k):
    return jnp.concatenate([own_ref[c,2*H+1:2*H+2,k*H:k*H+H] for c in range(C)],1)

def fwd_kernel(C,H,x_ref,own_ref,
               o_ref,z1_ref,p_ref,zc_ref,z1q_ref,zq_ref,us_ref,w1s_ref,
               W1,B1,U,B2,TRI,BLK,S1,S2,X2,KK,BASE):
    W=C*H; SB=B*C
    @pl.when(pl.program_id(0)==0)
    def _():
        for c in range(C):
            W1[H*c:H*c+H]=own_ref[c,:H]
            u=own_ref[c,H:2*H]
            U[H*c:H*c+H]=u-jnp.sum(u,0,keepdims=True)*(1.0/H)
            B1[c:c+1]=own_ref[c,2*H:2*H+1]
        raw=[own_ref[c,2*H+1:2*H+2,:H] for c in range(C)]
        B2[...]=jnp.concatenate([v-jnp.sum(v,1,keepdims=True)*(1.0/H) for v in raw],1)
        fill_masks(C,TRI,BLK,None)
    m16=lane_masks(C,H,B); m128=lane_masks(C,H,CH)
    ones=ones_of(C,H)
    K=x_ref[0,:CH,W:2*W]
    Kst=expand(C,K,m16); Qst=expand(C,x_ref[0,:CH,:W],m16)
    gam=pair_row(C,H,own_ref,1); bet=pair_row(C,H,own_ref,2); g2=gam*gam
    T=(bet+K.astype(F)-x_ref[0,:CH,2*W:].astype(F))*gam
    R=rates(C,x_ref,own_ref,H)
    RP=pair_cols(C,H,R,m128)
    w1b=W1[...].astype(LOW); w1s_ref[0]=w1b
    b1r=tile_rows(C,B1[...],1)
    uf=U[...]; ub=uf.astype(LOW); u0=ub
    b2=B2[...]; b20=b2
    KK[...]=((nt(Kst,Kst)+1.0)*BLK[...]).astype(LOW)
    BASE[...]=nn(Kst,w1b)
    CT=nn(T,ones)
    g2m=nn(jnp.broadcast_to(g2,(8,W)),ones)[0:1]
    for j in range(NB):
        sl=slice(B*j,B*j+B); st=slice(SB*j,SB*j+SB)
        z1=BASE[st]+b1r
        if j>0: z1=z1-nn(KK[st,:SB*j],S1[:SB*j])
        x2,g1=gelu2(z1)
        x2b=x2.astype(LOW)
        zc=collapse(C,nt(x2b,ub),m16)+b2
        t=T[sl]; zz=zc*zc; zg=zc*g2; ct=CT[sl]; rr=RP[sl]
        mm=nn(jnp.concatenate([zc,zz,zg,zz*g2,zc*t],0),ones)
        mu=mm[0:B]; mzz=mm[B:2*B]; mzg=mm[2*B:3*B]; mzzg=mm[3*B:4*B]; mzt=mm[4*B:]
        s=lax.rsqrt(mzz-mu*mu+EPS)
        m1=s*(mzg-mu*g2m)+ct
        m2=s*(s*(mzzg-2.0*mu*mzg+mu*mu*g2m)+mzt-mu*ct)
        zc=zc-mu
        d2=s*(zc*s*(g2-m2)+(t-m1))
        P=nn(expand(C,d2,m16),ub)
        s1=(P*(g1*stack_col(C,R[sl]))).astype(LOW)
        s2=d2*rr
        s2b=expand(C,s2,m16).astype(LOW)
        S1[st]=s1; S2[st]=s2b; X2[st]=x2b
        z1_ref[st]=z1; p_ref[st]=P; zc_ref[sl]=zc
        us_ref[0,j]=ub
        uf=uf-tn(s2b,x2b); ub=uf.astype(LOW)
        b2=b2-jnp.sum(s2,0,keepdims=True)
    U[...]=uf; B2[...]=b2
    S1v=S1[...]
    W1[...]=W1[...]-tn(Kst,S1v)
    B1[...]=B1[...]-nn(sums_of(C),S1v)
    tri=TRI[...]
    A1=(nt(Qst,Kst)+1.0)*tri
    z1q=nn(Qst,w1b)+tile_rows(C,0.0+b1r_src(b1r,C),NB)-nn(A1,S1v)
    x2q=gelu1(z1q).astype(LOW)
    A2=(nt(x2q,X2[...])+1.0)*tri
    zq=collapse(C,nt(x2q,u0)-nn(A2,S2[...]),m16)+b20
    zq=zq-nn(zq,ones)
    yq=zq*lax.rsqrt(nn(zq*zq,ones)+EPS)
    o_ref[...]=(x_ref[0,:CH,:W].astype(F)+yq*gam+bet).astype(LOW)
    z1q_ref[...]=z1q; zq_ref[...]=zq

def b1r_src(b1r,C):
    return jnp.concatenate([b1r[B*c:B*c+1] for c in range(C)],0)

def fwd_scan(x,own):
    n,tall,W=x.shape
    W//=3
    C=own.shape[0]; I=own.shape[2]; H=W//C; L=n*CH
    rows=lambda k,w: pl.BlockSpec((k,w),lambda i:(i,0))
    sd=jax.ShapeDtypeStruct
    V=pltpu.VMEM
    return pl.pallas_call(partial(fwd_kernel,C,H),grid=(n,),
        in_specs=[pl.BlockSpec((1,tall,3*W),lambda i:(i,0,0)),pl.BlockSpec(own.shape,lambda i:(0,0,0))],
        out_specs=[rows(CH,W),rows(C*CH,I),rows(C*CH,I),rows(CH,W),rows(C*CH,I),rows(CH,W),
            pl.BlockSpec((1,NB,W,I),lambda i:(i,0,0,0)),pl.BlockSpec((1,W,I),lambda i:(i,0,0))],
        out_shape=[sd((L,W),LOW),sd((C*L,I),F),sd((C*L,I),F),sd((L,W),F),sd((C*L,I),F),sd((L,W),F),sd((n,NB,W,I),LOW),sd((n,W,I),LOW)],
        scratch_shapes=[V((W,I),F),V((C,I),F),V((W,I),F),V((1,W),F),V((C*CH,C*CH),F),V((C*CH,C*CH),F),
            V((C*CH,I),LOW),V((C*CH,W),LOW),V((C*CH,I),LOW),V((C*CH,C*CH),LOW),V((C*CH,I),F)],
        compiler_params=pltpu.CompilerParams(vmem_limit_bytes=48*1024*1024),
    )(x,own)

SLOT=("BASE","DX2","X2","RG1","G1","RPG2","DS2Q","KK","YB","GB","DB","SB","M2B","RED","S2E","S1B","X2Q","DZQ","DZ1Q","DKQ","DQ","KST","QST","T0","RP","PG1","R")

def slot_shapes(C,W,I):
    m=C*CH
    V=pltpu.VMEM
    wide,pair,tall=V((m,I),F),V((CH,W),F),V((m,W),LOW)
    kinds=dict(BASE=wide,DX2=wide,X2=V((m,I),LOW),RG1=wide,G1=wide,RPG2=wide,DS2Q=pair,KK=V((m,m),LOW),YB=pair,GB=pair,DB=pair,SB=pair,M2B=pair,
        RED=V((4*CH,W),F),S2E=tall,S1B=V((m,I),LOW),X2Q=V((m,I),LOW),DZQ=tall,DZ1Q=V((m,I),LOW),DKQ=V((m,W),F),DQ=V((CH,W),LOW),KST=tall,QST=tall,
        T0=pair,RP=pair,PG1=wide,R=V((CH,CH),F))
    return [kinds[name] for name in SLOT]

def bwd_pre(C,H,ins,own_ref,S,TRI,BLKT,gam,bet,dgam_ref,dbet_ref,factor):
    x_ref,do_ref,z1_ref,p_ref,zc_ref,z1q_ref,zq_ref,us_ref,w1s_ref=ins
    W=C*H
    m16=lane_masks(C,H,B); m128=lane_masks(C,H,CH)
    ones=ones_of(C,H)
    g2=gam*gam
    K=x_ref[0,:CH,W:2*W]
    Kst=expand(C,K,m16); Qst=expand(C,x_ref[0,:CH,:W],m16)
    S["KST"][...]=Kst; S["QST"][...]=Qst
    R=rates(C,x_ref,own_ref,H)
    S["R"][...]=R
    RP=pair_cols(C,H,R,m128)
    S["RP"][...]=RP
    dO=do_ref[...].astype(F)
    zq=zq_ref[...]; sq=lax.rsqrt(nn(zq*zq,ones)+EPS); yq=zq*sq
    dyq=dO*gam
    rq=nn(jnp.concatenate([dyq,dyq*yq],0),ones)
    dzq=sq*(dyq-rq[:CH]-yq*rq[CH:])
    dzqb=expand(C,dzq.astype(LOW),m16)
    S["DZQ"][...]=dzqb
    dgam_ref[...]=dgam_ref[...]+factor*jnp.sum(dO*yq,0,keepdims=True)
    dbet_ref[...]=dbet_ref[...]+factor*jnp.sum(dO,0,keepdims=True)
    yield
    zc=zc_ref[...]
    s=lax.rsqrt(nn(zc*zc,ones)+EPS)
    y=zc*s
    t0=bet+K.astype(F)-x_ref[0,:CH,2*W:].astype(F)
    G=y*g2+t0*gam
    red=nn(jnp.concatenate([G,G*y,g2*y,g2*y*y],0),ones)
    m1=red[:CH]; m2=red[CH:2*CH]
    d2=s*(G-m1-y*m2)
    s2=expand(C,(d2*RP).astype(LOW),m16)
    S["YB"][...]=y; S["GB"][...]=G; S["DB"][...]=d2; S["SB"][...]=s; S["M2B"][...]=m2; S["RED"][...]=red; S["S2E"][...]=s2; S["T0"][...]=t0
    yield
    x2,g1,gg2=gelu3(z1_ref[...]); x2=x2.astype(LOW)
    P=p_ref[...]
    RS=stack_col(C,R)
    rg1=RS*g1
    s1=(P*rg1).astype(LOW)
    S["X2"][...]=x2; S["G1"][...]=g1; S["RG1"][...]=rg1; S["RPG2"][...]=RS*(P*gg2); S["PG1"][...]=P*g1; S["S1B"][...]=s1
    yield
    x2q,g1q=gelu2(z1q_ref[...]); x2q=x2q.astype(LOW)
    S["X2Q"][...]=x2q
    A2=((nt(x2q,S["X2"][...])+1.0)*TRI[...]).astype(LOW)
    dA2=(nt(dzqb,s2)*TRI[...]).astype(LOW)
    yield
    dx2q=nn(dzqb,us_ref[0,0])-nn(dA2,S["X2"][...])
    S["DX2"][...]=-tn(dA2,x2q)
    S["DS2Q"][...]=-collapse(C,tn(A2,dzqb),m16)
    dz1qb=(dx2q*g1q).astype(LOW)
    S["DZ1Q"][...]=dz1qb
    yield
    A1=((nt(Qst,Kst)+1.0)*TRI[...]).astype(LOW)
    dA1=(nt(dz1qb,S["S1B"][...])*TRI[...]).astype(LOW)
    S["KK"][...]=((nt(Kst,Kst)+1.0)*BLKT[...]).astype(LOW)
    yield
    S["DQ"][...]=(dO+collapse(C,nt(dz1qb,w1s_ref[0])-nn(dA1,Kst),m16)).astype(LOW)
    S["DKQ"][...]=tn(dA1,Qst)
    S["BASE"][...]=-tn(A1,dz1qb)
    yield

def bwd_steps(C,H,S,us_ref,u,w1,H1,h1,HU,h2,BLK,gam,bet,dgam_ref,dbet_ref,DZ1,DS1,DS2,DG,dx_ref,db_ref,o,side):
    W=C*H; SB=B*C
    m16=lane_masks(C,H,B); m128=lane_masks(C,H,CH)
    ones=ones_of(C,H); sums=sums_of(C)
    g2=gam*gam
    Kst=S["KST"][...]
    h1b=H1[...].astype(LOW)
    S["BASE"][...]=S["BASE"][...]-nn(Kst,h1b)-tile_rows(C,h1[...],NB)
    dk=nt(S["S1B"][...],h1b)+S["DKQ"][...]
    g2m=nn(jnp.broadcast_to(g2,(8,W)),ones)[0:1]
    hu=HU[...]; hh2=h2[...]
    for j in reversed(range(NB)):
        sl=slice(B*j,B*j+B); st=slice(SB*j,SB*j+SB)
        ub=us_ref[u,j]
        rr=S["RP"][sl]
        hub=hu.astype(LOW)
        x2j=S["X2"][st]
        ds1=S["BASE"][st]
        if j<NB-1: ds1=ds1-nn(S["KK"][st,SB*j+SB:],DZ1[SB*j+SB:])
        ds2=S["DS2Q"][sl]-collapse(C,nt(x2j,hub),m16)-hh2
        dx2=S["DX2"][st]-nn(S["S2E"][st],hub)
        dPb=(ds1*S["RG1"][st]).astype(LOW)
        e=rr*ds2+collapse(C,nt(dPb,ub),m16)
        s=S["SB"][sl]; m2=S["M2B"][sl]; y=S["YB"][sl]; g_=S["GB"][sl]; d2=S["DB"][sl]
        m1=S["RED"][sl]; gy=S["RED"][2*CH+B*j:2*CH+B*j+B]; gyy=S["RED"][3*CH+B*j:3*CH+B*j+B]
        ge=g2*e
        mm=nn(jnp.concatenate([e,e*y,e*d2,ge,ge*y],0),ones)
        a=mm[0:B]; b=mm[B:2*B]; cc=mm[2*B:3*B]; mge=mm[3*B:4*B]; mgey=mm[4*B:]
        dG=s*(e-a-y*b)
        mdY=s*(mge-a*g2m-b*gy-m2*a-b*m1)
        mdYY=s*(mgey-a*gy-b*gyy-2.0*b*m2)
        dZc=s*(g2*dG-s*(m2*e+g_*b)-mdY-y*(cc+mdYY))
        dZcb=expand(C,dZc.astype(LOW),m16)
        dx2=dx2+nn(dZcb,ub)
        dz1=(dx2*S["G1"][st]+ds1*S["RPG2"][st]).astype(LOW)
        DZ1[st]=dz1
        DS1[st]=ds1; DS2[sl]=ds2; DG[sl]=dG
        hu=hu+tn(jnp.concatenate([expand(C,d2.astype(LOW),m16),dZcb],0),jnp.concatenate([dPb,x2j],0))
        hh2=hh2+jnp.sum(dZc,0,keepdims=True)
        next(side,None)
    dz1=DZ1[...]
    M=(nt(dz1,S["S1B"][...])*BLK[...]).astype(LOW)
    dG=DG[...]; dGg=dG*gam
    dk=collapse(C,nt(dz1,w1)-dk-nn(M,Kst)-tn(M,Kst),m16)+dGg
    dx_ref[o,:CH,:W]=S["DQ"][...]
    dx_ref[o,:CH,W:2*W]=dk.astype(LOW)
    dx_ref[o,:CH,2*W:]=(-dGg).astype(LOW)
    dr1=jnp.sum(DS1[...]*S["PG1"][...],-1,keepdims=True)
    dr2=DS2[...]*S["DB"][...]
    lane=lax.broadcasted_iota(jnp.int32,(CH,CH),1)
    dr=jnp.zeros((CH,CH),F)
    for c in range(C):
        rows=[dr1[B*(C*j+c):B*(C*j+c)+B] for j in range(NB)]
        col=jnp.concatenate(rows,0)+jnp.sum(jnp.where(m128[c],dr2,0.0),-1,keepdims=True)
        dr=jnp.where(lane==c,col,dr)
    R=S["R"][...]
    dr=dr*R*(1.0-R*(H/RATE_SCALE))
    db_ref[...]=db_ref[...]+jnp.sum(dr,0,keepdims=True)
    dr=dr.T.astype(LOW)
    extra=dx_ref.shape[1]-CH
    dx_ref[o,CH:,:]=jnp.zeros((extra,3*W),LOW)
    dx_ref[o,CH:,:CH]=dr[:extra]
    dgam_ref[...]=dgam_ref[...]+jnp.sum(dG*(2*S["YB"][...]*gam+S["T0"][...]),0,keepdims=True)
    dbet_ref[...]=dbet_ref[...]+jnp.sum(dGg,0,keepdims=True)
    dz1qb=S["DZ1Q"][...]
    H1[...]=H1[...]+tn(Kst,dz1)+tn(S["QST"][...],dz1qb)
    h1[...]=h1[...]+nn(sums,dz1)+nn(sums,dz1qb)
    HU[...]=hu+tn(S["DZQ"][...],S["X2Q"][...])
    h2[...]=hh2+jnp.sum(collapse(C,S["DZQ"][...].astype(F),m16),0,keepdims=True)

def bwd_kernel(C,H,steps,*refs):
    first,near,far=refs[:9],refs[9:18],refs[18:27]
    us_ref,w1_ref,own_ref,dx_ref,H1,h1,HU,h2,dgam_ref,dbet_ref,db_ref,TRI,BLK,BLKT,DZ1,DS1,DS2,DG=refs[27:45]
    k=len(SLOT)
    even=dict(zip(SLOT,refs[45:45+k])); odd=dict(zip(SLOT,refs[45+k:]))
    gam=pair_row(C,H,own_ref,1); bet=pair_row(C,H,own_ref,2)
    @pl.when(pl.program_id(0)==0)
    def _():
        for ref in (H1,h1,HU,h2,dgam_ref,dbet_ref,db_ref): ref[...]=jnp.zeros_like(ref)
        fill_masks(C,TRI,BLK,BLKT)
        for _ in bwd_pre(C,H,first,own_ref,even,TRI,BLKT,gam,bet,dgam_ref,dbet_ref,1.0): pass
    more=jnp.where(pl.program_id(0)<steps-1,1.0,0.0)
    side=bwd_pre(C,H,near,own_ref,odd,TRI,BLKT,gam,bet,dgam_ref,dbet_ref,1.0)
    bwd_steps(C,H,even,us_ref,1,w1_ref[1],H1,h1,HU,h2,BLK,gam,bet,dgam_ref,dbet_ref,DZ1,DS1,DS2,DG,dx_ref,db_ref,1,side)
    side=bwd_pre(C,H,far,own_ref,even,TRI,BLKT,gam,bet,dgam_ref,dbet_ref,more)
    bwd_steps(C,H,odd,us_ref,0,w1_ref[0],H1,h1,HU,h2,BLK,gam,bet,dgam_ref,dbet_ref,DZ1,DS1,DS2,DG,dx_ref,db_ref,0,side)

def bwd_scan(x,own,do,z1,p,zc,z1q,zq,us,w1s):
    n,tall,W=x.shape
    W//=3
    C=own.shape[0]; I=own.shape[2]; H=W//C
    full=lambda *s: pl.BlockSpec(s,lambda i:(0,)*len(s))
    sd=jax.ShapeDtypeStruct
    V=pltpu.VMEM
    m=C*CH
    def chunk(at):
        rows=lambda k,w: pl.BlockSpec((k,w),lambda i:(at(i),0))
        return [pl.BlockSpec((1,tall,3*W),lambda i:(at(i),0,0)),rows(CH,W),rows(m,I),rows(m,I),rows(CH,W),rows(m,I),rows(CH,W),
            pl.BlockSpec((1,1,W,I),lambda i:(at(i),0,0,0)),pl.BlockSpec((1,W,I),lambda i:(at(i),0,0))]
    ins=(x,do,z1,p,zc,z1q,zq,us,w1s)
    return pl.pallas_call(partial(bwd_kernel,C,H,n//2),grid=(n//2,),
        in_specs=chunk(lambda i:n-1)+chunk(lambda i:n-2-2*i)+chunk(lambda i:jnp.maximum(n-3-2*i,0))+[
            pl.BlockSpec((2,NB,W,I),lambda i:(n//2-1-i,0,0,0)),pl.BlockSpec((2,W,I),lambda i:(n//2-1-i,0,0)),full(*own.shape)],
        out_specs=[pl.BlockSpec((2,tall,3*W),lambda i:(n//2-1-i,0,0)),full(W,I),full(C,I),full(W,I),full(1,W),full(1,W),full(1,W),full(1,CH)],
        out_shape=[sd((n,tall,3*W),LOW),sd((W,I),F),sd((C,I),F),sd((W,I),F),sd((1,W),F),sd((1,W),F),sd((1,W),F),sd((1,CH),F)],
        scratch_shapes=[V((m,m),F),V((m,m),F),V((m,m),F),V((m,I),LOW),V((m,I),F),V((CH,W),F),V((CH,W),F)]+slot_shapes(C,W,I)*2,
        compiler_params=pltpu.CompilerParams(vmem_limit_bytes=48*1024*1024),
    )(*ins,*ins,*ins,us,w1s,own)

RATE_SCALE = 0.25
NORM_EPS = 1e-05


def smooth_act(value):
    return 0.5 * value * (1.0 + jnp.tanh(C0 * (value + C1 * value * value * value)))


def root_norm(value, gain):
    return value * lax.rsqrt(jnp.mean(value * value, -1, keepdims=True) + NORM_EPS) * gain


def layer_norm(value, gain, bias):
    centre = value - jnp.mean(value, -1, keepdims=True)
    return centre * lax.rsqrt(jnp.mean(centre * centre, -1, keepdims=True) + NORM_EPS) * gain + bias


def gated_branch(mixed, gate_pre, gain, bias):
    return layer_norm(mixed, gain, bias) * smooth_act(gate_pre)


def swish_product(gate_val, linear_val):
    return jax.nn.silu(gate_val) * linear_val


def matmul(left, right):
    return jnp.dot(left, right, preferred_element_type=F)


def flip(array, axis, mask):
    peers = lax.axis_size(axis)
    return lax.ppermute(array, axis, [(i, i ^ mask) for i in range(peers)])


def masks_of(axis):
    masks = []
    while 1 << len(masks) < lax.axis_size(axis):
        masks.append(1 << len(masks))
    return masks


def side(axis, mask):
    return (lax.axis_index(axis) // mask) % 2


def gather_near(array, axis):
    for mask in reversed(masks_of(axis)):
        array = jnp.concatenate([array, flip(array, axis, mask)], 0)
    return array


def scatter_once(array, axis, mask):
    half = array.shape[0] // 2
    return array[:half].astype(F) + flip(array[half:].astype(LOW), axis, mask).astype(F)


def scatter_near(array, axis):
    for mask in masks_of(axis):
        array = scatter_once(array, axis, mask)
    return array


def halve(array, axis, mask, dim):
    bit = side(axis, mask)
    mine = lax.dynamic_index_in_dim(array, bit, dim, keepdims=False)
    other = lax.dynamic_index_in_dim(array, 1 - bit, dim, keepdims=False)
    return mine.astype(F) + flip(other.astype(LOW), axis, mask).astype(F)


def double(array, axis, mask):
    got = flip(array, axis, mask)
    upper = side(axis, mask) == 1
    return jnp.stack([jnp.where(upper, got, array), jnp.where(upper, array, got)])


def project_kernel(each, blocks, x_ref, g_ref, wq_ref, wk_ref, wv_ref, wr_ref, wg_ref, s_ref, n_ref, p_ref, LT):
    step = pl.program_id(0)
    rows, width = x_ref.shape
    span = wq_ref.shape[1]

    @pl.when(step == 0)
    def _():
        x = x_ref[...].astype(F)
        scale = lax.rsqrt(jnp.sum(x * x, -1, keepdims=True) * (1.0 / width) + NORM_EPS)
        n_ref[...] = (x * scale * g_ref[...]).astype(LOW)
        logits = nn(n_ref[...], wr_ref[...]).astype(LOW).astype(F)
        heads = logits.shape[1]
        logits = jnp.concatenate([logits, jnp.zeros((rows, 128 - heads), F)], 1)
        LT[...] = logits.T

    normed = n_ref[...]
    extra = s_ref.shape[1] - rows
    s_ref[0, rows:, :] = jnp.zeros((extra, 3 * span), LOW)

    @pl.when(step < blocks)
    def _():
        for i, w_ref in enumerate((wq_ref, wk_ref, wv_ref)):
            s_ref[0, :rows, span * i : span * i + span] = nn(normed, w_ref[...]).astype(LOW)
        r = lax.broadcasted_iota(jnp.int32, (extra, rows), 0)
        c = lax.broadcasted_iota(jnp.int32, (extra, rows), 1)
        pick = jnp.where((r < each) & (c == step * each + r), 1.0, 0.0)
        s_ref[0, rows:, :rows] = nn(pick, LT[...]).astype(LOW)
        p_ref[...] = nn(normed, wg_ref[...])

    @pl.when(step >= blocks)
    def _():
        s_ref[0, :rows, :] = jnp.zeros((rows, 3 * span), LOW)


def project(x, gain, wq, wk, wv, wr, wg, seqs, each, extra):
    rows, width = x.shape
    span = each * (width // wr.shape[1])
    blocks = width // span
    column = pl.BlockSpec((width, span), lambda s: (0, jnp.minimum(s, blocks - 1)))
    full = lambda *shape: pl.BlockSpec(shape, lambda s: (0,) * len(shape))
    sd = jax.ShapeDtypeStruct
    return pl.pallas_call(
        partial(project_kernel, each, blocks),
        grid=(seqs,),
        in_specs=[full(rows, width), full(1, width), column, column, column, full(*wr.shape), column],
        out_specs=[
            pl.BlockSpec((1, rows + extra, 3 * span), lambda s: (s, 0, 0)),
            full(rows, width),
            pl.BlockSpec((rows, span), lambda s: (0, jnp.minimum(s, blocks - 1))),
        ],
        out_shape=[sd((seqs, rows + extra, 3 * span), LOW), sd((rows, width), LOW), sd((rows, width), F)],
        scratch_shapes=[pltpu.VMEM((128, 128), F)],
        compiler_params=pltpu.CompilerParams(vmem_limit_bytes=48 * 1024 * 1024),
    )(x, gain[None], wq, wk, wv, wr, wg)


def summed(fed_parts, early):
    seqs = lax.axis_size("seq")
    early = early.reshape(seqs, -1, early.shape[-1])
    early = lax.all_to_all(early, "seq", split_axis=0, concat_axis=0, tiled=True)
    return jnp.concatenate(
        [jnp.sum(fed_parts.astype(F), 0).astype(LOW), jnp.sum(early.astype(F), 0).astype(LOW)], 0
    )


def share_rows(every_normed, back_sent, state_g, vectors, fed_parts, early, heads, local_heads, head, weights_in):
    seqs, tps = lax.axis_size("seq"), lax.axis_size("tp")
    width = every_normed.shape[1]
    lanes = back_sent.shape[2]
    rows = every_normed.shape[0] // seqs
    span = lanes // 3
    each = span // head
    first_g, first_bias_g, second_g, second_bias_g, gain_g, shift_g, bias_g = state_g
    inner = first_g.shape[1]
    fed = lax.all_gather(summed(fed_parts, early), "seq", axis=0, tiled=False)
    back = lax.all_to_all(back_sent, "seq", split_axis=0, concat_axis=0, tiled=True)
    qkv_g = back_sent[:, :rows].reshape(seqs * rows, lanes)
    logit_g = back_sent[:, rows : rows + each, :rows].transpose(1, 0, 2).reshape(each, seqs * rows)
    columns = jnp.einsum("ld,le->de", every_normed, qkv_g, preferred_element_type=F)
    rate_column = jnp.einsum("el,ld->ed", logit_g, every_normed, preferred_element_type=F)
    first_g = first_g.reshape(each, head, inner)
    second_g = second_g.reshape(each, head, inner)
    second_g = second_g - jnp.mean(second_g, 1, keepdims=True)
    second_bias_g, gain_g, shift_g = [a.reshape(each, head) for a in (second_bias_g, gain_g, shift_g)]
    second_bias_g = second_bias_g - jnp.mean(second_bias_g, 1, keepdims=True)
    bias_g = bias_g[0, :each]
    tail = jnp.concatenate(
        [second_bias_g, gain_g, shift_g, jnp.pad(bias_g[:, None], ((0, 0), (0, inner - 3 * head - 1)))], -1
    )
    states = jnp.concatenate(
        [
            jnp.stack([first_g, second_g], 1),
            jnp.stack([first_bias_g, tail], 1)[:, :, None],
            jnp.zeros((each, 2, 7, inner), F),
        ],
        2,
    )
    state_rows = states.size // lanes // tps
    rate_rows = rate_column.size // lanes // tps
    vectors = jnp.concatenate([vectors, jnp.zeros_like(vectors[:1])], 0)
    vector_rows = vectors.size // lanes // tps
    rest = jnp.concatenate(
        [rate_column.reshape(tps, rate_rows, lanes), vectors.reshape(tps, vector_rows, lanes)], 1
    )
    late = jnp.concatenate(
        [
            columns.reshape(tps, width // tps, lanes),
            states.reshape(tps, state_rows, lanes),
            jnp.pad(rest, ((0, 0), (0, 16 - rate_rows - vector_rows), (0, 0))),
        ],
        1,
    )
    late = lax.psum_scatter(late.astype(LOW), "tp", scatter_dimension=0, tiled=True)
    late = lax.all_gather(late, ("seq", "tp"), axis=0, tiled=True).reshape((seqs, tps) + late.shape[1:])
    weights = late[:, :, : width // tps].reshape(seqs, tps, width // tps, 3, span)
    weights = weights.transpose(3, 1, 2, 0, 4).reshape(3, width, seqs * span)[:, :, :width].astype(F)
    states = late[:, :, width // tps : width // tps + state_rows].reshape(seqs * each, 2, head + 8, inner)[:heads]
    states = lax.dynamic_slice_in_dim(states, lax.axis_index("tp") * local_heads, local_heads, 0).astype(F)
    rest = late[:, :, width // tps + state_rows :]
    rate_weight_grad = rest[:, :, :rate_rows].reshape(seqs * each, width)[:heads].T.astype(F)
    vectors = rest[:, :, rate_rows : rate_rows + vector_rows].reshape(seqs, 4, width)
    vectors = jnp.sum(vectors.astype(F), 0)
    norm_gain_grad = jnp.sum(sum(weights[i] * weights_in[i].astype(F) for i in range(3)), -1)
    return weights, states[:, :, :head], states[:, :, head], rate_weight_grad, vectors, fed, back, norm_gain_grad


def pack_kernel(head, me_ref, n_ref, x_ref, w_ref, wb_ref, u_ref, ub_ref, g_ref, s_ref, r_ref, v_ref, keep_ref, sent_ref, COL, UC, SMALL):
    seqs, _, lanes = x_ref.shape
    rows = n_ref.shape[0] // seqs
    width = n_ref.shape[1]
    here = width // 4
    normed = n_ref[...]
    COL[...] = tn(normed, x_ref[:, :rows].reshape(seqs * rows, lanes))
    rate = jnp.zeros((16, width), F)
    for s in range(seqs):
        logit = x_ref[s, rows : rows + 16, :rows]
        rate = rate + nn(logit, n_ref[rows * s : rows * s + rows])
    SMALL[...] = jnp.zeros_like(SMALL)
    for c in range(2):
        lane = slice(head * c, head * c + head)
        u = u_ref[lane]
        UC[lane] = u - jnp.sum(u, 0, keepdims=True) * (1.0 / head)
        ub = ub_ref[:, lane]
        ub = ub - jnp.sum(ub, 1, keepdims=True) * (1.0 / head)
        for i in range(2):
            SMALL[2 * c, i : i + 1] = wb_ref[c : c + 1, 128 * i : 128 * i + 128]
        SMALL[2 * c + 1, 0:1] = jnp.concatenate([ub, g_ref[:, lane]], 1)
        SMALL[2 * c + 1, 1:2] = jnp.concatenate([s_ref[:, lane], jnp.broadcast_to(r_ref[:, c : c + 1], (1, head))], 1)
    for t in range(4):
        for i in range(3):
            at = (t % 2) * 384 + 128 * i
            SMALL[t, 2 + i : 3 + i] = rate[t // 2 : t // 2 + 1, at : at + 128]
        for i in range(5):
            k = 5 * t + i
            if k < 18:
                SMALL[t, 5 + i : 6 + i] = v_ref[k // 6 : k // 6 + 1, (k % 6) * 128 : (k % 6) * 128 + 128]
    for place, o in enumerate((0, 2, 1, 3)):
        out = (keep_ref, sent_ref)[place // 2].at[place % 2]
        t = me_ref[0] ^ o
        out[:here] = COL[pl.ds(pl.multiple_of(t * here, 16), here)].astype(LOW)
        for n in range(9):
            c, k, half = n // 4, (n // 2) % 2, n % 2
            if n < 8:
                tile = (w_ref, UC)[k][pl.ds(pl.multiple_of(head * c + 16 * t, 16), 16), 128 * half : 128 * half + 128]
            else:
                tile = SMALL[t]
            row, lane = here + 16 * (n // 3), 128 * (n % 3)
            out[row : row + 16, lane : lane + 128] = tile.astype(LOW)


def last_kernel(seqs, each, heads, local_heads, me_ref, a_ref, b_ref, wq_ref, wk_ref, wv_ref,
                q_ref, k_ref, v_ref, n_ref, s_ref, r_ref):
    cut = a_ref.shape[3]
    span = a_ref.shape[4] // 3
    below = q_ref.shape[0] - cut
    for s in range(seqs):
        if s * each >= heads:
            continue
        x, q = s % 2, ((s >> 1) & 1) * 2 + (s >> 2)
        for i, o_ref in enumerate((q_ref, k_ref, v_ref)):
            o_ref[:cut, span * s : span * s + span] = a_ref[0, 0, 4 * x + q, :, span * i : span * i + span].astype(F)
            o_ref[cut:, span * s : span * s + span] = b_ref[0, x, 0, q, :below, span * i : span * i + span].astype(F)
    total = q_ref[...] * wq_ref[...].astype(F)
    for o_ref, w_ref in ((k_ref, wk_ref), (v_ref, wv_ref)):
        total = total + o_ref[...] * w_ref[...].astype(F)
    n_ref[...] = jnp.sum(total, -1, keepdims=True)

    def tile(x, q, n):
        return b_ref[0, x, 0, q, below + 16 * (n // 3) : below + 16 * (n // 3) + 16, 128 * (n % 3) : 128 * (n % 3) + 128]

    for i in range(local_heads):
        h = me_ref[0] * local_heads + i
        s = h // each
        upper = lax.rem(h, each) == 1
        x = lax.rem(s, 2)
        q = lax.rem(s // 2, 2) * 2 + s // 4
        for k in range(2):
            for j in range(2):
                low = tile(x, q, k * 2 + j).astype(F)
                high = tile(x, q, 4 + k * 2 + j).astype(F)
                s_ref[i, k, :, 128 * j : 128 * j + 128] = jnp.where(upper, high, low)
    for s in range(seqs):
        r_ref[0, s] = tile(s % 2, ((s >> 1) & 1) * 2 + (s >> 2), 8).astype(F)


def share_tiles(every_normed, back_sent, state_g, vectors, fed_parts, early, heads, local_heads, head, weights_in):
    seqs, tps = lax.axis_size("seq"), lax.axis_size("tp")
    width = every_normed.shape[1]
    lanes = back_sent.shape[2]
    each = 2
    inner = state_g[0].shape[1]
    here = width // tps
    share = here + 48
    me = lax.axis_index("tp").astype(jnp.int32).reshape(1)
    sd = jax.ShapeDtypeStruct
    late, late_sent = pl.pallas_call(
        partial(pack_kernel, head),
        in_specs=[pl.BlockSpec(memory_space=pltpu.SMEM)] + [pl.BlockSpec(memory_space=pltpu.VMEM)] * 10,
        out_specs=[pl.BlockSpec(memory_space=pltpu.VMEM)] * 2,
        out_shape=[sd((2, share, lanes), LOW)] * 2,
        scratch_shapes=[
            pltpu.VMEM((width, lanes), F),
            pltpu.VMEM((each * head, inner), F),
            pltpu.VMEM((4, 16, 128), F),
        ],
        compiler_params=pltpu.CompilerParams(vmem_limit_bytes=48 * 1024 * 1024),
    )(me, every_normed, back_sent, *state_g, vectors)
    late = late.astype(F) + flip(late_sent, "tp", 1).astype(F)
    late, fed_parts = lax.optimization_barrier((late, fed_parts))
    fed = summed(fed_parts, early)
    late = scatter_once(late, "tp", 2).astype(LOW)[0]
    late, fed = lax.optimization_barrier((late, fed))
    fed = lax.all_gather(fed, "seq", axis=0, tiled=False)
    late = double(late, "seq", 4)
    late = double(late, "seq", 2)
    late, back_sent = lax.optimization_barrier((late, back_sent))
    back = lax.all_to_all(back_sent, "seq", split_axis=0, concat_axis=0, tiled=True)
    cut = 128
    part_a, part_b = late[:, :, :cut], late[:, :, cut:]
    part_a, part_b = double(part_a, "seq", 1), double(part_b, "tp", 2)
    part_a, part_b, fed = lax.optimization_barrier((part_a, part_b, fed))
    part_a, part_b = double(part_a, "tp", 2), double(part_b, "seq", 1)
    part_a, part_b = double(part_a, "tp", 1), double(part_b, "tp", 1)
    part_a = part_a.reshape(2, 2, seqs, cut, lanes)
    part_b = part_b.reshape(2, 2, 2, seqs // 2, share - cut, lanes)
    square = pl.BlockSpec((here, width), lambda t: (t, 0))
    sd = jax.ShapeDtypeStruct
    *weights, norm_gain_grad, head_w, small = pl.pallas_call(
        partial(last_kernel, seqs, each, heads, local_heads),
        grid=(tps,),
        in_specs=[
            pl.BlockSpec(memory_space=pltpu.SMEM),
            pl.BlockSpec((1, 1, seqs, cut, lanes), lambda t: (t % 2, t // 2, 0, 0, 0)),
            pl.BlockSpec((1, 2, 1, seqs // 2, share - cut, lanes), lambda t: (t % 2, 0, t // 2, 0, 0, 0)),
            square, square, square,
        ],
        out_specs=[
            square, square, square,
            pl.BlockSpec((here, 1), lambda t: (t, 0)),
            pl.BlockSpec((local_heads, 2, head // tps, inner), lambda t: (0, 0, t, 0)),
            pl.BlockSpec((1, seqs, 16, 128), lambda t: (t, 0, 0, 0)),
        ],
        out_shape=[sd((width, width), F)] * 3
        + [sd((width, 1), F), sd((local_heads, 2, head, inner), F), sd((tps, seqs, 16, 128), F)],
        compiler_params=pltpu.CompilerParams(vmem_limit_bytes=48 * 1024 * 1024),
    )(me, part_a, part_b, *weights_in)
    head_t = small[:, :, :2].transpose(1, 0, 2, 3).reshape(seqs * each, 2, inner)
    head_t = lax.dynamic_slice_in_dim(head_t, me[0] * local_heads, local_heads, 0)
    rate_weight_grad = small[:, :, 2:5].transpose(1, 0, 2, 3).reshape(seqs * each, width)[:heads].T
    vectors = jnp.sum(small[:, :, 5:10], 1).reshape(-1)[: 3 * width].reshape(3, width)
    return weights, head_w, head_t, rate_weight_grad, vectors, fed, back, norm_gain_grad[:, 0]


def on_device(
    tokens, norm_gain, query_weight, key_weight, value_weight, rate_weight, rate_bias,
    first_weight, first_bias, second_weight, second_bias, inner_gain, inner_bias,
    branch_gate, output_weight, post_gain, post_bias, feed_gain, feed_gate, feed_linear,
    feed_down, cotangent,
):
    seqs = lax.axis_size("seq")
    rank = lax.axis_index("seq")
    heads = rate_weight.shape[1]
    local_heads, head, inner = first_weight.shape
    rows = tokens.shape[1]
    width = tokens.shape[2]
    each = -(-heads // seqs)
    span = each * head
    length = seqs * rows
    extra = -(-each // 16) * 16

    def to_chains(array):
        padded = jnp.pad(array, ((0, 0), (0, seqs * span - array.shape[1])))
        return padded.reshape(rows, seqs, span).transpose(1, 0, 2)

    def from_chains(array):
        return array.transpose(1, 0, 2).reshape(rows, seqs * span)[:, :width]

    def swap(array):
        return lax.all_to_all(array, "seq", split_axis=0, concat_axis=0, tiled=True)

    tail = jnp.concatenate(
        [second_bias, inner_gain, inner_bias, jnp.pad(rate_bias[:, None], ((0, 0), (0, inner - 3 * head - 1)))], -1
    )
    packed = jnp.concatenate(
        [
            first_weight,
            jnp.swapaxes(second_weight, 1, 2),
            first_bias[:, None],
            tail[:, None],
            jnp.zeros((local_heads, 6, inner), F),
        ],
        1,
    )
    every = lax.all_gather(packed, "tp", axis=0, tiled=True)
    own = lax.dynamic_slice_in_dim(every, jnp.minimum(rank * each, heads - each), each, 0)

    residual = tokens[0].astype(F)
    normed_val, norm_pull = jax.vjp(root_norm, residual, norm_gain)
    down_grad = cotangent[0]
    grad_out = down_grad.astype(F)
    every_grad = gather_near(down_grad, "tp")
    if span % 128 == 0 and width % span == 0 and rows == 128:
        sent, normed, gate_pre = project(
            tokens[0], norm_gain, query_weight, key_weight, value_weight, rate_weight, branch_gate, seqs, each, extra
        )
    else:
        normed = normed_val.astype(LOW)
        query_tok = matmul(normed, query_weight).astype(LOW)
        keys_tok = matmul(normed, key_weight).astype(LOW)
        values_tok = matmul(normed, value_weight).astype(LOW)
        logits_tok = matmul(normed, rate_weight).astype(LOW)
        gate_pre = matmul(normed, branch_gate)
        logit_rows = jnp.pad(logits_tok.T, ((0, seqs * each - heads), (0, 0))).reshape(seqs, each, rows)
        logit_rows = jnp.pad(logit_rows, ((0, 0), (0, extra - each), (0, 3 * span - rows)))
        sent = [to_chains(query_tok), to_chains(keys_tok), to_chains(values_tok)]
        sent = jnp.concatenate([jnp.concatenate(sent, -1), logit_rows], 1)
    got = swap(sent)

    every_normed = lax.all_gather(normed, "seq", axis=0, tiled=True)
    outs, *kept = fwd_scan(got, own)
    outs, every_normed, every_grad = lax.optimization_barrier((outs, every_normed, every_grad))
    mixed_tok = from_chains(swap(outs.reshape(seqs, rows, span))).astype(F)

    branch_val, branch_pull = jax.vjp(gated_branch, mixed_tok, gate_pre, post_gain, post_bias)
    branch_in = branch_val.astype(LOW)
    middle = residual + matmul(branch_in, output_weight)
    feed_val, feed_pull = jax.vjp(root_norm, middle, feed_gain)
    feed_in = feed_val.astype(LOW)
    every_in = gather_near(feed_in, "tp")
    gate_val = matmul(every_in, feed_gate)
    linear_val = matmul(every_in, feed_linear)
    act_val, act_pull = jax.vjp(swish_product, gate_val, linear_val)
    hidden = act_val.astype(LOW)

    hidden_grad = jnp.einsum("td,fd->tf", every_grad, feed_down, preferred_element_type=F)
    gate_grad, linear_grad = act_pull(hidden_grad)
    gate_low = gate_grad.astype(LOW)
    linear_low = linear_grad.astype(LOW)
    input_part = jnp.einsum("tf,df->td", gate_low, feed_gate, preferred_element_type=F) + jnp.einsum(
        "tf,df->td", linear_low, feed_linear, preferred_element_type=F
    )
    feed_in_grad = scatter_near(input_part, "tp")
    middle_part, feed_gain_grad = feed_pull(feed_in_grad)
    middle_grad = grad_out + middle_part
    out_low = middle_grad.astype(LOW)
    branch_grad = jnp.einsum("te,de->td", out_low, output_weight, preferred_element_type=F)
    mixed_grad, gate_pre_grad, post_gain_grad, post_bias_grad = branch_pull(branch_grad)
    out_grad_c = swap(to_chains(mixed_grad.astype(LOW))).reshape(length, span)

    second_part = matmul(hidden, feed_down).astype(LOW)
    second_part, out_grad_c = lax.optimization_barrier((second_part, out_grad_c))
    second_out = scatter_near(second_part, "tp")
    result = (middle + second_out).astype(LOW)[None]

    feed_down_grad = jnp.einsum("tf,td->fd", hidden, every_grad, preferred_element_type=F)
    both_low = jnp.concatenate([gate_low, linear_low], 1)
    feed_both_grad = jnp.einsum("tf,td->fd", both_low, every_in, preferred_element_type=F)
    gate_low_pre = gate_pre_grad.astype(LOW)
    out_low, gate_low_pre, out_grad_c = lax.optimization_barrier((out_low, gate_low_pre, out_grad_c))
    tps = lax.axis_size("tp")
    lefts = jnp.stack([branch_in, normed])
    rights = jnp.stack([out_low, gate_low_pre])
    part_rows = 2 * width // tps
    orders = [0]
    for mask in reversed(masks_of("tp")):
        orders = orders + [o + mask for o in orders]
    parts = []
    for o in orders:
        owner = lax.axis_index("tp") ^ o
        which, place = owner % 2, owner // 2
        left = lax.dynamic_slice(lefts, (which, 0, place * part_rows), (1, rows, part_rows))
        right = lax.dynamic_index_in_dim(rights, which, 0, keepdims=True)
        parts.append((left, right))
    half = tps // 2

    def products(chosen):
        left = jnp.concatenate([p[0] for p in chosen], 0)
        right = jnp.concatenate([p[1] for p in chosen], 0)
        return jnp.einsum("jtd,jte->jde", left, right, preferred_element_type=F)

    early_sent = products(parts[half:]).astype(LOW)
    early = products(parts[:half]) + flip(early_sent, "tp", 1).astype(F)
    fed_parts = jnp.concatenate(
        [
            feed_both_grad.astype(LOW).reshape(seqs, -1, width),
            feed_down_grad.astype(LOW).reshape(seqs, -1, width),
        ],
        1,
    )
    fed_parts, early, out_grad_c = lax.optimization_barrier((fed_parts, early.astype(LOW), out_grad_c))
    fed_parts = swap(fed_parts)
    for mask in masks_of("tp")[1:]:
        early = scatter_once(early, "tp", mask)

    back_sent, *state_g = bwd_scan(got, own, out_grad_c, *kept)
    early, back_sent = lax.optimization_barrier((early.astype(LOW), back_sent))
    vectors = jnp.stack([post_gain_grad, post_bias_grad, feed_gain_grad])
    share = share_tiles if each == 2 and tps == 4 and seqs == 8 else share_rows
    weights, head_w, head_t, rate_weight_grad, vectors, fed, back, norm_gain_grad = share(
        every_normed, back_sent, state_g, vectors, fed_parts, early, heads, local_heads, head,
        (query_weight, key_weight, value_weight),
    )
    query_low = from_chains(back[:, :rows, :span])
    keys_low = from_chains(back[:, :rows, span : 2 * span])
    values_low = from_chains(back[:, :rows, 2 * span :])
    logit_low = back[:, rows : rows + each, :rows].reshape(seqs * each, rows)[:heads].T

    normed_grad = (
        jnp.einsum("te,de->td", query_low, query_weight, preferred_element_type=F)
        + jnp.einsum("te,de->td", keys_low, key_weight, preferred_element_type=F)
        + jnp.einsum("te,de->td", values_low, value_weight, preferred_element_type=F)
        + jnp.einsum("te,de->td", logit_low, rate_weight, preferred_element_type=F)
        + jnp.einsum("te,de->td", gate_low_pre, branch_gate, preferred_element_type=F)
    )
    residual_part, unused = norm_pull(normed_grad)
    tokens_grad = (middle_grad + residual_part)[None]
    inner_units = feed_gate.shape[1]
    both = fed[:, : 2 * inner_units // seqs].reshape(2, inner_units, width).astype(F)
    down = fed[:, 2 * inner_units // seqs : 3 * inner_units // seqs].reshape(inner_units, width).astype(F)
    early = fed[:, 3 * inner_units // seqs :].reshape(-1, width)
    for mask in reversed(masks_of("tp")):
        early = double(early, "tp", mask)
    early = early.reshape(2, width, width).astype(F)
    norm_gain_grad = norm_gain_grad + jnp.sum(rate_weight_grad * rate_weight.astype(F), -1)
    norm_gain_grad = norm_gain_grad + jnp.sum(early[1] * branch_gate.astype(F), -1)
    norm_gain_grad = norm_gain_grad / norm_gain
    tail_sum = head_t[:, 1]
    return (
        result,
        tokens_grad,
        norm_gain_grad,
        weights[0],
        weights[1],
        weights[2],
        rate_weight_grad,
        tail_sum[:, 3 * head],
        head_w[:, 0],
        head_t[:, 0],
        jnp.swapaxes(head_w[:, 1], 1, 2),
        tail_sum[:, :head],
        tail_sum[:, head : 2 * head],
        tail_sum[:, 2 * head : 3 * head],
        early[1],
        early[0],
        vectors[0],
        vectors[1],
        vectors[2],
        both[0].T,
        both[1].T,
        down,
    )


def solution(mesh):
    in_specs = (
        P("tp", "seq", None),
        P(),
        P(),
        P(),
        P(),
        P(),
        P("tp"),
        P("tp", None, None),
        P("tp", None),
        P("tp", None, None),
        P("tp", None),
        P("tp", None),
        P("tp", None),
        P(),
        P(),
        P(),
        P(),
        P(),
        P(None, "tp"),
        P(None, "tp"),
        P("tp", None),
        P("tp", "seq", None),
    )
    out_specs = (
        P("tp", "seq", None),
        P("tp", "seq", None),
        P(),
        P(),
        P(),
        P(),
        P(),
        P("tp"),
        P("tp", None, None),
        P("tp", None),
        P("tp", None, None),
        P("tp", None),
        P("tp", None),
        P("tp", None),
        P(),
        P(),
        P(),
        P(),
        P(),
        P(None, "tp"),
        P(None, "tp"),
        P("tp", None),
    )
    return jax.shard_map(
        on_device, mesh=mesh, in_specs=in_specs, out_specs=out_specs, check_vma=False
    )
```

```python
from functools import partial

import jax
import jax.numpy as jnp
from jax import lax
from jax.sharding import PartitionSpec as P
from jax.experimental import pallas as pl
from jax.experimental.pallas import tpu as pltpu
from itertools import chain
C0=0.7978845608028654
C1=0.044715
EPS=1e-6
RATE_SCALE=0.25
B=16
CH=128
NB=CH//B
LOW=jnp.bfloat16
F=jnp.float32
def nn(a,b): return lax.dot_general(a.astype(LOW),b.astype(LOW),(((1,),(0,)),((),())),preferred_element_type=F)
def nt(a,b): return lax.dot_general(a.astype(LOW),b.astype(LOW),(((1,),(1,)),((),())),preferred_element_type=F)
def tn(a,b): return lax.dot_general(a.astype(LOW),b.astype(LOW),(((0,),(0,)),((),())),preferred_element_type=F)
def gelu1(z):
    return z*(0.5+0.5*jnp.tanh(z*(C0+(C0*C1)*(z*z))))
def gelu2(z):
    z2=z*z
    t=jnp.tanh(z*(C0+(C0*C1)*z2))
    h=0.5+0.5*t
    x=z*h
    return x,h+x*(1-t)*(C0+(3*C0*C1)*z2)
def gelu3(z):
    z2=z*z
    t=jnp.tanh(z*(C0+(C0*C1)*z2))
    u1=C0+(3*C0*C1)*z2
    h=0.5+0.5*t
    h1=h*(1-t)*u1
    x=z*h
    return x,h+z*h1,2*h1+z*(h*(1-t)*(6*C0*C1)*z-2*t*u1*h1)
def lane_masks(C,H,R):
    lane=lax.broadcasted_iota(jnp.int32,(R,C*H),1)
    return [(lane>=H*c)&(lane<H*c+H) for c in range(C)]
def expand(C,x,masks):
    if C==1: return x
    zero=jnp.zeros((B,x.shape[1]),x.dtype)
    return jnp.concatenate([jnp.where(masks[c],x[B*j:B*j+B],zero) for j in range(x.shape[0]//B) for c in range(C)],0)
def collapse(C,x,masks):
    if C==1: return x
    rows=[]
    for j in range(x.shape[0]//(B*C)):
        y=x[B*C*j:B*C*j+B]
        for c in range(1,C): y=jnp.where(masks[c],x[B*(C*j+c):B*(C*j+c)+B],y)
        rows.append(y)
    return jnp.concatenate(rows,0) if len(rows)>1 else rows[0]
def tile_rows(C,x,n):
    t=jnp.concatenate([jnp.broadcast_to(x[c:c+1],(B,x.shape[1])) for c in range(C)],0)
    return jnp.concatenate([t]*n,0) if n>1 else t
def fill_masks(C,TRI,BLK,back):
    n=CH*C
    r=lax.broadcasted_iota(jnp.int32,(n,n),0); c=lax.broadcasted_iota(jnp.int32,(n,n),1)
    rs,cs=r//(B*C),c//(B*C)
    same=((r//B)%C)==((c//B)%C)
    tri=same&((cs<rs)|((cs==rs)&((c%B)<=(r%B))))
    TRI[...]=jnp.where(tri,1.0,0.0)
    BLK[...]=jnp.where(same&(cs<rs),1.0,0.0)
    if back is not None: back[...]=jnp.where(same&(cs>rs),1.0,0.0)
def ones_of(C,H):
    r=lax.broadcasted_iota(jnp.int32,(C*H,C*H),0); c=lax.broadcasted_iota(jnp.int32,(C*H,C*H),1)
    return jnp.where((r//H)==(c//H),1.0/H,0.0).astype(LOW)
def sums_of(C):
    r=lax.broadcasted_iota(jnp.int32,(C,CH*C),0); c=lax.broadcasted_iota(jnp.int32,(C,CH*C),1)
    return jnp.where(((c//B)%C)==r,1.0,0.0).astype(LOW)
def stack_col(C,r):
    return jnp.concatenate([r[B*j:B*j+B,c:c+1] for j in range(r.shape[0]//B) for c in range(C)],0)
def pair_cols(C,H,r,masks):
    y=jnp.broadcast_to(r[:,0:1],(r.shape[0],C*H))
    for c in range(1,C): y=jnp.where(masks[c],r[:,c:c+1],y)
    return y

def rates(C,x_ref,own_ref,H):
    rows=[x_ref[0,CH+c:CH+c+1,:CH].astype(F)+own_ref[c,2*H+1:2*H+2,3*H:3*H+1] for c in range(C)]
    rows=jnp.concatenate(rows+[jnp.zeros((CH-C,CH),F)],0)
    return (jax.nn.sigmoid(rows)*(RATE_SCALE/H)).T

def pair_row(C,H,own_ref,k):
    return jnp.concatenate([own_ref[c,2*H+1:2*H+2,k*H:k*H+H] for c in range(C)],1)

def mask_stack(C,H):
    r=lax.broadcasted_iota(jnp.int32,(B*C,C*H),0)//B; c=lax.broadcasted_iota(jnp.int32,(B*C,C*H),1)//H
    return r==c

def fwd_pre(C,H,x,own_ref,BLK,gam,bet,S):
    W=C*H
    m16=lane_masks(C,H,B); m128=lane_masks(C,H,CH)
    K=x[0,:CH,W:2*W]
    Kst=expand(C,K,m16)
    S["KST"][...]=Kst; S["QST"][...]=expand(C,x[0,:CH,:W],m16)
    S["T"][...]=(bet+K.astype(F)-x[0,:CH,2*W:].astype(F))*gam
    yield
    R=rates(C,x,own_ref,H)
    S["R"][...]=R
    S["RP"][...]=pair_cols(C,H,R,m128)
    yield
    S["KK"][...]=((nt(Kst,Kst)+1.0)*BLK[...]).astype(LOW)
    tst=expand(C,S["T"][...],m16)
    S["TST"][...]=tst
    S["CT"][...]=nn(tst,jnp.full((W,W),1.0/H,LOW))
    yield

def fwd_steps(C,H,S,W1,B1,U,B2,gam,z1_ref,p_ref,zc_ref,us_ref,w1s_ref,o,side,times):
    W=C*H; SB=B*C; TALL=C*CH
    m16=lane_masks(C,H,B)
    ones=ones_of(C,H)
    g2=gam*gam
    Kst=S["KST"][...]
    w1b=W1[...].astype(LOW); w1s_ref[o]=w1b
    S["W1"][...]=w1b; S["B1"][...]=B1[...]; S["B2"][...]=B2[...]
    b1r=tile_rows(C,B1[...],1)
    uf=U[...]; ub=uf.astype(LOW); S["U"][...]=ub
    b2=B2[...]
    S["BASE"][...]=nn(Kst,w1b)
    g2m=jnp.concatenate([jnp.broadcast_to(jnp.sum(jnp.where(m16[c][:1],g2,0.0),1,keepdims=True)*(1.0/H),(B,W)) for c in range(C)],0)
    mst=mask_stack(C,H)
    full=jnp.full((W,W),1.0/H,LOW)
    I=W1.shape[1]
    wide=lambda v: jnp.concatenate([v]*(I//W),1)
    for j in range(NB):
        sl=slice(B*j,B*j+B); st=slice(SB*j,SB*j+SB)
        z1=S["BASE"][st]+b1r
        if j>0: z1=z1-nn(S["KK"][st,:SB*j],S["S1"][:SB*j])
        x2,g1=gelu2(z1)
        x2b=x2.astype(LOW)
        t=S["TST"][st]; ct=S["CT"][st]; rr=stack_col(C,S["R"][sl])
        tU=nn(t,ub)
        zc=jnp.where(mst,nt(x2b,ub)+b2,0.0)
        zz=zc*zc; zg=zc*g2
        AB=nn(jnp.concatenate([zg,zc],0),ub)
        mm=nn(jnp.concatenate([zc,zz,zg,zz*g2,zc*t],0),full)
        mu=mm[0:SB]; mzz=mm[SB:2*SB]; mzg=mm[2*SB:3*SB]; mzzg=mm[3*SB:4*SB]; mzt=mm[4*SB:]
        s=lax.rsqrt(mzz-mu*mu+EPS)
        m1=s*(mzg-mu*g2m)+ct
        m2=s*(s*(mzzg-2.0*mu*mzg+mu*mu*g2m)+mzt-mu*ct)
        ss=s*s
        P=wide(ss)*(AB[:SB]-wide(m2)*AB[SB:])+wide(s)*tU
        s1=(P*(g1*rr)).astype(LOW)
        d2=ss*(zg-m2*zc)+s*t+jnp.where(mst,ss*mu*(m2-g2)-s*m1,0.0)
        s2=d2*rr
        s2b=s2.astype(LOW)
        zc=collapse(C,zc-mu,m16)
        S["S1"][st]=s1; S["S2"][st]=s2b; S["X2"][st]=x2b
        z1_ref[TALL*o+SB*j:TALL*o+SB*j+SB]=z1; p_ref[TALL*o+SB*j:TALL*o+SB*j+SB]=P
        zc_ref[CH*o+B*j:CH*o+B*j+B]=zc
        us_ref[o,j]=ub
        uf=uf-tn(s2b,x2b); ub=uf.astype(LOW)
        b2=b2-jnp.sum(s2,0,keepdims=True)
        for _ in range(times): next(side,None)
    U[...]=uf; B2[...]=b2
    S1v=S["S1"][...]
    W1[...]=W1[...]-tn(Kst,S1v)
    B1[...]=B1[...]-nn(sums_of(C),S1v)

def fwd_query(C,H,S,x,TRI,gam,bet,o_ref,z1q_ref,zq_ref,o):
    W=C*H; TALL=C*CH
    m16=lane_masks(C,H,B)
    ones=ones_of(C,H)
    A1=((nt(S["QST"][...],S["KST"][...])+1.0)*TRI[...]).astype(LOW)
    yield
    z1q=nn(S["QST"][...],S["W1"][...])+tile_rows(C,S["B1"][...],NB)-nn(A1,S["S1"][...])
    z1q_ref[TALL*o:TALL*o+TALL]=z1q
    x2q=gelu1(z1q).astype(LOW)
    yield
    A2=((nt(x2q,S["X2"][...])+1.0)*TRI[...]).astype(LOW)
    yield
    zq=collapse(C,nt(x2q,S["U"][...])-nn(A2,S["S2"][...]),m16)+S["B2"][...]
    zq=zq-nn(zq,ones)
    zq_ref[CH*o:CH*o+CH]=zq
    yield
    yq=zq*lax.rsqrt(nn(zq*zq,ones)+EPS)
    o_ref[CH*o:CH*o+CH]=(x[0,:CH,:W].astype(F)+yq*gam+bet).astype(LOW)
    yield

FSLOT=("TST","KST","QST","T","R","RP","KK","CT","W1","B1","U","B2","BASE","S1","S2","X2")

def fwd_kernel(C,H,xa_ref,xb_ref,own_ref,o_ref,z1_ref,p_ref,zc_ref,z1q_ref,zq_ref,us_ref,w1s_ref,W1,B1,U,B2,TRI,BLK,*slots):
    k=len(FSLOT)
    even=dict(zip(FSLOT,slots[:k])); odd=dict(zip(FSLOT,slots[k:]))
    gam=pair_row(C,H,own_ref,1); bet=pair_row(C,H,own_ref,2)
    @pl.when(pl.program_id(0)==0)
    def _():
        for c in range(C):
            W1[H*c:H*c+H]=own_ref[c,:H]
            u=own_ref[c,H:2*H]
            U[H*c:H*c+H]=u-jnp.sum(u,0,keepdims=True)*(1.0/H)
            B1[c:c+1]=own_ref[c,2*H:2*H+1]
        raw=[own_ref[c,2*H+1:2*H+2,:H] for c in range(C)]
        B2[...]=jnp.concatenate([v-jnp.sum(v,1,keepdims=True)*(1.0/H) for v in raw],1)
        fill_masks(C,TRI,BLK,None)
    for _ in fwd_pre(C,H,xa_ref,own_ref,BLK,gam,bet,even): pass
    side=fwd_pre(C,H,xb_ref,own_ref,BLK,gam,bet,odd)
    fwd_steps(C,H,even,W1,B1,U,B2,gam,z1_ref,p_ref,zc_ref,us_ref,w1s_ref,0,side,1)
    for _ in side: pass
    side=fwd_query(C,H,even,xa_ref,TRI,gam,bet,o_ref,z1q_ref,zq_ref,0)
    fwd_steps(C,H,odd,W1,B1,U,B2,gam,z1_ref,p_ref,zc_ref,us_ref,w1s_ref,1,side,1)
    for _ in side: pass
    for _ in fwd_query(C,H,odd,xb_ref,TRI,gam,bet,o_ref,z1q_ref,zq_ref,1): pass

def fwd_scan(x,own):
    n,tall,W=x.shape
    W//=3
    C=own.shape[0]; I=own.shape[2]; H=W//C; L=n*CH; m=C*CH
    rows=lambda k,w: pl.BlockSpec((2*k,w),lambda i:(i,0))
    sd=jax.ShapeDtypeStruct
    V=pltpu.VMEM
    kinds=dict(KST=V((m,W),LOW),QST=V((m,W),LOW),T=V((CH,W),F),R=V((CH,CH),F),RP=V((CH,W),F),KK=V((m,m),LOW),CT=V((m,W),F),TST=V((m,W),F),W1=V((W,I),LOW),
        B1=V((C,I),F),U=V((W,I),LOW),B2=V((1,W),F),BASE=V((m,I),F),S1=V((m,I),LOW),S2=V((m,W),LOW),X2=V((m,I),LOW))
    return pl.pallas_call(partial(fwd_kernel,C,H),grid=(n//2,),
        in_specs=[pl.BlockSpec((1,tall,3*W),lambda i:(2*i,0,0)),pl.BlockSpec((1,tall,3*W),lambda i:(2*i+1,0,0)),pl.BlockSpec(own.shape,lambda i:(0,0,0))],
        out_specs=[rows(CH,W),rows(m,I),rows(m,I),rows(CH,W),rows(m,I),rows(CH,W),
            pl.BlockSpec((2,NB,W,I),lambda i:(i,0,0,0)),pl.BlockSpec((2,W,I),lambda i:(i,0,0))],
        out_shape=[sd((L,W),LOW),sd((C*L,I),F),sd((C*L,I),F),sd((L,W),F),sd((C*L,I),F),sd((L,W),F),sd((n,NB,W,I),LOW),sd((n,W,I),LOW)],
        scratch_shapes=[V((W,I),F),V((C,I),F),V((W,I),F),V((1,W),F),V((m,m),F),V((m,m),F)]+[kinds[name] for name in FSLOT]*2,
        compiler_params=pltpu.CompilerParams(vmem_limit_bytes=48*1024*1024),
    )(x,x,own)

SLOT=("BASE","DX2","X2","RG1","G1","RPG2","DS2Q","KK","YB","GB","DB","SB","M2B","RED","S2E","S1B","X2Q","DZQ","DZ1Q","DKQ","DQ","KST","QST","T0","RP","PG1","R")

def slot_shapes(C,W,I):
    m=C*CH
    V=pltpu.VMEM
    wide,pair,tall=V((m,I),F),V((CH,W),F),V((m,W),LOW)
    kinds=dict(BASE=wide,DX2=wide,X2=V((m,I),LOW),RG1=wide,G1=wide,RPG2=wide,DS2Q=pair,KK=V((m,m),LOW),YB=pair,GB=pair,DB=pair,SB=pair,M2B=pair,
        RED=V((4*CH,W),F),S2E=tall,S1B=V((m,I),LOW),X2Q=V((m,I),LOW),DZQ=tall,DZ1Q=V((m,I),LOW),DKQ=V((m,W),F),DQ=V((CH,W),LOW),KST=tall,QST=tall,
        T0=pair,RP=pair,PG1=wide,R=V((CH,CH),F))
    return [kinds[name] for name in SLOT]

def bwd_pre(C,H,ins,own_ref,S,TRI,BLKT,gam,bet,dgam_ref,dbet_ref,factor):
    x_ref,do_ref,z1_ref,p_ref,zc_ref,z1q_ref,zq_ref,us_ref,w1s_ref=ins
    W=C*H
    m16=lane_masks(C,H,B); m128=lane_masks(C,H,CH)
    ones=ones_of(C,H)
    g2=gam*gam
    K=x_ref[0,:CH,W:2*W]
    Kst=expand(C,K,m16); Qst=expand(C,x_ref[0,:CH,:W],m16)
    S["KST"][...]=Kst; S["QST"][...]=Qst
    R=rates(C,x_ref,own_ref,H)
    S["R"][...]=R
    RP=pair_cols(C,H,R,m128)
    S["RP"][...]=RP
    dO=do_ref[...].astype(F)
    zq=zq_ref[...]; sq=lax.rsqrt(nn(zq*zq,ones)+EPS); yq=zq*sq
    dyq=dO*gam
    rq=nn(jnp.concatenate([dyq,dyq*yq],0),ones)
    dzq=sq*(dyq-rq[:CH]-yq*rq[CH:])
    dzqb=expand(C,dzq.astype(LOW),m16)
    S["DZQ"][...]=dzqb
    dgam_ref[...]=dgam_ref[...]+factor*jnp.sum(dO*yq,0,keepdims=True)
    dbet_ref[...]=dbet_ref[...]+factor*jnp.sum(dO,0,keepdims=True)
    yield
    zc=zc_ref[...]
    s=lax.rsqrt(nn(zc*zc,ones)+EPS)
    y=zc*s
    t0=bet+K.astype(F)-x_ref[0,:CH,2*W:].astype(F)
    G=y*g2+t0*gam
    red=nn(jnp.concatenate([G,G*y,g2*y,g2*y*y],0),ones)
    m1=red[:CH]; m2=red[CH:2*CH]
    d2=s*(G-m1-y*m2)
    s2=expand(C,(d2*RP).astype(LOW),m16)
    S["YB"][...]=y; S["GB"][...]=G; S["DB"][...]=d2; S["SB"][...]=s; S["M2B"][...]=m2; S["RED"][...]=red; S["S2E"][...]=s2; S["T0"][...]=t0
    yield
    x2,g1,gg2=gelu3(z1_ref[...]); x2=x2.astype(LOW)
    P=p_ref[...]
    RS=stack_col(C,R)
    rg1=RS*g1
    s1=(P*rg1).astype(LOW)
    S["X2"][...]=x2; S["G1"][...]=g1; S["RG1"][...]=rg1; S["RPG2"][...]=RS*(P*gg2); S["PG1"][...]=P*g1; S["S1B"][...]=s1
    yield
    x2q,g1q=gelu2(z1q_ref[...]); x2q=x2q.astype(LOW)
    S["X2Q"][...]=x2q
    A2=((nt(x2q,S["X2"][...])+1.0)*TRI[...]).astype(LOW)
    dA2=(nt(dzqb,s2)*TRI[...]).astype(LOW)
    yield
    dx2q=nn(dzqb,us_ref[0,0])-nn(dA2,S["X2"][...])
    S["DX2"][...]=-tn(dA2,x2q)
    S["DS2Q"][...]=-collapse(C,tn(A2,dzqb),m16)
    dz1qb=(dx2q*g1q).astype(LOW)
    S["DZ1Q"][...]=dz1qb
    yield
    A1=((nt(Qst,Kst)+1.0)*TRI[...]).astype(LOW)
    dA1=(nt(dz1qb,S["S1B"][...])*TRI[...]).astype(LOW)
    S["KK"][...]=((nt(Kst,Kst)+1.0)*BLKT[...]).astype(LOW)
    yield
    S["DQ"][...]=(dO+collapse(C,nt(dz1qb,w1s_ref[0])-nn(dA1,Kst),m16)).astype(LOW)
    S["DKQ"][...]=tn(dA1,Qst)
    S["BASE"][...]=-tn(A1,dz1qb)
    yield

def bwd_steps(C,H,S,us_ref,u,w1,H1,h1,HU,h2,BLK,gam,bet,dgam_ref,dbet_ref,DZ1,DS1,DS2,DG,dx_ref,db_ref,o,side):
    W=C*H; SB=B*C
    m16=lane_masks(C,H,B); m128=lane_masks(C,H,CH)
    ones=ones_of(C,H); sums=sums_of(C)
    g2=gam*gam
    Kst=S["KST"][...]
    h1b=H1[...].astype(LOW)
    S["BASE"][...]=S["BASE"][...]-nn(Kst,h1b)-tile_rows(C,h1[...],NB)
    dk=nt(S["S1B"][...],h1b)+S["DKQ"][...]
    g2m=nn(jnp.broadcast_to(g2,(8,W)),ones)[0:1]
    hu=HU[...]; hh2=h2[...]
    for j in reversed(range(NB)):
        sl=slice(B*j,B*j+B); st=slice(SB*j,SB*j+SB)
        ub=us_ref[u,j]
        rr=S["RP"][sl]
        hub=hu.astype(LOW)
        x2j=S["X2"][st]
        ds1=S["BASE"][st]
        if j<NB-1: ds1=ds1-nn(S["KK"][st,SB*j+SB:],DZ1[SB*j+SB:])
        ds2=S["DS2Q"][sl]-collapse(C,nt(x2j,hub),m16)-hh2
        dx2=S["DX2"][st]-nn(S["S2E"][st],hub)
        dPb=(ds1*S["RG1"][st]).astype(LOW)
        e=rr*ds2+collapse(C,nt(dPb,ub),m16)
        s=S["SB"][sl]; m2=S["M2B"][sl]; y=S["YB"][sl]; g_=S["GB"][sl]; d2=S["DB"][sl]
        m1=S["RED"][sl]; gy=S["RED"][2*CH+B*j:2*CH+B*j+B]; gyy=S["RED"][3*CH+B*j:3*CH+B*j+B]
        ge=g2*e
        mm=nn(jnp.concatenate([e,e*y,e*d2,ge,ge*y],0),ones)
        a=mm[0:B]; b=mm[B:2*B]; cc=mm[2*B:3*B]; mge=mm[3*B:4*B]; mgey=mm[4*B:]
        dG=s*(e-a-y*b)
        mdY=s*(mge-a*g2m-b*gy-m2*a-b*m1)
        mdYY=s*(mgey-a*gy-b*gyy-2.0*b*m2)
        dZc=s*(g2*dG-s*(m2*e+g_*b)-mdY-y*(cc+mdYY))
        dZcb=expand(C,dZc.astype(LOW),m16)
        dx2=dx2+nn(dZcb,ub)
        dz1=(dx2*S["G1"][st]+ds1*S["RPG2"][st]).astype(LOW)
        DZ1[st]=dz1
        DS1[st]=ds1; DS2[sl]=ds2; DG[sl]=dG
        hu=hu+tn(jnp.concatenate([expand(C,d2.astype(LOW),m16),dZcb],0),jnp.concatenate([dPb,x2j],0))
        hh2=hh2+jnp.sum(dZc,0,keepdims=True)
        next(side,None)
    dz1=DZ1[...]
    M=(nt(dz1,S["S1B"][...])*BLK[...]).astype(LOW)
    dG=DG[...]; dGg=dG*gam
    dk=collapse(C,nt(dz1,w1)-dk-nn(M,Kst)-tn(M,Kst),m16)+dGg
    dx_ref[o,:CH,:W]=S["DQ"][...]
    dx_ref[o,:CH,W:2*W]=dk.astype(LOW)
    dx_ref[o,:CH,2*W:]=(-dGg).astype(LOW)
    dr1=jnp.sum(DS1[...]*S["PG1"][...],-1,keepdims=True)
    dr2=DS2[...]*S["DB"][...]
    lane=lax.broadcasted_iota(jnp.int32,(CH,CH),1)
    dr=jnp.zeros((CH,CH),F)
    for c in range(C):
        rows=[dr1[B*(C*j+c):B*(C*j+c)+B] for j in range(NB)]
        col=jnp.concatenate(rows,0)+jnp.sum(jnp.where(m128[c],dr2,0.0),-1,keepdims=True)
        dr=jnp.where(lane==c,col,dr)
    R=S["R"][...]
    dr=dr*R*(1.0-R*(H/RATE_SCALE))
    db_ref[...]=db_ref[...]+jnp.sum(dr,0,keepdims=True)
    dr=dr.T.astype(LOW)
    extra=dx_ref.shape[1]-CH
    dx_ref[o,CH:,:]=jnp.zeros((extra,3*W),LOW)
    dx_ref[o,CH:,:CH]=dr[:extra]
    dgam_ref[...]=dgam_ref[...]+jnp.sum(dG*(2*S["YB"][...]*gam+S["T0"][...]),0,keepdims=True)
    dbet_ref[...]=dbet_ref[...]+jnp.sum(dGg,0,keepdims=True)
    dz1qb=S["DZ1Q"][...]
    H1[...]=H1[...]+tn(Kst,dz1)+tn(S["QST"][...],dz1qb)
    h1[...]=h1[...]+nn(sums,dz1)+nn(sums,dz1qb)
    HU[...]=hu+tn(S["DZQ"][...],S["X2Q"][...])
    h2[...]=hh2+jnp.sum(collapse(C,S["DZQ"][...].astype(F),m16),0,keepdims=True)

def bwd_kernel(C,H,steps,*refs):
    first,near,far=refs[:9],refs[9:18],refs[18:27]
    us_ref,w1_ref,own_ref,dx_ref,H1,h1,HU,h2,dgam_ref,dbet_ref,db_ref,TRI,BLK,BLKT,DZ1,DS1,DS2,DG=refs[27:45]
    k=len(SLOT)
    even=dict(zip(SLOT,refs[45:45+k])); odd=dict(zip(SLOT,refs[45+k:]))
    gam=pair_row(C,H,own_ref,1); bet=pair_row(C,H,own_ref,2)
    @pl.when(pl.program_id(0)==0)
    def _():
        for ref in (H1,h1,HU,h2,dgam_ref,dbet_ref,db_ref): ref[...]=jnp.zeros_like(ref)
        fill_masks(C,TRI,BLK,BLKT)
        for _ in bwd_pre(C,H,first,own_ref,even,TRI,BLKT,gam,bet,dgam_ref,dbet_ref,1.0): pass
    more=jnp.where(pl.program_id(0)<steps-1,1.0,0.0)
    side=bwd_pre(C,H,near,own_ref,odd,TRI,BLKT,gam,bet,dgam_ref,dbet_ref,1.0)
    bwd_steps(C,H,even,us_ref,1,w1_ref[1],H1,h1,HU,h2,BLK,gam,bet,dgam_ref,dbet_ref,DZ1,DS1,DS2,DG,dx_ref,db_ref,1,side)
    side=bwd_pre(C,H,far,own_ref,even,TRI,BLKT,gam,bet,dgam_ref,dbet_ref,more)
    bwd_steps(C,H,odd,us_ref,0,w1_ref[0],H1,h1,HU,h2,BLK,gam,bet,dgam_ref,dbet_ref,DZ1,DS1,DS2,DG,dx_ref,db_ref,0,side)

def bwd_scan(x,own,do,z1,p,zc,z1q,zq,us,w1s):
    n,tall,W=x.shape
    W//=3
    C=own.shape[0]; I=own.shape[2]; H=W//C
    full=lambda *s: pl.BlockSpec(s,lambda i:(0,)*len(s))
    sd=jax.ShapeDtypeStruct
    V=pltpu.VMEM
    m=C*CH
    def chunk(at):
        rows=lambda k,w: pl.BlockSpec((k,w),lambda i:(at(i),0))
        return [pl.BlockSpec((1,tall,3*W),lambda i:(at(i),0,0)),rows(CH,W),rows(m,I),rows(m,I),rows(CH,W),rows(m,I),rows(CH,W),
            pl.BlockSpec((1,1,W,I),lambda i:(at(i),0,0,0)),pl.BlockSpec((1,W,I),lambda i:(at(i),0,0))]
    ins=(x,do,z1,p,zc,z1q,zq,us,w1s)
    return pl.pallas_call(partial(bwd_kernel,C,H,n//2),grid=(n//2,),
        in_specs=chunk(lambda i:n-1)+chunk(lambda i:n-2-2*i)+chunk(lambda i:jnp.maximum(n-3-2*i,0))+[
            pl.BlockSpec((2,NB,W,I),lambda i:(n//2-1-i,0,0,0)),pl.BlockSpec((2,W,I),lambda i:(n//2-1-i,0,0)),full(*own.shape)],
        out_specs=[pl.BlockSpec((2,tall,3*W),lambda i:(n//2-1-i,0,0)),full(W,I),full(C,I),full(W,I),full(1,W),full(1,W),full(1,W),full(1,CH)],
        out_shape=[sd((n,tall,3*W),LOW),sd((W,I),F),sd((C,I),F),sd((W,I),F),sd((1,W),F),sd((1,W),F),sd((1,W),F),sd((1,CH),F)],
        scratch_shapes=[V((m,m),F),V((m,m),F),V((m,m),F),V((m,I),LOW),V((m,I),F),V((CH,W),F),V((CH,W),F)]+slot_shapes(C,W,I)*2,
        compiler_params=pltpu.CompilerParams(vmem_limit_bytes=48*1024*1024),
        cost_estimate=pl.CostEstimate(flops=1000,bytes_accessed=1000,transcendentals=0),
    )(*ins,*ins,*ins,us,w1s,own)

RATE_SCALE = 0.25
NORM_EPS = 1e-05


def smooth_act(value):
    return 0.5 * value * (1.0 + jnp.tanh(C0 * (value + C1 * value * value * value)))


def root_norm(value, gain):
    return value * lax.rsqrt(jnp.mean(value * value, -1, keepdims=True) + NORM_EPS) * gain


def layer_norm(value, gain, bias):
    centre = value - jnp.mean(value, -1, keepdims=True)
    return centre * lax.rsqrt(jnp.mean(centre * centre, -1, keepdims=True) + NORM_EPS) * gain + bias


def gated_branch(mixed, gate_pre, gain, bias):
    return layer_norm(mixed, gain, bias) * smooth_act(gate_pre)


def swish_product(gate_val, linear_val):
    return jax.nn.silu(gate_val) * linear_val


def matmul(left, right):
    return jnp.dot(left, right, preferred_element_type=F)


def flip(array, axis, mask):
    peers = lax.axis_size(axis)
    return lax.ppermute(array, axis, [(i, i ^ mask) for i in range(peers)])


def masks_of(axis):
    masks = []
    while 1 << len(masks) < lax.axis_size(axis):
        masks.append(1 << len(masks))
    return masks


def side(axis, mask):
    return (lax.axis_index(axis) // mask) % 2


def gather_near(array, axis):
    for mask in reversed(masks_of(axis)):
        array = jnp.concatenate([array, flip(array, axis, mask)], 0)
    return array


def scatter_once(array, axis, mask):
    half = array.shape[0] // 2
    return array[:half].astype(F) + flip(array[half:].astype(LOW), axis, mask).astype(F)


def scatter_near(array, axis):
    for mask in masks_of(axis):
        array = scatter_once(array, axis, mask)
    return array


def halve(array, axis, mask, dim):
    bit = side(axis, mask)
    mine = lax.dynamic_index_in_dim(array, bit, dim, keepdims=False)
    other = lax.dynamic_index_in_dim(array, 1 - bit, dim, keepdims=False)
    return mine.astype(F) + flip(other.astype(LOW), axis, mask).astype(F)


def double(array, axis, mask):
    got = flip(array, axis, mask)
    upper = side(axis, mask) == 1
    return jnp.stack([jnp.where(upper, got, array), jnp.where(upper, array, got)])


def params_kernel(f_ref, s_ref, fb_ref, sb_ref, g_ref, b_ref, r_ref, o_ref):
    heads, head, inner = f_ref.shape
    for i in range(heads):
        o_ref[i, :head] = f_ref[i]
        o_ref[i, head : 2 * head] = s_ref[i]
        o_ref[i, 2 * head :] = jnp.zeros((8, inner), F)
        o_ref[i, 2 * head : 2 * head + 1] = fb_ref[i : i + 1]
        small = [ref[i : i + 1] for ref in (sb_ref, g_ref, b_ref)]
        small.append(jnp.broadcast_to(r_ref[:, i : i + 1], (1, inner - 3 * head)))
        o_ref[i, 2 * head + 1 : 2 * head + 2] = jnp.concatenate(small, 1)


def pack_params(first_weight, *others):
    heads, head, inner = first_weight.shape
    return pl.pallas_call(
        params_kernel,
        in_specs=[pl.BlockSpec(memory_space=pltpu.VMEM)] * 7,
        out_specs=pl.BlockSpec(memory_space=pltpu.VMEM),
        out_shape=jax.ShapeDtypeStruct((heads, 2 * head + 8, inner), F),
    )(first_weight, *others)


def project_kernel(each, blocks, x_ref, g_ref, wq_ref, wk_ref, wv_ref, wr_ref, wg_ref, s_ref, n_ref, p_ref, LT):
    step = pl.program_id(0)
    rows, width = x_ref.shape
    span = wq_ref.shape[1]

    @pl.when(step == 0)
    def _():
        x = x_ref[...].astype(F)
        scale = lax.rsqrt(jnp.sum(x * x, -1, keepdims=True) * (1.0 / width) + NORM_EPS)
        n_ref[...] = (x * scale * g_ref[...]).astype(LOW)
        LT[...] = jnp.zeros_like(LT)
        LT[: wr_ref.shape[0]] = nt(wr_ref[...], n_ref[...]).astype(LOW).astype(F)

    normed = n_ref[...]
    extra = s_ref.shape[1] - rows
    s_ref[0, rows:, :] = jnp.zeros((extra, 3 * span), LOW)

    @pl.when(step < blocks)
    def _():
        for i, w_ref in enumerate((wq_ref, wk_ref, wv_ref)):
            s_ref[0, :rows, span * i : span * i + span] = nn(normed, w_ref[...]).astype(LOW)
        r = lax.broadcasted_iota(jnp.int32, (extra, rows), 0)
        c = lax.broadcasted_iota(jnp.int32, (extra, rows), 1)
        pick = jnp.where((r < each) & (c == step * each + r), 1.0, 0.0)
        s_ref[0, rows:, :rows] = nn(pick, LT[...]).astype(LOW)
        p_ref[...] = nn(normed, wg_ref[...])

    @pl.when(step >= blocks)
    def _():
        s_ref[0, :rows, :] = jnp.zeros((rows, 3 * span), LOW)


def project(x, gain, wq, wk, wv, wr, wg, seqs, each, extra):
    rows, width = x.shape
    span = each * (width // wr.shape[0])
    blocks = width // span
    column = pl.BlockSpec((width, span), lambda s: (0, jnp.minimum(s, blocks - 1)))
    full = lambda *shape: pl.BlockSpec(shape, lambda s: (0,) * len(shape))
    sd = jax.ShapeDtypeStruct
    return pl.pallas_call(
        partial(project_kernel, each, blocks),
        grid=(seqs,),
        in_specs=[full(rows, width), full(1, width), column, column, column, full(*wr.shape), column],
        out_specs=[
            pl.BlockSpec((1, rows + extra, 3 * span), lambda s: (s, 0, 0)),
            full(rows, width),
            pl.BlockSpec((rows, span), lambda s: (0, jnp.minimum(s, blocks - 1))),
        ],
        out_shape=[sd((seqs, rows + extra, 3 * span), LOW), sd((rows, width), LOW), sd((rows, width), F)],
        scratch_shapes=[pltpu.VMEM((128, 128), F)],
        compiler_params=pltpu.CompilerParams(vmem_limit_bytes=60 * 1024 * 1024),
    )(x, gain[None], wq, wk, wv, wr, wg)


def tokens_kernel(each, blocks, x_ref, g_ref, m_ref, b_ref, d_ref, wq_ref, wk_ref, wv_ref, wr_ref, wg_ref, o_ref, ACC, LG):
    step = pl.program_id(0)
    rows, width = x_ref.shape
    span = wq_ref.shape[1]
    extra = b_ref.shape[1] - rows

    @pl.when(step == 0)
    def _():
        ACC[...] = jnp.zeros_like(ACC)
        LG[...] = jnp.zeros_like(LG)

    @pl.when(step < blocks)
    def _():
        total = nt(d_ref[...], wg_ref[...])
        for i, w_ref in enumerate((wq_ref, wk_ref, wv_ref)):
            total = total + nt(b_ref[0, :rows, span * i : span * i + span], w_ref[...])
        ACC[...] = ACC[...] + total
        r = lax.broadcasted_iota(jnp.int32, (rows, extra), 0)
        c = lax.broadcasted_iota(jnp.int32, (rows, extra), 1)
        place = jnp.where((c < each) & (r == step * each + c), 1.0, 0.0)
        LG[...] = LG[...] + nn(place, b_ref[0, rows:, :rows])

    @pl.when(step == pl.num_programs(0) - 1)
    def _():
        heads = wr_ref.shape[0]
        x = x_ref[...].astype(F)
        scale = lax.rsqrt(jnp.sum(x * x, -1, keepdims=True) * (1.0 / width) + NORM_EPS)
        grad = (ACC[...] + nn(LG[...].T[:, :heads], wr_ref[...])) * g_ref[...]
        along = jnp.sum(x * grad, -1, keepdims=True) * (1.0 / width)
        o_ref[...] = m_ref[...] + scale * (grad - x * (scale * scale * along))


def tokens_back(x, gain, middle_grad, back, gate_low, wq, wk, wv, wr, wg, each):
    rows, width = x.shape
    seqs, tall, lanes = back.shape
    span = lanes // 3
    blocks = width // span
    column = pl.BlockSpec((width, span), lambda s: (0, jnp.minimum(s, blocks - 1)))
    full = lambda *shape: pl.BlockSpec(shape, lambda s: (0,) * len(shape))
    return pl.pallas_call(
        partial(tokens_kernel, each, blocks),
        grid=(blocks,),
        in_specs=[
            full(rows, width), full(1, width), full(rows, width),
            pl.BlockSpec((1, tall, lanes), lambda s: (s, 0, 0)),
            pl.BlockSpec((rows, span), lambda s: (0, s)),
            column, column, column, full(*wr.shape), column,
        ],
        out_specs=full(rows, width),
        out_shape=jax.ShapeDtypeStruct((rows, width), F),
        scratch_shapes=[pltpu.VMEM((rows, width), F), pltpu.VMEM((128, 128), F)],
        compiler_params=pltpu.CompilerParams(vmem_limit_bytes=16 * 1024 * 1024),
    )(x, gain[None], middle_grad, back, gate_low, wq, wk, wv, wr, wg)


def feed_kernel(a_ref, b_ref, c_ref, g_ref, l_ref, d_ref):
    unit = g_ref.shape[1]
    g_ref[...] = a_ref[0, :unit].astype(F).T
    l_ref[...] = b_ref[0, :unit].astype(F).T
    half = unit // 2
    for i in range(2):
        d_ref[half * i : half * i + half] = c_ref[i, unit : unit + half].astype(F)


def feed_outputs(fed, inner_units):
    seqs, tall, width = fed.shape
    steps = seqs // 2
    unit = inner_units // steps
    sd = jax.ShapeDtypeStruct
    return pl.pallas_call(
        feed_kernel,
        grid=(steps,),
        in_specs=[
            pl.BlockSpec((1, tall, width), lambda i: (i, 0, 0)),
            pl.BlockSpec((1, tall, width), lambda i: (i + steps, 0, 0)),
            pl.BlockSpec((2, tall, width), lambda i: (i, 0, 0)),
        ],
        out_specs=[
            pl.BlockSpec((width, unit), lambda i: (0, i)),
            pl.BlockSpec((width, unit), lambda i: (0, i)),
            pl.BlockSpec((unit, width), lambda i: (i, 0)),
        ],
        out_shape=[sd((width, inner_units), F)] * 2 + [sd((inner_units, width), F)],
        compiler_params=pltpu.CompilerParams(vmem_limit_bytes=16 * 1024 * 1024),
    )(fed, fed, fed)


def swapped(array):
    seqs = lax.axis_size("seq")
    array = array.reshape(seqs, -1, array.shape[-1])
    return lax.all_to_all(array, "seq", split_axis=0, concat_axis=0, tiled=True)


def summed(parts):
    return jnp.sum(parts.astype(F), 0).astype(LOW)


def share_rows(every_normed, back_sent, state_g, vectors, fed_parts, early, aside, heads, local_heads, head, weights_in):
    seqs, tps = lax.axis_size("seq"), lax.axis_size("tp")
    width = every_normed.shape[1]
    lanes = back_sent.shape[2]
    rows = every_normed.shape[0] // seqs
    span = lanes // 3
    each = span // head
    first_g, first_bias_g, second_g, second_bias_g, gain_g, shift_g, bias_g = state_g
    inner = first_g.shape[1]
    fed = lax.all_gather(summed(fed_parts), "seq", axis=0, tiled=False)
    early = lax.all_gather(summed(swapped(early)), "seq", axis=0, tiled=True)
    for mask in reversed(masks_of("tp")):
        early = double(early, "tp", mask)
    early = early.reshape(2, width, width).astype(F)
    back = lax.all_to_all(back_sent, "seq", split_axis=0, concat_axis=0, tiled=True)
    qkv_g = back_sent[:, :rows].reshape(seqs * rows, lanes)
    logit_g = back_sent[:, rows : rows + each, :rows].transpose(1, 0, 2).reshape(each, seqs * rows)
    columns = jnp.einsum("ld,le->de", every_normed, qkv_g, preferred_element_type=F)
    rate_column = jnp.einsum("el,ld->ed", logit_g, every_normed, preferred_element_type=F)
    first_g = first_g.reshape(each, head, inner)
    second_g = second_g.reshape(each, head, inner)
    second_g = second_g - jnp.mean(second_g, 1, keepdims=True)
    second_bias_g, gain_g, shift_g = [a.reshape(each, head) for a in (second_bias_g, gain_g, shift_g)]
    second_bias_g = second_bias_g - jnp.mean(second_bias_g, 1, keepdims=True)
    bias_g = bias_g[0, :each]
    tail = jnp.concatenate(
        [second_bias_g, gain_g, shift_g, jnp.pad(bias_g[:, None], ((0, 0), (0, inner - 3 * head - 1)))], -1
    )
    states = jnp.concatenate(
        [
            jnp.stack([first_g, second_g], 1),
            jnp.stack([first_bias_g, tail], 1)[:, :, None],
            jnp.zeros((each, 2, 7, inner), F),
        ],
        2,
    )
    state_rows = states.size // lanes // tps
    rate_rows = rate_column.size // lanes // tps
    vectors = jnp.concatenate([vectors, jnp.zeros_like(vectors[:1])], 0)
    vector_rows = vectors.size // lanes // tps
    rest = jnp.concatenate(
        [rate_column.reshape(tps, rate_rows, lanes), vectors.reshape(tps, vector_rows, lanes)], 1
    )
    late = jnp.concatenate(
        [
            columns.reshape(tps, width // tps, lanes),
            states.reshape(tps, state_rows, lanes),
            jnp.pad(rest, ((0, 0), (0, 16 - rate_rows - vector_rows), (0, 0))),
        ],
        1,
    )
    late = lax.psum_scatter(late.astype(LOW), "tp", scatter_dimension=0, tiled=True)
    late = lax.all_gather(late, ("seq", "tp"), axis=0, tiled=True).reshape((seqs, tps) + late.shape[1:])
    weights = late[:, :, : width // tps].reshape(seqs, tps, width // tps, 3, span)
    weights = weights.transpose(3, 1, 2, 0, 4).reshape(3, width, seqs * span)[:, :, :width].astype(F)
    states = late[:, :, width // tps : width // tps + state_rows].reshape(seqs * each, 2, head + 8, inner)[:heads]
    states = lax.dynamic_slice_in_dim(states, lax.axis_index("tp") * local_heads, local_heads, 0).astype(F)
    rest = late[:, :, width // tps + state_rows :]
    rate_weight_grad = rest[:, :, :rate_rows].reshape(seqs * each, width)[:heads].T.astype(F)
    vectors = rest[:, :, rate_rows : rate_rows + vector_rows].reshape(seqs, 4, width)
    vectors = jnp.sum(vectors.astype(F), 0)
    grads = (weights[0], weights[1], weights[2], early[1])
    norm_gain_grad = jnp.sum(sum(g * w.astype(F) for g, w in zip(grads, weights_in)), -1)
    head_w = (states[:, 0, :head], jnp.swapaxes(states[:, 1, :head], 1, 2))
    return weights, head_w, states[:, :, head], rate_weight_grad, vectors, fed, back, early, aside, norm_gain_grad


def pack_kernel(head, me_ref, n_ref, x_ref, w_ref, wb_ref, u_ref, ub_ref, g_ref, s_ref, r_ref, v_ref, keep_ref, sent_ref, COL, UC, SMALL):
    seqs, _, lanes = x_ref.shape
    rows = n_ref.shape[0] // seqs
    width = n_ref.shape[1]
    here = width // 4
    normed = n_ref[...]
    COL[...] = tn(normed, x_ref[:, :rows].reshape(seqs * rows, lanes))
    rate = jnp.zeros((16, width), F)
    for s in range(seqs):
        logit = x_ref[s, rows : rows + 16, :rows]
        rate = rate + nn(logit, n_ref[rows * s : rows * s + rows])
    SMALL[...] = jnp.zeros_like(SMALL)
    for c in range(2):
        lane = slice(head * c, head * c + head)
        u = u_ref[lane]
        UC[lane] = u - jnp.sum(u, 0, keepdims=True) * (1.0 / head)
        ub = ub_ref[:, lane]
        ub = ub - jnp.sum(ub, 1, keepdims=True) * (1.0 / head)
        for i in range(2):
            SMALL[2 * c, i : i + 1] = wb_ref[c : c + 1, 128 * i : 128 * i + 128]
        SMALL[2 * c + 1, 0:1] = jnp.concatenate([ub, g_ref[:, lane]], 1)
        SMALL[2 * c + 1, 1:2] = jnp.concatenate([s_ref[:, lane], jnp.broadcast_to(r_ref[:, c : c + 1], (1, head))], 1)
    for t in range(4):
        for i in range(3):
            at = (t % 2) * 384 + 128 * i
            SMALL[t, 2 + i : 3 + i] = rate[t // 2 : t // 2 + 1, at : at + 128]
        for i in range(5):
            k = 5 * t + i
            if k < 18:
                SMALL[t, 5 + i : 6 + i] = v_ref[k // 6 : k // 6 + 1, (k % 6) * 128 : (k % 6) * 128 + 128]
    for place, o in enumerate((0, 2, 1, 3)):
        out = (keep_ref, sent_ref)[place // 2].at[place % 2]
        t = me_ref[0] ^ o
        out[:here] = COL[pl.ds(pl.multiple_of(t * here, 16), here)].astype(LOW)
        for n in range(9):
            c, k, half = n // 4, (n // 2) % 2, n % 2
            if n < 8:
                tile = (w_ref, UC)[k][pl.ds(pl.multiple_of(head * c + 16 * t, 16), 16), 128 * half : 128 * half + 128]
            else:
                tile = SMALL[t]
            row, lane = here + 16 * (n // 3), 128 * (n % 3)
            out[row : row + 16, lane : lane + 128] = tile.astype(LOW)


def last_kernel(seqs, each, heads, local_heads, me_ref, *refs):
    ours = lax.rem(pl.program_id(0), 2) == lax.rem(me_ref[0], 2)

    @pl.when(ours)
    def _():
        last_part(seqs, each, heads, local_heads, me_ref, refs[0], refs[1], *refs[4:])

    @pl.when(jnp.logical_not(ours))
    def _():
        last_part(seqs, each, heads, local_heads, me_ref, refs[2], refs[3], *refs[4:])


def last_part(seqs, each, heads, local_heads, me_ref, a_ref, b_ref, wq_ref, wk_ref, wv_ref, wg_ref,
              q_ref, k_ref, v_ref, n_ref, f_ref, s_ref, r_ref, out_ref, gate_ref, gate_n_ref, ST):
    t = pl.program_id(0)
    cut = a_ref.shape[2]
    lanes = a_ref.shape[3]
    span = lanes // 3
    below = q_ref.shape[0] - cut

    def spot(s):
        return s % 2, ((s >> 1) & 1) * 2 + (s >> 2)

    for s in range(seqs):
        if s * each >= heads:
            continue
        x, q = spot(s)
        for i, o_ref in enumerate((q_ref, k_ref, v_ref)):
            o_ref[:cut, span * s : span * s + span] = a_ref[0, 4 * x + q, :, span * i : span * i + span].astype(F)
            o_ref[cut:, span * s : span * s + span] = b_ref[x, 0, q, :below, span * i : span * i + span].astype(F)
    total = q_ref[...] * wq_ref[...].astype(F)
    for o_ref, w_ref in ((k_ref, wk_ref), (v_ref, wv_ref)):
        total = total + o_ref[...] * w_ref[...].astype(F)
    n_ref[...] = jnp.sum(total, -1, keepdims=True)

    def tile(x, q, n):
        row, lane = below + 16 * (n // 3), 128 * (n % 3)
        return b_ref[x, 0, q, row : row + 16, lane : lane + 128].astype(F)

    for i in range(local_heads):
        h = me_ref[0] * local_heads + i
        s = h // each
        upper = lax.rem(h, each) == 1
        x = lax.rem(s, 2)
        q = lax.rem(s // 2, 2) * 2 + s // 4
        for k in range(2):
            for j in range(2):
                ST[i, k, pl.ds(pl.multiple_of(16 * t, 16), 16), 128 * j : 128 * j + 128] = jnp.where(
                    upper, tile(x, q, 4 + k * 2 + j), tile(x, q, k * 2 + j)
                )
    for s in range(seqs):
        r_ref[0, s] = tile(*spot(s), 8)

    first = below + 48
    tall = out_ref.shape[0] // seqs

    def square(o_ref):
        for s in range(seqs):
            x, q = spot(s)
            for i in range(2):
                row = first + tall * i
                o_ref[tall * s : tall * s + tall, lanes * i : lanes * i + lanes] = b_ref[x, 0, q, row : row + tall].astype(F)

    @pl.when(t == 3)
    def _():
        for i in range(local_heads):
            f_ref[i] = ST[i, 0]
            s_ref[i] = ST[i, 1]

    @pl.when(t % 2 == 0)
    def _():
        square(out_ref)

    @pl.when(t % 2 == 1)
    def _():
        square(gate_ref)
        gate_n_ref[...] = jnp.sum(gate_ref[...] * wg_ref[...].astype(F), -1, keepdims=True)


def share_tiles(every_normed, back_sent, state_g, vectors, fed_parts, early, aside, heads, local_heads, head, weights_in):
    seqs, tps = lax.axis_size("seq"), lax.axis_size("tp")
    width = every_normed.shape[1]
    lanes = back_sent.shape[2]
    each = 2
    inner = state_g[0].shape[1]
    here = width // tps
    share = here + 48
    me = lax.axis_index("tp").astype(jnp.int32).reshape(1)
    sd = jax.ShapeDtypeStruct
    late, late_sent = pl.pallas_call(
        partial(pack_kernel, head),
        in_specs=[pl.BlockSpec(memory_space=pltpu.SMEM)] + [pl.BlockSpec(memory_space=pltpu.VMEM)] * 10,
        out_specs=[pl.BlockSpec(memory_space=pltpu.VMEM)] * 2,
        out_shape=[sd((2, share, lanes), LOW)] * 2,
        scratch_shapes=[
            pltpu.VMEM((width, lanes), F),
            pltpu.VMEM((each * head, inner), F),
            pltpu.VMEM((4, 16, 128), F),
        ],
        compiler_params=pltpu.CompilerParams(vmem_limit_bytes=20 * 1024 * 1024),
    )(me, every_normed, back_sent, *state_g, vectors)
    late = late.astype(F) + flip(late_sent, "tp", 1).astype(F)
    fed = lax.all_gather(summed(fed_parts), "seq", axis=0, tiled=False)
    late = scatter_once(late, "tp", 2).astype(LOW)[0]
    early = summed(swapped(early))
    late = jnp.concatenate([late, early[:, :lanes], early[:, lanes:]], 0)
    share = late.shape[0]
    late = double(late, "seq", 4)
    late = double(late, "seq", 2)
    late, back_sent = lax.optimization_barrier((late, back_sent))
    back = lax.all_to_all(back_sent, "seq", split_axis=0, concat_axis=0, tiled=True)
    cut = 160
    part_a, part_b = late[:, :, :cut], late[:, :, cut:]
    part_a, part_b = double(part_a, "seq", 1), double(part_b, "tp", 2)
    part_a, part_b = double(part_a, "tp", 2), double(part_b, "seq", 1)
    part_a, part_b, fed, back, aside = lax.optimization_barrier((part_a, part_b, fed, back, aside))
    part_a = part_a.reshape(2, seqs, cut, lanes)
    part_b = part_b.reshape(2, 2, seqs // 2, share - cut, lanes)
    got_a, got_b = flip(part_a, "tp", 1), flip(part_b, "tp", 1)
    a_spec = pl.BlockSpec((1, seqs, cut, lanes), lambda t: (t // 2, 0, 0, 0))
    b_spec = pl.BlockSpec((2, 1, seqs // 2, share - cut, lanes), lambda t: (0, t // 2, 0, 0, 0))
    square = pl.BlockSpec((here, width), lambda t: (t, 0))
    taller = pl.BlockSpec((2 * here, width), lambda t: (t // 2, 0))
    *weights, norm_gain_grad, head_f, head_s, small, out_g, gate_g, gate_n = pl.pallas_call(
        partial(last_kernel, seqs, each, heads, local_heads),
        grid=(tps,),
        in_specs=[
            pl.BlockSpec(memory_space=pltpu.SMEM),
            a_spec, b_spec, a_spec, b_spec, square, square, square, taller,
        ],
        out_specs=[
            square, square, square,
            pl.BlockSpec((here, 1), lambda t: (t, 0)),
            pl.BlockSpec((local_heads, head, inner), lambda t: (0, 0, 0)),
            pl.BlockSpec((local_heads, head, inner), lambda t: (0, 0, 0)),
            pl.BlockSpec((1, seqs, 16, 128), lambda t: (t, 0, 0, 0)),
            taller, taller,
            pl.BlockSpec((2 * here, 1), lambda t: (t // 2, 0)),
        ],
        out_shape=[sd((width, width), F)] * 3
        + [sd((width, 1), F), sd((local_heads, head, inner), F), sd((local_heads, head, inner), F)]
        + [sd((tps, seqs, 16, 128), F)]
        + [sd((width, width), F)] * 2
        + [sd((width, 1), F)],
        scratch_shapes=[pltpu.VMEM((local_heads, 2, head, inner), F)],
        compiler_params=pltpu.CompilerParams(vmem_limit_bytes=48 * 1024 * 1024),
    )(me, part_a, part_b, got_a, got_b, *weights_in)
    norm_gain_grad = norm_gain_grad + gate_n
    head_t = small[:, :, :2].transpose(1, 0, 2, 3).reshape(seqs * each, 2, inner)
    head_t = lax.dynamic_slice_in_dim(head_t, me[0] * local_heads, local_heads, 0)
    rate_weight_grad = small[:, :, 2:5].transpose(1, 0, 2, 3).reshape(seqs * each, width)[:heads].T
    vectors = jnp.sum(small[:, :, 5:10], 1).reshape(-1)[: 3 * width].reshape(3, width)
    return weights, (head_f, jnp.swapaxes(head_s, 1, 2)), head_t, rate_weight_grad, vectors, fed, back, (out_g, gate_g), aside, norm_gain_grad[:, 0]


def on_device(
    tokens, norm_gain, query_weight, key_weight, value_weight, rate_weight, rate_bias,
    first_weight, first_bias, second_weight, second_bias, inner_gain, inner_bias,
    branch_gate, output_weight, post_gain, post_bias, feed_gain, feed_gate, feed_linear,
    feed_down, cotangent,
):
    seqs = lax.axis_size("seq")
    rank = lax.axis_index("seq")
    heads = rate_weight.shape[1]
    local_heads, head, inner = first_weight.shape
    rows = tokens.shape[1]
    width = tokens.shape[2]
    each = -(-heads // seqs)
    span = each * head
    length = seqs * rows
    extra = -(-each // 16) * 16

    def to_chains(array):
        padded = jnp.pad(array, ((0, 0), (0, seqs * span - array.shape[1])))
        return padded.reshape(rows, seqs, span).transpose(1, 0, 2)

    def from_chains(array):
        return array.transpose(1, 0, 2).reshape(rows, seqs * span)[:, :width]

    def swap(array):
        return lax.all_to_all(array, "seq", split_axis=0, concat_axis=0, tiled=True)

    packed = pack_params(
        first_weight, jnp.swapaxes(second_weight, 1, 2), first_bias, second_bias, inner_gain, inner_bias, rate_bias[None]
    )
    every = lax.all_gather(packed, "tp", axis=0, tiled=True)
    own = lax.dynamic_slice_in_dim(every, jnp.minimum(rank * each, heads - each), each, 0)

    residual = tokens[0].astype(F)
    normed_val, norm_pull = jax.vjp(root_norm, residual, norm_gain)
    down_grad = cotangent[0]
    grad_out = down_grad.astype(F)
    every_grad = gather_near(down_grad, "tp")
    if span % 128 == 0 and width % span == 0 and rows == 128:
        sent, normed, gate_pre = project(
            tokens[0], norm_gain, query_weight, key_weight, value_weight, rate_weight.T, branch_gate, seqs, each, extra
        )
    else:
        normed = normed_val.astype(LOW)
        query_tok = matmul(normed, query_weight).astype(LOW)
        keys_tok = matmul(normed, key_weight).astype(LOW)
        values_tok = matmul(normed, value_weight).astype(LOW)
        logits_tok = matmul(normed, rate_weight).astype(LOW)
        gate_pre = matmul(normed, branch_gate)
        logit_rows = jnp.pad(logits_tok.T, ((0, seqs * each - heads), (0, 0))).reshape(seqs, each, rows)
        logit_rows = jnp.pad(logit_rows, ((0, 0), (0, extra - each), (0, 3 * span - rows)))
        sent = [to_chains(query_tok), to_chains(keys_tok), to_chains(values_tok)]
        sent = jnp.concatenate([jnp.concatenate(sent, -1), logit_rows], 1)
    got = swap(sent)

    every_normed = lax.all_gather(normed, "seq", axis=0, tiled=True)
    outs, *kept = fwd_scan(got, own)
    outs, every_normed, every_grad = lax.optimization_barrier((outs, every_normed, every_grad))
    mixed_tok = from_chains(swap(outs.reshape(seqs, rows, span))).astype(F)

    branch_val, branch_pull = jax.vjp(gated_branch, mixed_tok, gate_pre, post_gain, post_bias)
    branch_in = branch_val.astype(LOW)
    middle = residual + matmul(branch_in, output_weight)
    feed_val, feed_pull = jax.vjp(root_norm, middle, feed_gain)
    feed_in = feed_val.astype(LOW)
    every_in = gather_near(feed_in, "tp")
    gate_val = matmul(every_in, feed_gate)
    linear_val = matmul(every_in, feed_linear)
    act_val, act_pull = jax.vjp(swish_product, gate_val, linear_val)
    hidden = act_val.astype(LOW)

    hidden_grad = jnp.einsum("td,fd->tf", every_grad, feed_down, preferred_element_type=F)
    gate_grad, linear_grad = act_pull(hidden_grad)
    gate_low = gate_grad.astype(LOW)
    linear_low = linear_grad.astype(LOW)
    input_part = jnp.einsum("tf,df->td", gate_low, feed_gate, preferred_element_type=F) + jnp.einsum(
        "tf,df->td", linear_low, feed_linear, preferred_element_type=F
    )
    feed_down_grad = jnp.einsum("tf,td->fd", hidden, every_grad, preferred_element_type=F)
    both_low = jnp.concatenate([gate_low, linear_low], 1)
    feed_both_grad = jnp.einsum("tf,td->fd", both_low, every_in, preferred_element_type=F)
    fed_parts = jnp.concatenate(
        [
            feed_both_grad.astype(LOW).reshape(seqs, -1, width),
            feed_down_grad.astype(LOW).reshape(seqs, -1, width),
        ],
        1,
    )
    feed_in_grad = input_part
    for mask in masks_of("tp"):
        half = feed_in_grad.shape[0] // 2
        arrived = flip(feed_in_grad[half:].astype(LOW), "tp", mask)
        if mask == masks_of("tp")[-1]:
            arrived, fed_parts = lax.optimization_barrier((arrived, fed_parts))
        feed_in_grad = feed_in_grad[:half].astype(F) + arrived.astype(F)
    middle_part, feed_gain_grad = feed_pull(feed_in_grad)
    middle_grad = grad_out + middle_part
    out_low = middle_grad.astype(LOW)
    branch_grad = jnp.einsum("te,de->td", out_low, output_weight, preferred_element_type=F)
    mixed_grad, gate_pre_grad, post_gain_grad, post_bias_grad = branch_pull(branch_grad)
    out_grad_c = swap(to_chains(mixed_grad.astype(LOW))).reshape(length, span)

    second_part = matmul(hidden, feed_down).astype(LOW)
    second_part, out_grad_c = lax.optimization_barrier((second_part, out_grad_c))
    second_out = scatter_near(second_part, "tp")
    result = (middle + second_out).astype(LOW)[None]

    gate_low_pre = gate_pre_grad.astype(LOW)
    out_low, gate_low_pre, out_grad_c = lax.optimization_barrier((out_low, gate_low_pre, out_grad_c))
    tps = lax.axis_size("tp")
    lefts = jnp.stack([branch_in, normed])
    rights = jnp.stack([out_low, gate_low_pre])
    part_rows = 2 * width // tps
    orders = [0]
    for mask in reversed(masks_of("tp")):
        orders = orders + [o + mask for o in orders]
    parts = []
    for o in orders:
        owner = lax.axis_index("tp") ^ o
        which, place = owner % 2, owner // 2
        left = lax.dynamic_slice(lefts, (which, 0, place * part_rows), (1, rows, part_rows))
        right = lax.dynamic_index_in_dim(rights, which, 0, keepdims=True)
        parts.append((left, right))
    half = tps // 2

    def products(chosen):
        left = jnp.concatenate([p[0] for p in chosen], 0)
        right = jnp.concatenate([p[1] for p in chosen], 0)
        return jnp.einsum("jtd,jte->jde", left, right, preferred_element_type=F)

    early_sent = products(parts[half:]).astype(LOW)
    early = products(parts[:half]) + flip(early_sent, "tp", 1).astype(F)
    fed_parts, early, out_grad_c = lax.optimization_barrier((fed_parts, early.astype(LOW), out_grad_c))
    fed_parts = swap(fed_parts)
    for mask in masks_of("tp")[1:]:
        early = scatter_once(early, "tp", mask)

    back_sent, *state_g = bwd_scan(got, own, out_grad_c, *kept)
    early, fed_parts, back_sent = lax.optimization_barrier((early.astype(LOW), fed_parts, back_sent))
    vectors = jnp.stack([post_gain_grad, post_bias_grad, feed_gain_grad])
    share = share_tiles if each == 2 and tps == 4 and seqs == 8 else share_rows
    weights, head_w, head_t, rate_weight_grad, vectors, fed, back, early, result, norm_gain_grad = share(
        every_normed, back_sent, state_g, vectors, fed_parts, early, result, heads, local_heads, head,
        (query_weight, key_weight, value_weight, branch_gate),
    )
    if span % 128 == 0 and width % span == 0 and rows == 128:
        tokens_grad = tokens_back(
            tokens[0], norm_gain, middle_grad, back, gate_low_pre,
            query_weight, key_weight, value_weight, rate_weight.T, branch_gate, each,
        )[None]
    else:
        query_low = from_chains(back[:, :rows, :span])
        keys_low = from_chains(back[:, :rows, span : 2 * span])
        values_low = from_chains(back[:, :rows, 2 * span :])
        logit_low = back[:, rows : rows + each, :rows].reshape(seqs * each, rows)[:heads].T

        normed_grad = (
            jnp.einsum("te,de->td", query_low, query_weight, preferred_element_type=F)
            + jnp.einsum("te,de->td", keys_low, key_weight, preferred_element_type=F)
            + jnp.einsum("te,de->td", values_low, value_weight, preferred_element_type=F)
            + jnp.einsum("te,de->td", logit_low, rate_weight, preferred_element_type=F)
            + jnp.einsum("te,de->td", gate_low_pre, branch_gate, preferred_element_type=F)
        )
        residual_part, unused = norm_pull(normed_grad)
        tokens_grad = (middle_grad + residual_part)[None]
    inner_units = feed_gate.shape[1]
    if 2 * inner_units // seqs % 128 == 0:
        fed_grads = feed_outputs(fed, inner_units)
    else:
        both = fed[:, : 2 * inner_units // seqs].reshape(2, inner_units, width).astype(F)
        down = fed[:, 2 * inner_units // seqs : 3 * inner_units // seqs].reshape(inner_units, width).astype(F)
        fed_grads = (both[0].T, both[1].T, down)
    norm_gain_grad = norm_gain_grad + jnp.sum(rate_weight_grad * rate_weight.astype(F), -1)
    norm_gain_grad = norm_gain_grad / norm_gain
    tail_sum = head_t[:, 1]
    return (
        result,
        tokens_grad,
        norm_gain_grad,
        weights[0],
        weights[1],
        weights[2],
        rate_weight_grad,
        tail_sum[:, 3 * head],
        head_w[0],
        head_t[:, 0],
        head_w[1],
        tail_sum[:, :head],
        tail_sum[:, head : 2 * head],
        tail_sum[:, 2 * head : 3 * head],
        early[1],
        early[0],
        vectors[0],
        vectors[1],
        vectors[2],
        *fed_grads,
    )


def solution(mesh):
    in_specs = (
        P("tp", "seq", None),
        P(),
        P(),
        P(),
        P(),
        P(),
        P("tp"),
        P("tp", None, None),
        P("tp", None),
        P("tp", None, None),
        P("tp", None),
        P("tp", None),
        P("tp", None),
        P(),
        P(),
        P(),
        P(),
        P(),
        P(None, "tp"),
        P(None, "tp"),
        P("tp", None),
        P("tp", "seq", None),
    )
    out_specs = (
        P("tp", "seq", None),
        P("tp", "seq", None),
        P(),
        P(),
        P(),
        P(),
        P(),
        P("tp"),
        P("tp", None, None),
        P("tp", None),
        P("tp", None, None),
        P("tp", None),
        P("tp", None),
        P("tp", None),
        P(),
        P(),
        P(),
        P(),
        P(),
        P(None, "tp"),
        P(None, "tp"),
        P("tp", None),
    )
    return jax.shard_map(
        on_device, mesh=mesh, in_specs=in_specs, out_specs=out_specs, check_vma=False
    )
```

```python
from functools import partial

import jax
import jax.numpy as jnp
from jax import lax
from jax.sharding import PartitionSpec as P
from jax.experimental import pallas as pl
from jax.experimental.pallas import tpu as pltpu
from itertools import chain
C0=0.7978845608028654
C1=0.044715
EPS=1e-6
RATE_SCALE=0.25
B=16
CH=128
NB=CH//B
LOW=jnp.bfloat16
F=jnp.float32
def nn(a,b): return lax.dot_general(a.astype(LOW),b.astype(LOW),(((1,),(0,)),((),())),preferred_element_type=F)
def nt(a,b): return lax.dot_general(a.astype(LOW),b.astype(LOW),(((1,),(1,)),((),())),preferred_element_type=F)
def tn(a,b): return lax.dot_general(a.astype(LOW),b.astype(LOW),(((0,),(0,)),((),())),preferred_element_type=F)
def gelu1(z):
    return z*(0.5+0.5*jnp.tanh(z*(C0+(C0*C1)*(z*z))))
def gelu2(z):
    z2=z*z
    t=jnp.tanh(z*(C0+(C0*C1)*z2))
    h=0.5+0.5*t
    x=z*h
    return x,h+x*(1-t)*(C0+(3*C0*C1)*z2)
def gelu3(z):
    z2=z*z
    t=jnp.tanh(z*(C0+(C0*C1)*z2))
    u1=C0+(3*C0*C1)*z2
    h=0.5+0.5*t
    h1=h*(1-t)*u1
    x=z*h
    return x,h+z*h1,2*h1+z*(h*(1-t)*(6*C0*C1)*z-2*t*u1*h1)
def lane_masks(C,H,R):
    lane=lax.broadcasted_iota(jnp.int32,(R,C*H),1)
    return [(lane>=H*c)&(lane<H*c+H) for c in range(C)]
def expand(C,x,masks):
    if C==1: return x
    zero=jnp.zeros((B,x.shape[1]),x.dtype)
    return jnp.concatenate([jnp.where(masks[c],x[B*j:B*j+B],zero) for j in range(x.shape[0]//B) for c in range(C)],0)
def collapse(C,x,masks):
    if C==1: return x
    rows=[]
    for j in range(x.shape[0]//(B*C)):
        y=x[B*C*j:B*C*j+B]
        for c in range(1,C): y=jnp.where(masks[c],x[B*(C*j+c):B*(C*j+c)+B],y)
        rows.append(y)
    return jnp.concatenate(rows,0) if len(rows)>1 else rows[0]
def tile_rows(C,x,n):
    t=jnp.concatenate([jnp.broadcast_to(x[c:c+1],(B,x.shape[1])) for c in range(C)],0)
    return jnp.concatenate([t]*n,0) if n>1 else t
def fill_masks(C,TRI,BLK,back):
    n=CH*C
    r=lax.broadcasted_iota(jnp.int32,(n,n),0); c=lax.broadcasted_iota(jnp.int32,(n,n),1)
    rs,cs=r//(B*C),c//(B*C)
    same=((r//B)%C)==((c//B)%C)
    tri=same&((cs<rs)|((cs==rs)&((c%B)<=(r%B))))
    TRI[...]=jnp.where(tri,1.0,0.0)
    BLK[...]=jnp.where(same&(cs<rs),1.0,0.0)
    if back is not None: back[...]=jnp.where(same&(cs>rs),1.0,0.0)
def ones_of(C,H):
    r=lax.broadcasted_iota(jnp.int32,(C*H,C*H),0); c=lax.broadcasted_iota(jnp.int32,(C*H,C*H),1)
    return jnp.where((r//H)==(c//H),1.0/H,0.0).astype(LOW)
def sums_of(C):
    r=lax.broadcasted_iota(jnp.int32,(C,CH*C),0); c=lax.broadcasted_iota(jnp.int32,(C,CH*C),1)
    return jnp.where(((c//B)%C)==r,1.0,0.0).astype(LOW)
def stack_col(C,r):
    return jnp.concatenate([r[B*j:B*j+B,c:c+1] for j in range(r.shape[0]//B) for c in range(C)],0)
def pair_cols(C,H,r,masks):
    y=jnp.broadcast_to(r[:,0:1],(r.shape[0],C*H))
    for c in range(1,C): y=jnp.where(masks[c],r[:,c:c+1],y)
    return y

def rates(C,x_ref,own_ref,H):
    rows=[x_ref[0,CH+c:CH+c+1,:CH].astype(F)+own_ref[c,2*H+1:2*H+2,3*H:3*H+1] for c in range(C)]
    rows=jnp.concatenate(rows+[jnp.zeros((CH-C,CH),F)],0)
    return (jax.nn.sigmoid(rows)*(RATE_SCALE/H)).T

def pair_row(C,H,own_ref,k):
    return jnp.concatenate([own_ref[c,2*H+1:2*H+2,k*H:k*H+H] for c in range(C)],1)

def mask_stack(C,H):
    r=lax.broadcasted_iota(jnp.int32,(B*C,C*H),0)//B; c=lax.broadcasted_iota(jnp.int32,(B*C,C*H),1)//H
    return r==c

def fwd_pre(C,H,x,own_ref,BLK,gam,bet,S):
    W=C*H
    m16=lane_masks(C,H,B); m128=lane_masks(C,H,CH)
    K=x[0,:CH,W:2*W]
    Kst=expand(C,K,m16)
    S["KST"][...]=Kst; S["QST"][...]=expand(C,x[0,:CH,:W],m16)
    S["T"][...]=(bet+K.astype(F)-x[0,:CH,2*W:].astype(F))*gam
    yield
    R=rates(C,x,own_ref,H)
    S["R"][...]=R
    S["RP"][...]=pair_cols(C,H,R,m128)
    yield
    S["KK"][...]=((nt(Kst,Kst)+1.0)*BLK[...]).astype(LOW)
    tst=expand(C,S["T"][...],m16)
    S["TST"][...]=tst
    S["CT"][...]=nn(tst,jnp.full((W,W),1.0/H,LOW))
    yield

def fwd_steps(C,H,S,W1,B1,U,B2,gam,z1_ref,p_ref,zc_ref,us_ref,w1s_ref,o,side,times):
    W=C*H; SB=B*C; TALL=C*CH
    m16=lane_masks(C,H,B)
    ones=ones_of(C,H)
    g2=gam*gam
    Kst=S["KST"][...]
    w1b=W1[...].astype(LOW); w1s_ref[o]=w1b
    S["W1"][...]=w1b; S["B1"][...]=B1[...]; S["B2"][...]=B2[...]
    b1r=tile_rows(C,B1[...],1)
    uf=U[...]; ub=uf.astype(LOW); S["U"][...]=ub
    b2=B2[...]
    S["BASE"][...]=nn(Kst,w1b)
    g2m=jnp.concatenate([jnp.broadcast_to(jnp.sum(jnp.where(m16[c][:1],g2,0.0),1,keepdims=True)*(1.0/H),(B,W)) for c in range(C)],0)
    mst=mask_stack(C,H)
    full=jnp.full((W,W),1.0/H,LOW)
    I=W1.shape[1]
    wide=lambda v: jnp.concatenate([v]*(I//W),1)
    for j in range(NB):
        sl=slice(B*j,B*j+B); st=slice(SB*j,SB*j+SB)
        z1=S["BASE"][st]+b1r
        if j>0: z1=z1-nn(S["KK"][st,:SB*j],S["S1"][:SB*j])
        x2,g1=gelu2(z1)
        x2b=x2.astype(LOW)
        t=S["TST"][st]; ct=S["CT"][st]; rr=stack_col(C,S["R"][sl])
        tU=nn(t,ub)
        zc=jnp.where(mst,nt(x2b,ub)+b2,0.0)
        zz=zc*zc; zg=zc*g2
        AB=nn(jnp.concatenate([zg,zc],0),ub)
        mm=nn(jnp.concatenate([zc,zz,zg,zz*g2,zc*t],0),full)
        mu=mm[0:SB]; mzz=mm[SB:2*SB]; mzg=mm[2*SB:3*SB]; mzzg=mm[3*SB:4*SB]; mzt=mm[4*SB:]
        s=lax.rsqrt(mzz-mu*mu+EPS)
        m1=s*(mzg-mu*g2m)+ct
        m2=s*(s*(mzzg-2.0*mu*mzg+mu*mu*g2m)+mzt-mu*ct)
        ss=s*s
        P=wide(ss)*(AB[:SB]-wide(m2)*AB[SB:])+wide(s)*tU
        s1=(P*(g1*rr)).astype(LOW)
        d2=ss*(zg-m2*zc)+s*t+jnp.where(mst,ss*mu*(m2-g2)-s*m1,0.0)
        s2=d2*rr
        s2b=s2.astype(LOW)
        zc=collapse(C,zc-mu,m16)
        S["S1"][st]=s1; S["S2"][st]=s2b; S["X2"][st]=x2b
        z1_ref[TALL*o+SB*j:TALL*o+SB*j+SB]=z1; p_ref[TALL*o+SB*j:TALL*o+SB*j+SB]=P
        zc_ref[CH*o+B*j:CH*o+B*j+B]=zc
        us_ref[o,j]=ub
        uf=uf-tn(s2b,x2b); ub=uf.astype(LOW)
        b2=b2-jnp.sum(s2,0,keepdims=True)
        for _ in range(times): next(side,None)
    U[...]=uf; B2[...]=b2
    S1v=S["S1"][...]
    W1[...]=W1[...]-tn(Kst,S1v)
    B1[...]=B1[...]-nn(sums_of(C),S1v)

def fwd_query(C,H,S,x,TRI,gam,bet,o_ref,z1q_ref,zq_ref,o):
    W=C*H; TALL=C*CH
    m16=lane_masks(C,H,B)
    ones=ones_of(C,H)
    A1=((nt(S["QST"][...],S["KST"][...])+1.0)*TRI[...]).astype(LOW)
    yield
    z1q=nn(S["QST"][...],S["W1"][...])+tile_rows(C,S["B1"][...],NB)-nn(A1,S["S1"][...])
    z1q_ref[TALL*o:TALL*o+TALL]=z1q
    x2q=gelu1(z1q).astype(LOW)
    yield
    A2=((nt(x2q,S["X2"][...])+1.0)*TRI[...]).astype(LOW)
    yield
    zq=collapse(C,nt(x2q,S["U"][...])-nn(A2,S["S2"][...]),m16)+S["B2"][...]
    zq=zq-nn(zq,ones)
    zq_ref[CH*o:CH*o+CH]=zq
    yield
    yq=zq*lax.rsqrt(nn(zq*zq,ones)+EPS)
    o_ref[CH*o:CH*o+CH]=(x[0,:CH,:W].astype(F)+yq*gam+bet).astype(LOW)
    yield

FSLOT=("TST","KST","QST","T","R","RP","KK","CT","W1","B1","U","B2","BASE","S1","S2","X2")

def fwd_kernel(C,H,xa_ref,xb_ref,own_ref,o_ref,z1_ref,p_ref,zc_ref,z1q_ref,zq_ref,us_ref,w1s_ref,W1,B1,U,B2,TRI,BLK,*slots):
    k=len(FSLOT)
    even=dict(zip(FSLOT,slots[:k])); odd=dict(zip(FSLOT,slots[k:]))
    gam=pair_row(C,H,own_ref,1); bet=pair_row(C,H,own_ref,2)
    @pl.when(pl.program_id(0)==0)
    def _():
        for c in range(C):
            W1[H*c:H*c+H]=own_ref[c,:H]
            u=own_ref[c,H:2*H]
            U[H*c:H*c+H]=u-jnp.sum(u,0,keepdims=True)*(1.0/H)
            B1[c:c+1]=own_ref[c,2*H:2*H+1]
        raw=[own_ref[c,2*H+1:2*H+2,:H] for c in range(C)]
        B2[...]=jnp.concatenate([v-jnp.sum(v,1,keepdims=True)*(1.0/H) for v in raw],1)
        fill_masks(C,TRI,BLK,None)
    for _ in fwd_pre(C,H,xa_ref,own_ref,BLK,gam,bet,even): pass
    side=fwd_pre(C,H,xb_ref,own_ref,BLK,gam,bet,odd)
    fwd_steps(C,H,even,W1,B1,U,B2,gam,z1_ref,p_ref,zc_ref,us_ref,w1s_ref,0,side,1)
    for _ in side: pass
    side=fwd_query(C,H,even,xa_ref,TRI,gam,bet,o_ref,z1q_ref,zq_ref,0)
    fwd_steps(C,H,odd,W1,B1,U,B2,gam,z1_ref,p_ref,zc_ref,us_ref,w1s_ref,1,side,1)
    for _ in side: pass
    for _ in fwd_query(C,H,odd,xb_ref,TRI,gam,bet,o_ref,z1q_ref,zq_ref,1): pass

def fwd_scan(x,own):
    n,tall,W=x.shape
    W//=3
    C=own.shape[0]; I=own.shape[2]; H=W//C; L=n*CH; m=C*CH
    rows=lambda k,w: pl.BlockSpec((2*k,w),lambda i:(i,0))
    sd=jax.ShapeDtypeStruct
    V=pltpu.VMEM
    kinds=dict(KST=V((m,W),LOW),QST=V((m,W),LOW),T=V((CH,W),F),R=V((CH,CH),F),RP=V((CH,W),F),KK=V((m,m),LOW),CT=V((m,W),F),TST=V((m,W),F),W1=V((W,I),LOW),
        B1=V((C,I),F),U=V((W,I),LOW),B2=V((1,W),F),BASE=V((m,I),F),S1=V((m,I),LOW),S2=V((m,W),LOW),X2=V((m,I),LOW))
    return pl.pallas_call(partial(fwd_kernel,C,H),grid=(n//2,),
        in_specs=[pl.BlockSpec((1,tall,3*W),lambda i:(2*i,0,0)),pl.BlockSpec((1,tall,3*W),lambda i:(2*i+1,0,0)),pl.BlockSpec(own.shape,lambda i:(0,0,0))],
        out_specs=[rows(CH,W),rows(m,I),rows(m,I),rows(CH,W),rows(m,I),rows(CH,W),
            pl.BlockSpec((2,NB,W,I),lambda i:(i,0,0,0)),pl.BlockSpec((2,W,I),lambda i:(i,0,0))],
        out_shape=[sd((L,W),LOW),sd((C*L,I),F),sd((C*L,I),F),sd((L,W),F),sd((C*L,I),F),sd((L,W),F),sd((n,NB,W,I),LOW),sd((n,W,I),LOW)],
        scratch_shapes=[V((W,I),F),V((C,I),F),V((W,I),F),V((1,W),F),V((m,m),F),V((m,m),F)]+[kinds[name] for name in FSLOT]*2,
        compiler_params=pltpu.CompilerParams(vmem_limit_bytes=48*1024*1024),
    )(x,x,own)

SLOT=("BASE","DX2","X2","RG1","G1","RPG2","DS2Q","KK","YB","GB","DB","SB","M2B","RED","S2E","S1B","X2Q","DZQ","DZ1Q","DKQ","DQ","KST","QST","T0","RP","PG1","R")

def slot_shapes(C,W,I):
    m=C*CH
    V=pltpu.VMEM
    wide,pair,tall=V((m,I),F),V((CH,W),F),V((m,W),LOW)
    kinds=dict(BASE=wide,DX2=wide,X2=V((m,I),LOW),RG1=wide,G1=wide,RPG2=wide,DS2Q=pair,KK=V((m,m),LOW),YB=pair,GB=pair,DB=pair,SB=pair,M2B=pair,
        RED=V((4*CH,W),F),S2E=tall,S1B=V((m,I),LOW),X2Q=V((m,I),LOW),DZQ=tall,DZ1Q=V((m,I),LOW),DKQ=V((m,W),F),DQ=V((CH,W),LOW),KST=tall,QST=tall,
        T0=pair,RP=pair,PG1=wide,R=V((CH,CH),F))
    return [kinds[name] for name in SLOT]

def bwd_pre(C,H,ins,own_ref,S,TRI,BLKT,gam,bet,dgam_ref,dbet_ref,factor):
    x_ref,do_ref,z1_ref,p_ref,zc_ref,z1q_ref,zq_ref,us_ref,w1s_ref=ins
    W=C*H
    m16=lane_masks(C,H,B); m128=lane_masks(C,H,CH)
    ones=ones_of(C,H)
    g2=gam*gam
    K=x_ref[0,:CH,W:2*W]
    Kst=expand(C,K,m16); Qst=expand(C,x_ref[0,:CH,:W],m16)
    S["KST"][...]=Kst; S["QST"][...]=Qst
    R=rates(C,x_ref,own_ref,H)
    S["R"][...]=R
    RP=pair_cols(C,H,R,m128)
    S["RP"][...]=RP
    dO=do_ref[...].astype(F)
    zq=zq_ref[...]; sq=lax.rsqrt(nn(zq*zq,ones)+EPS); yq=zq*sq
    dyq=dO*gam
    rq=nn(jnp.concatenate([dyq,dyq*yq],0),ones)
    dzq=sq*(dyq-rq[:CH]-yq*rq[CH:])
    dzqb=expand(C,dzq.astype(LOW),m16)
    S["DZQ"][...]=dzqb
    dgam_ref[...]=dgam_ref[...]+factor*jnp.sum(dO*yq,0,keepdims=True)
    dbet_ref[...]=dbet_ref[...]+factor*jnp.sum(dO,0,keepdims=True)
    yield
    zc=zc_ref[...]
    s=lax.rsqrt(nn(zc*zc,ones)+EPS)
    y=zc*s
    t0=bet+K.astype(F)-x_ref[0,:CH,2*W:].astype(F)
    G=y*g2+t0*gam
    red=nn(jnp.concatenate([G,G*y,g2*y,g2*y*y],0),ones)
    m1=red[:CH]; m2=red[CH:2*CH]
    d2=s*(G-m1-y*m2)
    s2=expand(C,(d2*RP).astype(LOW),m16)
    S["YB"][...]=y; S["GB"][...]=G; S["DB"][...]=d2; S["SB"][...]=s; S["M2B"][...]=m2; S["RED"][...]=red; S["S2E"][...]=s2; S["T0"][...]=t0
    yield
    x2,g1,gg2=gelu3(z1_ref[...]); x2=x2.astype(LOW)
    P=p_ref[...]
    RS=stack_col(C,R)
    rg1=RS*g1
    s1=(P*rg1).astype(LOW)
    S["X2"][...]=x2; S["G1"][...]=g1; S["RG1"][...]=rg1; S["RPG2"][...]=RS*(P*gg2); S["PG1"][...]=P*g1; S["S1B"][...]=s1
    yield
    x2q,g1q=gelu2(z1q_ref[...]); x2q=x2q.astype(LOW)
    S["X2Q"][...]=x2q
    A2=((nt(x2q,S["X2"][...])+1.0)*TRI[...]).astype(LOW)
    dA2=(nt(dzqb,s2)*TRI[...]).astype(LOW)
    yield
    dx2q=nn(dzqb,us_ref[0,0])-nn(dA2,S["X2"][...])
    S["DX2"][...]=-tn(dA2,x2q)
    S["DS2Q"][...]=-collapse(C,tn(A2,dzqb),m16)
    dz1qb=(dx2q*g1q).astype(LOW)
    S["DZ1Q"][...]=dz1qb
    yield
    A1=((nt(Qst,Kst)+1.0)*TRI[...]).astype(LOW)
    dA1=(nt(dz1qb,S["S1B"][...])*TRI[...]).astype(LOW)
    S["KK"][...]=((nt(Kst,Kst)+1.0)*BLKT[...]).astype(LOW)
    yield
    S["DQ"][...]=(dO+collapse(C,nt(dz1qb,w1s_ref[0])-nn(dA1,Kst),m16)).astype(LOW)
    S["DKQ"][...]=tn(dA1,Qst)
    S["BASE"][...]=-tn(A1,dz1qb)
    yield

def bwd_steps(C,H,S,us_ref,u,w1,H1,h1,HU,h2,BLK,gam,bet,dgam_ref,dbet_ref,DZ1,DS1,DS2,DG,dx_ref,db_ref,o,side):
    W=C*H; SB=B*C
    m16=lane_masks(C,H,B); m128=lane_masks(C,H,CH)
    ones=ones_of(C,H); sums=sums_of(C)
    g2=gam*gam
    Kst=S["KST"][...]
    h1b=H1[...].astype(LOW)
    S["BASE"][...]=S["BASE"][...]-nn(Kst,h1b)-tile_rows(C,h1[...],NB)
    dk=nt(S["S1B"][...],h1b)+S["DKQ"][...]
    g2m=nn(jnp.broadcast_to(g2,(8,W)),ones)[0:1]
    hu=HU[...]; hh2=h2[...]
    for j in reversed(range(NB)):
        sl=slice(B*j,B*j+B); st=slice(SB*j,SB*j+SB)
        ub=us_ref[u,j]
        rr=S["RP"][sl]
        hub=hu.astype(LOW)
        x2j=S["X2"][st]
        ds1=S["BASE"][st]
        if j<NB-1: ds1=ds1-nn(S["KK"][st,SB*j+SB:],DZ1[SB*j+SB:])
        ds2=S["DS2Q"][sl]-collapse(C,nt(x2j,hub),m16)-hh2
        dx2=S["DX2"][st]-nn(S["S2E"][st],hub)
        dPb=(ds1*S["RG1"][st]).astype(LOW)
        e=rr*ds2+collapse(C,nt(dPb,ub),m16)
        s=S["SB"][sl]; m2=S["M2B"][sl]; y=S["YB"][sl]; g_=S["GB"][sl]; d2=S["DB"][sl]
        m1=S["RED"][sl]; gy=S["RED"][2*CH+B*j:2*CH+B*j+B]; gyy=S["RED"][3*CH+B*j:3*CH+B*j+B]
        ge=g2*e
        mm=nn(jnp.concatenate([e,e*y,e*d2,ge,ge*y],0),ones)
        a=mm[0:B]; b=mm[B:2*B]; cc=mm[2*B:3*B]; mge=mm[3*B:4*B]; mgey=mm[4*B:]
        dG=s*(e-a-y*b)
        mdY=s*(mge-a*g2m-b*gy-m2*a-b*m1)
        mdYY=s*(mgey-a*gy-b*gyy-2.0*b*m2)
        dZc=s*(g2*dG-s*(m2*e+g_*b)-mdY-y*(cc+mdYY))
        dZcb=expand(C,dZc.astype(LOW),m16)
        dx2=dx2+nn(dZcb,ub)
        dz1=(dx2*S["G1"][st]+ds1*S["RPG2"][st]).astype(LOW)
        DZ1[st]=dz1
        DS1[st]=ds1; DS2[sl]=ds2; DG[sl]=dG
        hu=hu+tn(jnp.concatenate([expand(C,d2.astype(LOW),m16),dZcb],0),jnp.concatenate([dPb,x2j],0))
        hh2=hh2+jnp.sum(dZc,0,keepdims=True)
        next(side,None)
    dz1=DZ1[...]
    M=(nt(dz1,S["S1B"][...])*BLK[...]).astype(LOW)
    dG=DG[...]; dGg=dG*gam
    dk=collapse(C,nt(dz1,w1)-dk-nn(M,Kst)-tn(M,Kst),m16)+dGg
    dx_ref[o,:CH,:W]=S["DQ"][...]
    dx_ref[o,:CH,W:2*W]=dk.astype(LOW)
    dx_ref[o,:CH,2*W:]=(-dGg).astype(LOW)
    dr1=jnp.sum(DS1[...]*S["PG1"][...],-1,keepdims=True)
    dr2=DS2[...]*S["DB"][...]
    lane=lax.broadcasted_iota(jnp.int32,(CH,CH),1)
    dr=jnp.zeros((CH,CH),F)
    for c in range(C):
        rows=[dr1[B*(C*j+c):B*(C*j+c)+B] for j in range(NB)]
        col=jnp.concatenate(rows,0)+jnp.sum(jnp.where(m128[c],dr2,0.0),-1,keepdims=True)
        dr=jnp.where(lane==c,col,dr)
    R=S["R"][...]
    dr=dr*R*(1.0-R*(H/RATE_SCALE))
    db_ref[...]=db_ref[...]+jnp.sum(dr,0,keepdims=True)
    dr=dr.T.astype(LOW)
    extra=dx_ref.shape[1]-CH
    dx_ref[o,CH:,:]=jnp.zeros((extra,3*W),LOW)
    dx_ref[o,CH:,:CH]=dr[:extra]
    dgam_ref[...]=dgam_ref[...]+jnp.sum(dG*(2*S["YB"][...]*gam+S["T0"][...]),0,keepdims=True)
    dbet_ref[...]=dbet_ref[...]+jnp.sum(dGg,0,keepdims=True)
    dz1qb=S["DZ1Q"][...]
    H1[...]=H1[...]+tn(Kst,dz1)+tn(S["QST"][...],dz1qb)
    h1[...]=h1[...]+nn(sums,dz1)+nn(sums,dz1qb)
    HU[...]=hu+tn(S["DZQ"][...],S["X2Q"][...])
    h2[...]=hh2+jnp.sum(collapse(C,S["DZQ"][...].astype(F),m16),0,keepdims=True)

def bwd_kernel(C,H,steps,*refs):
    first,near,far=refs[:9],refs[9:18],refs[18:27]
    us_ref,w1_ref,own_ref,dx_ref,H1,h1,HU,h2,dgam_ref,dbet_ref,db_ref,TRI,BLK,BLKT,DZ1,DS1,DS2,DG=refs[27:45]
    k=len(SLOT)
    even=dict(zip(SLOT,refs[45:45+k])); odd=dict(zip(SLOT,refs[45+k:]))
    gam=pair_row(C,H,own_ref,1); bet=pair_row(C,H,own_ref,2)
    @pl.when(pl.program_id(0)==0)
    def _():
        for ref in (H1,h1,HU,h2,dgam_ref,dbet_ref,db_ref): ref[...]=jnp.zeros_like(ref)
        fill_masks(C,TRI,BLK,BLKT)
        for _ in bwd_pre(C,H,first,own_ref,even,TRI,BLKT,gam,bet,dgam_ref,dbet_ref,1.0): pass
    more=jnp.where(pl.program_id(0)<steps-1,1.0,0.0)
    side=bwd_pre(C,H,near,own_ref,odd,TRI,BLKT,gam,bet,dgam_ref,dbet_ref,1.0)
    bwd_steps(C,H,even,us_ref,1,w1_ref[1],H1,h1,HU,h2,BLK,gam,bet,dgam_ref,dbet_ref,DZ1,DS1,DS2,DG,dx_ref,db_ref,1,side)
    side=bwd_pre(C,H,far,own_ref,even,TRI,BLKT,gam,bet,dgam_ref,dbet_ref,more)
    bwd_steps(C,H,odd,us_ref,0,w1_ref[0],H1,h1,HU,h2,BLK,gam,bet,dgam_ref,dbet_ref,DZ1,DS1,DS2,DG,dx_ref,db_ref,0,side)

def bwd_scan(x,own,do,z1,p,zc,z1q,zq,us,w1s):
    n,tall,W=x.shape
    W//=3
    C=own.shape[0]; I=own.shape[2]; H=W//C
    full=lambda *s: pl.BlockSpec(s,lambda i:(0,)*len(s))
    sd=jax.ShapeDtypeStruct
    V=pltpu.VMEM
    m=C*CH
    def chunk(at):
        rows=lambda k,w: pl.BlockSpec((k,w),lambda i:(at(i),0))
        return [pl.BlockSpec((1,tall,3*W),lambda i:(at(i),0,0)),rows(CH,W),rows(m,I),rows(m,I),rows(CH,W),rows(m,I),rows(CH,W),
            pl.BlockSpec((1,1,W,I),lambda i:(at(i),0,0,0)),pl.BlockSpec((1,W,I),lambda i:(at(i),0,0))]
    ins=(x,do,z1,p,zc,z1q,zq,us,w1s)
    return pl.pallas_call(partial(bwd_kernel,C,H,n//2),grid=(n//2,),
        in_specs=chunk(lambda i:n-1)+chunk(lambda i:n-2-2*i)+chunk(lambda i:jnp.maximum(n-3-2*i,0))+[
            pl.BlockSpec((2,NB,W,I),lambda i:(n//2-1-i,0,0,0)),pl.BlockSpec((2,W,I),lambda i:(n//2-1-i,0,0)),full(*own.shape)],
        out_specs=[pl.BlockSpec((2,tall,3*W),lambda i:(n//2-1-i,0,0)),full(W,I),full(C,I),full(W,I),full(1,W),full(1,W),full(1,W),full(1,CH)],
        out_shape=[sd((n,tall,3*W),LOW),sd((W,I),F),sd((C,I),F),sd((W,I),F),sd((1,W),F),sd((1,W),F),sd((1,W),F),sd((1,CH),F)],
        scratch_shapes=[V((m,m),F),V((m,m),F),V((m,m),F),V((m,I),LOW),V((m,I),F),V((CH,W),F),V((CH,W),F)]+slot_shapes(C,W,I)*2,
        compiler_params=pltpu.CompilerParams(vmem_limit_bytes=48*1024*1024),
        cost_estimate=pl.CostEstimate(flops=1000,bytes_accessed=1000,transcendentals=0),
    )(*ins,*ins,*ins,us,w1s,own)

RATE_SCALE = 0.25
NORM_EPS = 1e-05


def smooth_act(value):
    return 0.5 * value * (1.0 + jnp.tanh(C0 * (value + C1 * value * value * value)))


def root_norm(value, gain):
    return value * lax.rsqrt(jnp.mean(value * value, -1, keepdims=True) + NORM_EPS) * gain


def layer_norm(value, gain, bias):
    centre = value - jnp.mean(value, -1, keepdims=True)
    return centre * lax.rsqrt(jnp.mean(centre * centre, -1, keepdims=True) + NORM_EPS) * gain + bias


def gated_branch(mixed, gate_pre, gain, bias):
    return layer_norm(mixed, gain, bias) * smooth_act(gate_pre)


def swish_product(gate_val, linear_val):
    return jax.nn.silu(gate_val) * linear_val


def matmul(left, right):
    return jnp.dot(left, right, preferred_element_type=F)


def flip(array, axis, mask):
    peers = lax.axis_size(axis)
    return lax.ppermute(array, axis, [(i, i ^ mask) for i in range(peers)])


def masks_of(axis):
    masks = []
    while 1 << len(masks) < lax.axis_size(axis):
        masks.append(1 << len(masks))
    return masks


def side(axis, mask):
    return (lax.axis_index(axis) // mask) % 2


def gather_near(array, axis):
    for mask in reversed(masks_of(axis)):
        array = jnp.concatenate([array, flip(array, axis, mask)], 0)
    return array


def scatter_once(array, axis, mask):
    half = array.shape[0] // 2
    return array[:half].astype(F) + flip(array[half:].astype(LOW), axis, mask).astype(F)


def scatter_near(array, axis):
    for mask in masks_of(axis):
        array = scatter_once(array, axis, mask)
    return array


def halve(array, axis, mask, dim):
    bit = side(axis, mask)
    mine = lax.dynamic_index_in_dim(array, bit, dim, keepdims=False)
    other = lax.dynamic_index_in_dim(array, 1 - bit, dim, keepdims=False)
    return mine.astype(F) + flip(other.astype(LOW), axis, mask).astype(F)


def double(array, axis, mask):
    got = flip(array, axis, mask)
    upper = side(axis, mask) == 1
    return jnp.stack([jnp.where(upper, got, array), jnp.where(upper, array, got)])


def params_kernel(f_ref, s_ref, fb_ref, sb_ref, g_ref, b_ref, r_ref, o_ref):
    heads, head, inner = f_ref.shape
    for i in range(heads):
        o_ref[i, :head] = f_ref[i]
        o_ref[i, head : 2 * head] = s_ref[i]
        o_ref[i, 2 * head :] = jnp.zeros((8, inner), F)
        o_ref[i, 2 * head : 2 * head + 1] = fb_ref[i : i + 1]
        small = [ref[i : i + 1] for ref in (sb_ref, g_ref, b_ref)]
        small.append(jnp.broadcast_to(r_ref[:, i : i + 1], (1, inner - 3 * head)))
        o_ref[i, 2 * head + 1 : 2 * head + 2] = jnp.concatenate(small, 1)


def pack_params(first_weight, *others):
    heads, head, inner = first_weight.shape
    return pl.pallas_call(
        params_kernel,
        in_specs=[pl.BlockSpec(memory_space=pltpu.VMEM)] * 7,
        out_specs=pl.BlockSpec(memory_space=pltpu.VMEM),
        out_shape=jax.ShapeDtypeStruct((heads, 2 * head + 8, inner), F),
    )(first_weight, *others)


def project_kernel(each, blocks, x_ref, g_ref, wq_ref, wk_ref, wv_ref, wr_ref, wg_ref, s_ref, n_ref, p_ref, LT):
    step = pl.program_id(0)
    rows, width = x_ref.shape
    span = wq_ref.shape[1]

    @pl.when(step == 0)
    def _():
        x = x_ref[...].astype(F)
        scale = lax.rsqrt(jnp.sum(x * x, -1, keepdims=True) * (1.0 / width) + NORM_EPS)
        n_ref[...] = (x * scale * g_ref[...]).astype(LOW)
        LT[...] = jnp.zeros_like(LT)
        LT[: wr_ref.shape[0]] = nt(wr_ref[...], n_ref[...]).astype(LOW).astype(F)

    normed = n_ref[...]
    extra = s_ref.shape[1] - rows
    s_ref[0, rows:, :] = jnp.zeros((extra, 3 * span), LOW)

    @pl.when(step < blocks)
    def _():
        for i, w_ref in enumerate((wq_ref, wk_ref, wv_ref)):
            s_ref[0, :rows, span * i : span * i + span] = nn(normed, w_ref[...]).astype(LOW)
        r = lax.broadcasted_iota(jnp.int32, (extra, rows), 0)
        c = lax.broadcasted_iota(jnp.int32, (extra, rows), 1)
        pick = jnp.where((r < each) & (c == step * each + r), 1.0, 0.0)
        s_ref[0, rows:, :rows] = nn(pick, LT[...]).astype(LOW)
        p_ref[...] = nn(normed, wg_ref[...])

    @pl.when(step >= blocks)
    def _():
        s_ref[0, :rows, :] = jnp.zeros((rows, 3 * span), LOW)


def project(x, gain, wq, wk, wv, wr, wg, seqs, each, extra):
    rows, width = x.shape
    span = each * (width // wr.shape[0])
    blocks = width // span
    column = pl.BlockSpec((width, span), lambda s: (0, jnp.minimum(s, blocks - 1)))
    full = lambda *shape: pl.BlockSpec(shape, lambda s: (0,) * len(shape))
    sd = jax.ShapeDtypeStruct
    return pl.pallas_call(
        partial(project_kernel, each, blocks),
        grid=(seqs,),
        in_specs=[full(rows, width), full(1, width), column, column, column, full(*wr.shape), column],
        out_specs=[
            pl.BlockSpec((1, rows + extra, 3 * span), lambda s: (s, 0, 0)),
            full(rows, width),
            pl.BlockSpec((rows, span), lambda s: (0, jnp.minimum(s, blocks - 1))),
        ],
        out_shape=[sd((seqs, rows + extra, 3 * span), LOW), sd((rows, width), LOW), sd((rows, width), F)],
        scratch_shapes=[pltpu.VMEM((128, 128), F)],
        compiler_params=pltpu.CompilerParams(vmem_limit_bytes=60 * 1024 * 1024),
    )(x, gain[None], wq, wk, wv, wr, wg)


def tokens_kernel(each, blocks, x_ref, g_ref, m_ref, b_ref, d_ref, wq_ref, wk_ref, wv_ref, wr_ref, wg_ref, o_ref, ACC, LG):
    step = pl.program_id(0)
    rows, width = x_ref.shape
    span = wq_ref.shape[1]
    extra = b_ref.shape[1] - rows

    @pl.when(step == 0)
    def _():
        ACC[...] = jnp.zeros_like(ACC)
        LG[...] = jnp.zeros_like(LG)

    @pl.when(step < blocks)
    def _():
        total = nt(d_ref[...], wg_ref[...])
        for i, w_ref in enumerate((wq_ref, wk_ref, wv_ref)):
            total = total + nt(b_ref[0, :rows, span * i : span * i + span], w_ref[...])
        ACC[...] = ACC[...] + total
        r = lax.broadcasted_iota(jnp.int32, (rows, extra), 0)
        c = lax.broadcasted_iota(jnp.int32, (rows, extra), 1)
        place = jnp.where((c < each) & (r == step * each + c), 1.0, 0.0)
        LG[...] = LG[...] + nn(place, b_ref[0, rows:, :rows])

    @pl.when(step == pl.num_programs(0) - 1)
    def _():
        heads = wr_ref.shape[0]
        x = x_ref[...].astype(F)
        scale = lax.rsqrt(jnp.sum(x * x, -1, keepdims=True) * (1.0 / width) + NORM_EPS)
        grad = (ACC[...] + nn(LG[...].T[:, :heads], wr_ref[...])) * g_ref[...]
        along = jnp.sum(x * grad, -1, keepdims=True) * (1.0 / width)
        o_ref[...] = m_ref[...] + scale * (grad - x * (scale * scale * along))


def tokens_back(x, gain, middle_grad, back, gate_low, wq, wk, wv, wr, wg, each):
    rows, width = x.shape
    seqs, tall, lanes = back.shape
    span = lanes // 3
    blocks = width // span
    column = pl.BlockSpec((width, span), lambda s: (0, jnp.minimum(s, blocks - 1)))
    full = lambda *shape: pl.BlockSpec(shape, lambda s: (0,) * len(shape))
    return pl.pallas_call(
        partial(tokens_kernel, each, blocks),
        grid=(blocks,),
        in_specs=[
            full(rows, width), full(1, width), full(rows, width),
            pl.BlockSpec((1, tall, lanes), lambda s: (s, 0, 0)),
            pl.BlockSpec((rows, span), lambda s: (0, s)),
            column, column, column, full(*wr.shape), column,
        ],
        out_specs=full(rows, width),
        out_shape=jax.ShapeDtypeStruct((rows, width), F),
        scratch_shapes=[pltpu.VMEM((rows, width), F), pltpu.VMEM((128, 128), F)],
        compiler_params=pltpu.CompilerParams(vmem_limit_bytes=16 * 1024 * 1024),
    )(x, gain[None], middle_grad, back, gate_low, wq, wk, wv, wr, wg)


def feed_kernel(a_ref, b_ref, c_ref, g_ref, l_ref, d_ref):
    unit = g_ref.shape[1]
    g_ref[...] = a_ref[0, :unit].astype(F).T
    l_ref[...] = b_ref[0, :unit].astype(F).T
    half = unit // 2
    for i in range(2):
        d_ref[half * i : half * i + half] = c_ref[i, unit : unit + half].astype(F)


def feed_outputs(fed, inner_units):
    seqs, tall, width = fed.shape
    steps = seqs // 2
    unit = inner_units // steps
    sd = jax.ShapeDtypeStruct
    return pl.pallas_call(
        feed_kernel,
        grid=(steps,),
        in_specs=[
            pl.BlockSpec((1, tall, width), lambda i: (i, 0, 0)),
            pl.BlockSpec((1, tall, width), lambda i: (i + steps, 0, 0)),
            pl.BlockSpec((2, tall, width), lambda i: (i, 0, 0)),
        ],
        out_specs=[
            pl.BlockSpec((width, unit), lambda i: (0, i)),
            pl.BlockSpec((width, unit), lambda i: (0, i)),
            pl.BlockSpec((unit, width), lambda i: (i, 0)),
        ],
        out_shape=[sd((width, inner_units), F)] * 2 + [sd((inner_units, width), F)],
        compiler_params=pltpu.CompilerParams(vmem_limit_bytes=16 * 1024 * 1024),
    )(fed, fed, fed)


def swapped(array):
    seqs = lax.axis_size("seq")
    array = array.reshape(seqs, -1, array.shape[-1])
    return lax.all_to_all(array, "seq", split_axis=0, concat_axis=0, tiled=True)


def summed(parts):
    return jnp.sum(parts.astype(F), 0).astype(LOW)


def share_rows(every_normed, back_sent, state_g, vectors, fed_parts, early, aside, heads, local_heads, head, weights_in):
    seqs, tps = lax.axis_size("seq"), lax.axis_size("tp")
    width = every_normed.shape[1]
    lanes = back_sent.shape[2]
    rows = every_normed.shape[0] // seqs
    span = lanes // 3
    each = span // head
    first_g, first_bias_g, second_g, second_bias_g, gain_g, shift_g, bias_g = state_g
    inner = first_g.shape[1]
    fed = lax.all_gather(summed(fed_parts), "seq", axis=0, tiled=False)
    early = lax.all_gather(summed(swapped(early)), "seq", axis=0, tiled=True)
    for mask in reversed(masks_of("tp")):
        early = double(early, "tp", mask)
    early = early.reshape(2, width, width).astype(F)
    back = lax.all_to_all(back_sent, "seq", split_axis=0, concat_axis=0, tiled=True)
    qkv_g = back_sent[:, :rows].reshape(seqs * rows, lanes)
    logit_g = back_sent[:, rows : rows + each, :rows].transpose(1, 0, 2).reshape(each, seqs * rows)
    columns = jnp.einsum("ld,le->de", every_normed, qkv_g, preferred_element_type=F)
    rate_column = jnp.einsum("el,ld->ed", logit_g, every_normed, preferred_element_type=F)
    first_g = first_g.reshape(each, head, inner)
    second_g = second_g.reshape(each, head, inner)
    second_g = second_g - jnp.mean(second_g, 1, keepdims=True)
    second_bias_g, gain_g, shift_g = [a.reshape(each, head) for a in (second_bias_g, gain_g, shift_g)]
    second_bias_g = second_bias_g - jnp.mean(second_bias_g, 1, keepdims=True)
    bias_g = bias_g[0, :each]
    tail = jnp.concatenate(
        [second_bias_g, gain_g, shift_g, jnp.pad(bias_g[:, None], ((0, 0), (0, inner - 3 * head - 1)))], -1
    )
    states = jnp.concatenate(
        [
            jnp.stack([first_g, second_g], 1),
            jnp.stack([first_bias_g, tail], 1)[:, :, None],
            jnp.zeros((each, 2, 7, inner), F),
        ],
        2,
    )
    state_rows = states.size // lanes // tps
    rate_rows = rate_column.size // lanes // tps
    vectors = jnp.concatenate([vectors, jnp.zeros_like(vectors[:1])], 0)
    vector_rows = vectors.size // lanes // tps
    rest = jnp.concatenate(
        [rate_column.reshape(tps, rate_rows, lanes), vectors.reshape(tps, vector_rows, lanes)], 1
    )
    late = jnp.concatenate(
        [
            columns.reshape(tps, width // tps, lanes),
            states.reshape(tps, state_rows, lanes),
            jnp.pad(rest, ((0, 0), (0, 16 - rate_rows - vector_rows), (0, 0))),
        ],
        1,
    )
    late = lax.psum_scatter(late.astype(LOW), "tp", scatter_dimension=0, tiled=True)
    late = lax.all_gather(late, ("seq", "tp"), axis=0, tiled=True).reshape((seqs, tps) + late.shape[1:])
    weights = late[:, :, : width // tps].reshape(seqs, tps, width // tps, 3, span)
    weights = weights.transpose(3, 1, 2, 0, 4).reshape(3, width, seqs * span)[:, :, :width].astype(F)
    states = late[:, :, width // tps : width // tps + state_rows].reshape(seqs * each, 2, head + 8, inner)[:heads]
    states = lax.dynamic_slice_in_dim(states, lax.axis_index("tp") * local_heads, local_heads, 0).astype(F)
    rest = late[:, :, width // tps + state_rows :]
    rate_weight_grad = rest[:, :, :rate_rows].reshape(seqs * each, width)[:heads].T.astype(F)
    vectors = rest[:, :, rate_rows : rate_rows + vector_rows].reshape(seqs, 4, width)
    vectors = jnp.sum(vectors.astype(F), 0)
    grads = (weights[0], weights[1], weights[2], early[1])
    norm_gain_grad = jnp.sum(sum(g * w.astype(F) for g, w in zip(grads, weights_in)), -1)
    head_w = (states[:, 0, :head], jnp.swapaxes(states[:, 1, :head], 1, 2))
    return weights, head_w, states[:, :, head], rate_weight_grad, vectors, fed, back, early, aside, norm_gain_grad


def pack_kernel(head, me_ref, n_ref, x_ref, w_ref, wb_ref, u_ref, ub_ref, g_ref, s_ref, r_ref, v_ref, keep_ref, sent_ref, COL, UC, SMALL):
    seqs, _, lanes = x_ref.shape
    rows = n_ref.shape[0] // seqs
    width = n_ref.shape[1]
    here = width // 4
    normed = n_ref[...]
    COL[...] = tn(normed, x_ref[:, :rows].reshape(seqs * rows, lanes))
    rate = jnp.zeros((16, width), F)
    for s in range(seqs):
        logit = x_ref[s, rows : rows + 16, :rows]
        rate = rate + nn(logit, n_ref[rows * s : rows * s + rows])
    SMALL[...] = jnp.zeros_like(SMALL)
    for c in range(2):
        lane = slice(head * c, head * c + head)
        u = u_ref[lane]
        UC[lane] = u - jnp.sum(u, 0, keepdims=True) * (1.0 / head)
        ub = ub_ref[:, lane]
        ub = ub - jnp.sum(ub, 1, keepdims=True) * (1.0 / head)
        for i in range(2):
            SMALL[2 * c, i : i + 1] = wb_ref[c : c + 1, 128 * i : 128 * i + 128]
        SMALL[2 * c + 1, 0:1] = jnp.concatenate([ub, g_ref[:, lane]], 1)
        SMALL[2 * c + 1, 1:2] = jnp.concatenate([s_ref[:, lane], jnp.broadcast_to(r_ref[:, c : c + 1], (1, head))], 1)
    for t in range(4):
        for i in range(3):
            at = (t % 2) * 384 + 128 * i
            SMALL[t, 2 + i : 3 + i] = rate[t // 2 : t // 2 + 1, at : at + 128]
        for i in range(5):
            k = 5 * t + i
            if k < 18:
                SMALL[t, 5 + i : 6 + i] = v_ref[k // 6 : k // 6 + 1, (k % 6) * 128 : (k % 6) * 128 + 128]
    for place, o in enumerate((0, 2, 1, 3)):
        out = (keep_ref, sent_ref)[place // 2].at[place % 2]
        t = me_ref[0] ^ o
        out[:here] = COL[pl.ds(pl.multiple_of(t * here, 16), here)].astype(LOW)
        for n in range(9):
            c, k, half = n // 4, (n // 2) % 2, n % 2
            if n < 8:
                tile = (w_ref, UC)[k][pl.ds(pl.multiple_of(head * c + 16 * t, 16), 16), 128 * half : 128 * half + 128]
            else:
                tile = SMALL[t]
            row, lane = here + 16 * (n // 3), 128 * (n % 3)
            out[row : row + 16, lane : lane + 128] = tile.astype(LOW)


def last_kernel(seqs, each, heads, local_heads, me_ref, *refs):
    ours = lax.rem(pl.program_id(0), 2) == lax.rem(me_ref[0], 2)

    @pl.when(ours)
    def _():
        last_part(seqs, each, heads, local_heads, me_ref, refs[0], refs[1], *refs[4:])

    @pl.when(jnp.logical_not(ours))
    def _():
        last_part(seqs, each, heads, local_heads, me_ref, refs[2], refs[3], *refs[4:])


def last_part(seqs, each, heads, local_heads, me_ref, a_ref, b_ref, wq_ref, wk_ref, wv_ref, wg_ref,
              q_ref, k_ref, v_ref, n_ref, f_ref, s_ref, r_ref, out_ref, gate_ref, gate_n_ref, ST):
    t = pl.program_id(0)
    cut = a_ref.shape[2]
    lanes = a_ref.shape[3]
    span = lanes // 3
    below = q_ref.shape[0] - cut

    def spot(s):
        return s % 2, ((s >> 1) & 1) * 2 + (s >> 2)

    for s in range(seqs):
        if s * each >= heads:
            continue
        x, q = spot(s)
        for i, o_ref in enumerate((q_ref, k_ref, v_ref)):
            o_ref[:cut, span * s : span * s + span] = a_ref[0, 4 * x + q, :, span * i : span * i + span].astype(F)
            o_ref[cut:, span * s : span * s + span] = b_ref[x, 0, q, :below, span * i : span * i + span].astype(F)
    total = q_ref[...] * wq_ref[...].astype(F)
    for o_ref, w_ref in ((k_ref, wk_ref), (v_ref, wv_ref)):
        total = total + o_ref[...] * w_ref[...].astype(F)
    n_ref[...] = jnp.sum(total, -1, keepdims=True)

    def tile(x, q, n):
        row, lane = below + 16 * (n // 3), 128 * (n % 3)
        return b_ref[x, 0, q, row : row + 16, lane : lane + 128].astype(F)

    for i in range(local_heads):
        h = me_ref[0] * local_heads + i
        s = h // each
        upper = lax.rem(h, each) == 1
        x = lax.rem(s, 2)
        q = lax.rem(s // 2, 2) * 2 + s // 4
        for k in range(2):
            for j in range(2):
                ST[i, k, pl.ds(pl.multiple_of(16 * t, 16), 16), 128 * j : 128 * j + 128] = jnp.where(
                    upper, tile(x, q, 4 + k * 2 + j), tile(x, q, k * 2 + j)
                )
    for s in range(seqs):
        r_ref[0, s] = tile(*spot(s), 8)

    first = below + 48
    tall = out_ref.shape[0] // seqs

    def square(o_ref):
        for s in range(seqs):
            x, q = spot(s)
            for i in range(2):
                row = first + tall * i
                o_ref[tall * s : tall * s + tall, lanes * i : lanes * i + lanes] = b_ref[x, 0, q, row : row + tall].astype(F)

    @pl.when(t == 3)
    def _():
        for i in range(local_heads):
            f_ref[i] = ST[i, 0]
            s_ref[i] = ST[i, 1]

    @pl.when(t % 2 == 0)
    def _():
        square(out_ref)

    @pl.when(t % 2 == 1)
    def _():
        square(gate_ref)
        gate_n_ref[...] = jnp.sum(gate_ref[...] * wg_ref[...].astype(F), -1, keepdims=True)


def share_tiles(every_normed, back_sent, state_g, vectors, fed_parts, early, aside, heads, local_heads, head, weights_in):
    seqs, tps = lax.axis_size("seq"), lax.axis_size("tp")
    width = every_normed.shape[1]
    lanes = back_sent.shape[2]
    each = 2
    inner = state_g[0].shape[1]
    here = width // tps
    share = here + 48
    me = lax.axis_index("tp").astype(jnp.int32).reshape(1)
    sd = jax.ShapeDtypeStruct
    late, late_sent = pl.pallas_call(
        partial(pack_kernel, head),
        in_specs=[pl.BlockSpec(memory_space=pltpu.SMEM)] + [pl.BlockSpec(memory_space=pltpu.VMEM)] * 10,
        out_specs=[pl.BlockSpec(memory_space=pltpu.VMEM)] * 2,
        out_shape=[sd((2, share, lanes), LOW)] * 2,
        scratch_shapes=[
            pltpu.VMEM((width, lanes), F),
            pltpu.VMEM((each * head, inner), F),
            pltpu.VMEM((4, 16, 128), F),
        ],
        compiler_params=pltpu.CompilerParams(vmem_limit_bytes=20 * 1024 * 1024),
    )(me, every_normed, back_sent, *state_g, vectors)
    late = late.astype(F) + flip(late_sent, "tp", 1).astype(F)
    late = scatter_once(late, "tp", 2).astype(LOW)[0]
    early = summed(swapped(early))
    late = jnp.concatenate([late, early[:, :lanes], early[:, lanes:]], 0)
    share = late.shape[0]
    late = double(late, "seq", 4)
    late, fed = lax.optimization_barrier((late, summed(fed_parts)))
    fed = lax.all_gather(fed, "seq", axis=0, tiled=False)
    late = double(late, "seq", 2)
    back = lax.all_to_all(back_sent, "seq", split_axis=0, concat_axis=0, tiled=True)
    cut = 160
    part_a, part_b = late[:, :, :cut], late[:, :, cut:]
    part_a, part_b = double(part_a, "seq", 1), double(part_b, "tp", 2)
    part_a, part_b = double(part_a, "tp", 2), double(part_b, "seq", 1)
    part_a, part_b, fed, back, aside = lax.optimization_barrier((part_a, part_b, fed, back, aside))
    part_a = part_a.reshape(2, seqs, cut, lanes)
    part_b = part_b.reshape(2, 2, seqs // 2, share - cut, lanes)
    got_a, got_b = flip(part_a, "tp", 1), flip(part_b, "tp", 1)
    a_spec = pl.BlockSpec((1, seqs, cut, lanes), lambda t: (t // 2, 0, 0, 0))
    b_spec = pl.BlockSpec((2, 1, seqs // 2, share - cut, lanes), lambda t: (0, t // 2, 0, 0, 0))
    square = pl.BlockSpec((here, width), lambda t: (t, 0))
    taller = pl.BlockSpec((2 * here, width), lambda t: (t // 2, 0))
    *weights, norm_gain_grad, head_f, head_s, small, out_g, gate_g, gate_n = pl.pallas_call(
        partial(last_kernel, seqs, each, heads, local_heads),
        grid=(tps,),
        in_specs=[
            pl.BlockSpec(memory_space=pltpu.SMEM),
            a_spec, b_spec, a_spec, b_spec, square, square, square, taller,
        ],
        out_specs=[
            square, square, square,
            pl.BlockSpec((here, 1), lambda t: (t, 0)),
            pl.BlockSpec((local_heads, head, inner), lambda t: (0, 0, 0)),
            pl.BlockSpec((local_heads, head, inner), lambda t: (0, 0, 0)),
            pl.BlockSpec((1, seqs, 16, 128), lambda t: (t, 0, 0, 0)),
            taller, taller,
            pl.BlockSpec((2 * here, 1), lambda t: (t // 2, 0)),
        ],
        out_shape=[sd((width, width), F)] * 3
        + [sd((width, 1), F), sd((local_heads, head, inner), F), sd((local_heads, head, inner), F)]
        + [sd((tps, seqs, 16, 128), F)]
        + [sd((width, width), F)] * 2
        + [sd((width, 1), F)],
        scratch_shapes=[pltpu.VMEM((local_heads, 2, head, inner), F)],
        compiler_params=pltpu.CompilerParams(vmem_limit_bytes=48 * 1024 * 1024),
    )(me, part_a, part_b, got_a, got_b, *weights_in)
    norm_gain_grad = norm_gain_grad + gate_n
    head_t = small[:, :, :2].transpose(1, 0, 2, 3).reshape(seqs * each, 2, inner)
    head_t = lax.dynamic_slice_in_dim(head_t, me[0] * local_heads, local_heads, 0)
    rate_weight_grad = small[:, :, 2:5].transpose(1, 0, 2, 3).reshape(seqs * each, width)[:heads].T
    vectors = jnp.sum(small[:, :, 5:10], 1).reshape(-1)[: 3 * width].reshape(3, width)
    return weights, (head_f, jnp.swapaxes(head_s, 1, 2)), head_t, rate_weight_grad, vectors, fed, back, (out_g, gate_g), aside, norm_gain_grad[:, 0]


def on_device(
    tokens, norm_gain, query_weight, key_weight, value_weight, rate_weight, rate_bias,
    first_weight, first_bias, second_weight, second_bias, inner_gain, inner_bias,
    branch_gate, output_weight, post_gain, post_bias, feed_gain, feed_gate, feed_linear,
    feed_down, cotangent,
):
    seqs = lax.axis_size("seq")
    rank = lax.axis_index("seq")
    heads = rate_weight.shape[1]
    local_heads, head, inner = first_weight.shape
    rows = tokens.shape[1]
    width = tokens.shape[2]
    each = -(-heads // seqs)
    span = each * head
    length = seqs * rows
    extra = -(-each // 16) * 16

    def to_chains(array):
        padded = jnp.pad(array, ((0, 0), (0, seqs * span - array.shape[1])))
        return padded.reshape(rows, seqs, span).transpose(1, 0, 2)

    def from_chains(array):
        return array.transpose(1, 0, 2).reshape(rows, seqs * span)[:, :width]

    def swap(array):
        return lax.all_to_all(array, "seq", split_axis=0, concat_axis=0, tiled=True)

    packed = pack_params(
        first_weight, jnp.swapaxes(second_weight, 1, 2), first_bias, second_bias, inner_gain, inner_bias, rate_bias[None]
    )
    every = lax.all_gather(packed, "tp", axis=0, tiled=True)
    own = lax.dynamic_slice_in_dim(every, jnp.minimum(rank * each, heads - each), each, 0)

    residual = tokens[0].astype(F)
    normed_val, norm_pull = jax.vjp(root_norm, residual, norm_gain)
    down_grad = cotangent[0]
    grad_out = down_grad.astype(F)
    every_grad = gather_near(down_grad, "tp")
    if span % 128 == 0 and width % span == 0 and rows == 128:
        sent, normed, gate_pre = project(
            tokens[0], norm_gain, query_weight, key_weight, value_weight, rate_weight.T, branch_gate, seqs, each, extra
        )
    else:
        normed = normed_val.astype(LOW)
        query_tok = matmul(normed, query_weight).astype(LOW)
        keys_tok = matmul(normed, key_weight).astype(LOW)
        values_tok = matmul(normed, value_weight).astype(LOW)
        logits_tok = matmul(normed, rate_weight).astype(LOW)
        gate_pre = matmul(normed, branch_gate)
        logit_rows = jnp.pad(logits_tok.T, ((0, seqs * each - heads), (0, 0))).reshape(seqs, each, rows)
        logit_rows = jnp.pad(logit_rows, ((0, 0), (0, extra - each), (0, 3 * span - rows)))
        sent = [to_chains(query_tok), to_chains(keys_tok), to_chains(values_tok)]
        sent = jnp.concatenate([jnp.concatenate(sent, -1), logit_rows], 1)
    got = swap(sent)

    every_normed = lax.all_gather(normed, "seq", axis=0, tiled=True)
    outs, *kept = fwd_scan(got, own)
    outs, every_normed, every_grad = lax.optimization_barrier((outs, every_normed, every_grad))
    mixed_tok = from_chains(swap(outs.reshape(seqs, rows, span))).astype(F)

    branch_val, branch_pull = jax.vjp(gated_branch, mixed_tok, gate_pre, post_gain, post_bias)
    branch_in = branch_val.astype(LOW)
    middle = residual + matmul(branch_in, output_weight)
    feed_val, feed_pull = jax.vjp(root_norm, middle, feed_gain)
    feed_in = feed_val.astype(LOW)
    every_in = gather_near(feed_in, "tp")
    gate_val = matmul(every_in, feed_gate)
    linear_val = matmul(every_in, feed_linear)
    act_val, act_pull = jax.vjp(swish_product, gate_val, linear_val)
    hidden = act_val.astype(LOW)

    hidden_grad = jnp.einsum("td,fd->tf", every_grad, feed_down, preferred_element_type=F)
    gate_grad, linear_grad = act_pull(hidden_grad)
    gate_low = gate_grad.astype(LOW)
    linear_low = linear_grad.astype(LOW)
    input_part = jnp.einsum("tf,df->td", gate_low, feed_gate, preferred_element_type=F) + jnp.einsum(
        "tf,df->td", linear_low, feed_linear, preferred_element_type=F
    )
    feed_down_grad = jnp.einsum("tf,td->fd", hidden, every_grad, preferred_element_type=F)
    both_low = jnp.concatenate([gate_low, linear_low], 1)
    feed_both_grad = jnp.einsum("tf,td->fd", both_low, every_in, preferred_element_type=F)
    fed_parts = jnp.concatenate(
        [
            feed_both_grad.astype(LOW).reshape(seqs, -1, width),
            feed_down_grad.astype(LOW).reshape(seqs, -1, width),
        ],
        1,
    )
    feed_in_grad = input_part
    for mask in masks_of("tp"):
        half = feed_in_grad.shape[0] // 2
        arrived = flip(feed_in_grad[half:].astype(LOW), "tp", mask)
        if mask == masks_of("tp")[-1]:
            arrived, fed_parts = lax.optimization_barrier((arrived, fed_parts))
        feed_in_grad = feed_in_grad[:half].astype(F) + arrived.astype(F)
    middle_part, feed_gain_grad = feed_pull(feed_in_grad)
    middle_grad = grad_out + middle_part
    out_low = middle_grad.astype(LOW)
    branch_grad = jnp.einsum("te,de->td", out_low, output_weight, preferred_element_type=F)
    mixed_grad, gate_pre_grad, post_gain_grad, post_bias_grad = branch_pull(branch_grad)
    out_grad_c = swap(to_chains(mixed_grad.astype(LOW))).reshape(length, span)

    second_part = matmul(hidden, feed_down).astype(LOW)
    second_part, out_grad_c = lax.optimization_barrier((second_part, out_grad_c))
    second_out = scatter_near(second_part, "tp")
    result = (middle + second_out).astype(LOW)[None]

    gate_low_pre = gate_pre_grad.astype(LOW)
    out_low, gate_low_pre, out_grad_c = lax.optimization_barrier((out_low, gate_low_pre, out_grad_c))
    tps = lax.axis_size("tp")
    lefts = jnp.stack([branch_in, normed])
    rights = jnp.stack([out_low, gate_low_pre])
    part_rows = 2 * width // tps
    orders = [0]
    for mask in reversed(masks_of("tp")):
        orders = orders + [o + mask for o in orders]
    parts = []
    for o in orders:
        owner = lax.axis_index("tp") ^ o
        which, place = owner % 2, owner // 2
        left = lax.dynamic_slice(lefts, (which, 0, place * part_rows), (1, rows, part_rows))
        right = lax.dynamic_index_in_dim(rights, which, 0, keepdims=True)
        parts.append((left, right))
    half = tps // 2

    def products(chosen):
        left = jnp.concatenate([p[0] for p in chosen], 0)
        right = jnp.concatenate([p[1] for p in chosen], 0)
        return jnp.einsum("jtd,jte->jde", left, right, preferred_element_type=F)

    early_sent = products(parts[half:]).astype(LOW)
    early = products(parts[:half]) + flip(early_sent, "tp", 1).astype(F)
    fed_parts, early, out_grad_c = lax.optimization_barrier((fed_parts, early.astype(LOW), out_grad_c))
    fed_parts = swap(fed_parts)
    for mask in masks_of("tp")[1:]:
        early = scatter_once(early, "tp", mask)

    back_sent, *state_g = bwd_scan(got, own, out_grad_c, *kept)
    early, fed_parts, back_sent = lax.optimization_barrier((early.astype(LOW), fed_parts, back_sent))
    vectors = jnp.stack([post_gain_grad, post_bias_grad, feed_gain_grad])
    share = share_tiles if each == 2 and tps == 4 and seqs == 8 else share_rows
    weights, head_w, head_t, rate_weight_grad, vectors, fed, back, early, result, norm_gain_grad = share(
        every_normed, back_sent, state_g, vectors, fed_parts, early, result, heads, local_heads, head,
        (query_weight, key_weight, value_weight, branch_gate),
    )
    if span % 128 == 0 and width % span == 0 and rows == 128:
        tokens_grad = tokens_back(
            tokens[0], norm_gain, middle_grad, back, gate_low_pre,
            query_weight, key_weight, value_weight, rate_weight.T, branch_gate, each,
        )[None]
    else:
        query_low = from_chains(back[:, :rows, :span])
        keys_low = from_chains(back[:, :rows, span : 2 * span])
        values_low = from_chains(back[:, :rows, 2 * span :])
        logit_low = back[:, rows : rows + each, :rows].reshape(seqs * each, rows)[:heads].T

        normed_grad = (
            jnp.einsum("te,de->td", query_low, query_weight, preferred_element_type=F)
            + jnp.einsum("te,de->td", keys_low, key_weight, preferred_element_type=F)
            + jnp.einsum("te,de->td", values_low, value_weight, preferred_element_type=F)
            + jnp.einsum("te,de->td", logit_low, rate_weight, preferred_element_type=F)
            + jnp.einsum("te,de->td", gate_low_pre, branch_gate, preferred_element_type=F)
        )
        residual_part, unused = norm_pull(normed_grad)
        tokens_grad = (middle_grad + residual_part)[None]
    inner_units = feed_gate.shape[1]
    if 2 * inner_units // seqs % 128 == 0:
        fed_grads = feed_outputs(fed, inner_units)
    else:
        both = fed[:, : 2 * inner_units // seqs].reshape(2, inner_units, width).astype(F)
        down = fed[:, 2 * inner_units // seqs : 3 * inner_units // seqs].reshape(inner_units, width).astype(F)
        fed_grads = (both[0].T, both[1].T, down)
    norm_gain_grad = norm_gain_grad + jnp.sum(rate_weight_grad * rate_weight.astype(F), -1)
    norm_gain_grad = norm_gain_grad / norm_gain
    tail_sum = head_t[:, 1]
    return (
        result,
        tokens_grad,
        norm_gain_grad,
        weights[0],
        weights[1],
        weights[2],
        rate_weight_grad,
        tail_sum[:, 3 * head],
        head_w[0],
        head_t[:, 0],
        head_w[1],
        tail_sum[:, :head],
        tail_sum[:, head : 2 * head],
        tail_sum[:, 2 * head : 3 * head],
        early[1],
        early[0],
        vectors[0],
        vectors[1],
        vectors[2],
        *fed_grads,
    )


def solution(mesh):
    in_specs = (
        P("tp", "seq", None),
        P(),
        P(),
        P(),
        P(),
        P(),
        P("tp"),
        P("tp", None, None),
        P("tp", None),
        P("tp", None, None),
        P("tp", None),
        P("tp", None),
        P("tp", None),
        P(),
        P(),
        P(),
        P(),
        P(),
        P(None, "tp"),
        P(None, "tp"),
        P("tp", None),
        P("tp", "seq", None),
    )
    out_specs = (
        P("tp", "seq", None),
        P("tp", "seq", None),
        P(),
        P(),
        P(),
        P(),
        P(),
        P("tp"),
        P("tp", None, None),
        P("tp", None),
        P("tp", None, None),
        P("tp", None),
        P("tp", None),
        P("tp", None),
        P(),
        P(),
        P(),
        P(),
        P(),
        P(None, "tp"),
        P(None, "tp"),
        P("tp", None),
    )
    return jax.shard_map(
        on_device, mesh=mesh, in_specs=in_specs, out_specs=out_specs, check_vma=False
    )
```

```python
from functools import partial

import jax
import jax.numpy as jnp
from jax import lax
from jax.sharding import PartitionSpec as P
from jax.experimental import pallas as pl
from jax.experimental.pallas import tpu as pltpu
from itertools import chain
C0=0.7978845608028654
C1=0.044715
EPS=1e-6
RATE_SCALE=0.25
B=16
CH=128
NB=CH//B
LOW=jnp.bfloat16
F=jnp.float32
def nn(a,b): return lax.dot_general(a.astype(LOW),b.astype(LOW),(((1,),(0,)),((),())),preferred_element_type=F)
def nt(a,b): return lax.dot_general(a.astype(LOW),b.astype(LOW),(((1,),(1,)),((),())),preferred_element_type=F)
def tn(a,b): return lax.dot_general(a.astype(LOW),b.astype(LOW),(((0,),(0,)),((),())),preferred_element_type=F)
def gelu1(z):
    return z*(0.5+0.5*jnp.tanh(z*(C0+(C0*C1)*(z*z))))
def gelu2(z):
    z2=z*z
    t=jnp.tanh(z*(C0+(C0*C1)*z2))
    h=0.5+0.5*t
    x=z*h
    return x,h+x*(1-t)*(C0+(3*C0*C1)*z2)
def gelu3(z):
    z2=z*z
    t=jnp.tanh(z*(C0+(C0*C1)*z2))
    u1=C0+(3*C0*C1)*z2
    h=0.5+0.5*t
    h1=h*(1-t)*u1
    x=z*h
    return x,h+z*h1,2*h1+z*(h*(1-t)*(6*C0*C1)*z-2*t*u1*h1)
def lane_masks(C,H,R):
    lane=lax.broadcasted_iota(jnp.int32,(R,C*H),1)
    return [(lane>=H*c)&(lane<H*c+H) for c in range(C)]
def expand(C,x,masks):
    if C==1: return x
    zero=jnp.zeros((B,x.shape[1]),x.dtype)
    return jnp.concatenate([jnp.where(masks[c],x[B*j:B*j+B],zero) for j in range(x.shape[0]//B) for c in range(C)],0)
def collapse(C,x,masks):
    if C==1: return x
    rows=[]
    for j in range(x.shape[0]//(B*C)):
        y=x[B*C*j:B*C*j+B]
        for c in range(1,C): y=jnp.where(masks[c],x[B*(C*j+c):B*(C*j+c)+B],y)
        rows.append(y)
    return jnp.concatenate(rows,0) if len(rows)>1 else rows[0]
def tile_rows(C,x,n):
    t=jnp.concatenate([jnp.broadcast_to(x[c:c+1],(B,x.shape[1])) for c in range(C)],0)
    return jnp.concatenate([t]*n,0) if n>1 else t
def fill_masks(C,TRI,BLK,back):
    n=CH*C
    r=lax.broadcasted_iota(jnp.int32,(n,n),0); c=lax.broadcasted_iota(jnp.int32,(n,n),1)
    rs,cs=r//(B*C),c//(B*C)
    same=((r//B)%C)==((c//B)%C)
    tri=same&((cs<rs)|((cs==rs)&((c%B)<=(r%B))))
    TRI[...]=jnp.where(tri,1.0,0.0)
    BLK[...]=jnp.where(same&(cs<rs),1.0,0.0)
    if back is not None: back[...]=jnp.where(same&(cs>rs),1.0,0.0)
def ones_of(C,H):
    r=lax.broadcasted_iota(jnp.int32,(C*H,C*H),0); c=lax.broadcasted_iota(jnp.int32,(C*H,C*H),1)
    return jnp.where((r//H)==(c//H),1.0/H,0.0).astype(LOW)
def sums_of(C):
    r=lax.broadcasted_iota(jnp.int32,(C,CH*C),0); c=lax.broadcasted_iota(jnp.int32,(C,CH*C),1)
    return jnp.where(((c//B)%C)==r,1.0,0.0).astype(LOW)
def stack_col(C,r):
    return jnp.concatenate([r[B*j:B*j+B,c:c+1] for j in range(r.shape[0]//B) for c in range(C)],0)
def pair_cols(C,H,r,masks):
    y=jnp.broadcast_to(r[:,0:1],(r.shape[0],C*H))
    for c in range(1,C): y=jnp.where(masks[c],r[:,c:c+1],y)
    return y

def rates(C,x_ref,own_ref,H):
    rows=[x_ref[0,CH+c:CH+c+1,:CH].astype(F)+own_ref[c,2*H+1:2*H+2,3*H:3*H+1] for c in range(C)]
    rows=jnp.concatenate(rows+[jnp.zeros((CH-C,CH),F)],0)
    return (jax.nn.sigmoid(rows)*(RATE_SCALE/H)).T

def pair_row(C,H,own_ref,k):
    return jnp.concatenate([own_ref[c,2*H+1:2*H+2,k*H:k*H+H] for c in range(C)],1)

def mask_stack(C,H):
    r=lax.broadcasted_iota(jnp.int32,(B*C,C*H),0)//B; c=lax.broadcasted_iota(jnp.int32,(B*C,C*H),1)//H
    return r==c

def fwd_pre(C,H,x,own_ref,BLK,gam,bet,S):
    W=C*H
    m16=lane_masks(C,H,B); m128=lane_masks(C,H,CH)
    K=x[0,:CH,W:2*W]
    Kst=expand(C,K,m16)
    S["KST"][...]=Kst; S["QST"][...]=expand(C,x[0,:CH,:W],m16)
    S["T"][...]=(bet+K.astype(F)-x[0,:CH,2*W:].astype(F))*gam
    yield
    R=rates(C,x,own_ref,H)
    S["R"][...]=R
    S["RP"][...]=pair_cols(C,H,R,m128)
    yield
    S["KK"][...]=((nt(Kst,Kst)+1.0)*BLK[...]).astype(LOW)
    tst=expand(C,S["T"][...],m16)
    S["TST"][...]=tst
    S["CT"][...]=nn(tst,jnp.full((W,W),1.0/H,LOW))
    yield

def fwd_steps(C,H,S,W1,B1,U,B2,gam,z1_ref,p_ref,zc_ref,us_ref,w1s_ref,o,side,times):
    W=C*H; SB=B*C; TALL=C*CH
    m16=lane_masks(C,H,B)
    ones=ones_of(C,H)
    g2=gam*gam
    Kst=S["KST"][...]
    w1b=W1[...].astype(LOW); w1s_ref[o]=w1b
    S["W1"][...]=w1b; S["B1"][...]=B1[...]; S["B2"][...]=B2[...]
    b1r=tile_rows(C,B1[...],1)
    uf=U[...]; ub=uf.astype(LOW); S["U"][...]=ub
    b2=B2[...]
    S["BASE"][...]=nn(Kst,w1b)
    g2m=jnp.concatenate([jnp.broadcast_to(jnp.sum(jnp.where(m16[c][:1],g2,0.0),1,keepdims=True)*(1.0/H),(B,W)) for c in range(C)],0)
    mst=mask_stack(C,H)
    full=jnp.full((W,W),1.0/H,LOW)
    I=W1.shape[1]
    wide=lambda v: jnp.concatenate([v]*(I//W),1)
    for j in range(NB):
        sl=slice(B*j,B*j+B); st=slice(SB*j,SB*j+SB)
        z1=S["BASE"][st]+b1r
        if j>0: z1=z1-nn(S["KK"][st,:SB*j],S["S1"][:SB*j])
        x2,g1=gelu2(z1)
        x2b=x2.astype(LOW)
        t=S["TST"][st]; ct=S["CT"][st]; rr=stack_col(C,S["R"][sl])
        tU=nn(t,ub)
        zc=jnp.where(mst,nt(x2b,ub)+b2,0.0)
        zz=zc*zc; zg=zc*g2
        AB=nn(jnp.concatenate([zg,zc],0),ub)
        mm=nn(jnp.concatenate([zc,zz,zg,zz*g2,zc*t],0),full)
        mu=mm[0:SB]; mzz=mm[SB:2*SB]; mzg=mm[2*SB:3*SB]; mzzg=mm[3*SB:4*SB]; mzt=mm[4*SB:]
        s=lax.rsqrt(mzz-mu*mu+EPS)
        m1=s*(mzg-mu*g2m)+ct
        m2=s*(s*(mzzg-2.0*mu*mzg+mu*mu*g2m)+mzt-mu*ct)
        ss=s*s
        P=wide(ss)*(AB[:SB]-wide(m2)*AB[SB:])+wide(s)*tU
        s1=(P*(g1*rr)).astype(LOW)
        d2=ss*(zg-m2*zc)+s*t+jnp.where(mst,ss*mu*(m2-g2)-s*m1,0.0)
        s2=d2*rr
        s2b=s2.astype(LOW)
        zc=collapse(C,zc-mu,m16)
        S["S1"][st]=s1; S["S2"][st]=s2b; S["X2"][st]=x2b
        z1_ref[TALL*o+SB*j:TALL*o+SB*j+SB]=z1; p_ref[TALL*o+SB*j:TALL*o+SB*j+SB]=P
        zc_ref[CH*o+B*j:CH*o+B*j+B]=zc
        us_ref[o,j]=ub
        uf=uf-tn(s2b,x2b); ub=uf.astype(LOW)
        b2=b2-jnp.sum(s2,0,keepdims=True)
        for _ in range(times): next(side,None)
    U[...]=uf; B2[...]=b2
    S1v=S["S1"][...]
    W1[...]=W1[...]-tn(Kst,S1v)
    B1[...]=B1[...]-nn(sums_of(C),S1v)

def fwd_query(C,H,S,x,TRI,gam,bet,o_ref,z1q_ref,zq_ref,o):
    W=C*H; TALL=C*CH
    m16=lane_masks(C,H,B)
    ones=ones_of(C,H)
    A1=((nt(S["QST"][...],S["KST"][...])+1.0)*TRI[...]).astype(LOW)
    yield
    z1q=nn(S["QST"][...],S["W1"][...])+tile_rows(C,S["B1"][...],NB)-nn(A1,S["S1"][...])
    z1q_ref[TALL*o:TALL*o+TALL]=z1q
    x2q=gelu1(z1q).astype(LOW)
    yield
    A2=((nt(x2q,S["X2"][...])+1.0)*TRI[...]).astype(LOW)
    yield
    zq=collapse(C,nt(x2q,S["U"][...])-nn(A2,S["S2"][...]),m16)+S["B2"][...]
    zq=zq-nn(zq,ones)
    zq_ref[CH*o:CH*o+CH]=zq
    yield
    yq=zq*lax.rsqrt(nn(zq*zq,ones)+EPS)
    o_ref[CH*o:CH*o+CH]=(x[0,:CH,:W].astype(F)+yq*gam+bet).astype(LOW)
    yield

FSLOT=("TST","KST","QST","T","R","RP","KK","CT","W1","B1","U","B2","BASE","S1","S2","X2")

def fwd_kernel(C,H,xa_ref,xb_ref,own_ref,o_ref,z1_ref,p_ref,zc_ref,z1q_ref,zq_ref,us_ref,w1s_ref,W1,B1,U,B2,TRI,BLK,*slots):
    k=len(FSLOT)
    even=dict(zip(FSLOT,slots[:k])); odd=dict(zip(FSLOT,slots[k:]))
    gam=pair_row(C,H,own_ref,1); bet=pair_row(C,H,own_ref,2)
    @pl.when(pl.program_id(0)==0)
    def _():
        for c in range(C):
            W1[H*c:H*c+H]=own_ref[c,:H]
            u=own_ref[c,H:2*H]
            U[H*c:H*c+H]=u-jnp.sum(u,0,keepdims=True)*(1.0/H)
            B1[c:c+1]=own_ref[c,2*H:2*H+1]
        raw=[own_ref[c,2*H+1:2*H+2,:H] for c in range(C)]
        B2[...]=jnp.concatenate([v-jnp.sum(v,1,keepdims=True)*(1.0/H) for v in raw],1)
        fill_masks(C,TRI,BLK,None)
    for _ in fwd_pre(C,H,xa_ref,own_ref,BLK,gam,bet,even): pass
    side=fwd_pre(C,H,xb_ref,own_ref,BLK,gam,bet,odd)
    fwd_steps(C,H,even,W1,B1,U,B2,gam,z1_ref,p_ref,zc_ref,us_ref,w1s_ref,0,side,1)
    for _ in side: pass
    side=fwd_query(C,H,even,xa_ref,TRI,gam,bet,o_ref,z1q_ref,zq_ref,0)
    fwd_steps(C,H,odd,W1,B1,U,B2,gam,z1_ref,p_ref,zc_ref,us_ref,w1s_ref,1,side,1)
    for _ in side: pass
    for _ in fwd_query(C,H,odd,xb_ref,TRI,gam,bet,o_ref,z1q_ref,zq_ref,1): pass

def fwd_scan(x,own):
    n,tall,W=x.shape
    W//=3
    C=own.shape[0]; I=own.shape[2]; H=W//C; L=n*CH; m=C*CH
    rows=lambda k,w: pl.BlockSpec((2*k,w),lambda i:(i,0))
    sd=jax.ShapeDtypeStruct
    V=pltpu.VMEM
    kinds=dict(KST=V((m,W),LOW),QST=V((m,W),LOW),T=V((CH,W),F),R=V((CH,CH),F),RP=V((CH,W),F),KK=V((m,m),LOW),CT=V((m,W),F),TST=V((m,W),F),W1=V((W,I),LOW),
        B1=V((C,I),F),U=V((W,I),LOW),B2=V((1,W),F),BASE=V((m,I),F),S1=V((m,I),LOW),S2=V((m,W),LOW),X2=V((m,I),LOW))
    return pl.pallas_call(partial(fwd_kernel,C,H),grid=(n//2,),
        in_specs=[pl.BlockSpec((1,tall,3*W),lambda i:(2*i,0,0)),pl.BlockSpec((1,tall,3*W),lambda i:(2*i+1,0,0)),pl.BlockSpec(own.shape,lambda i:(0,0,0))],
        out_specs=[rows(CH,W),rows(m,I),rows(m,I),rows(CH,W),rows(m,I),rows(CH,W),
            pl.BlockSpec((2,NB,W,I),lambda i:(i,0,0,0)),pl.BlockSpec((2,W,I),lambda i:(i,0,0))],
        out_shape=[sd((L,W),LOW),sd((C*L,I),F),sd((C*L,I),F),sd((L,W),F),sd((C*L,I),F),sd((L,W),F),sd((n,NB,W,I),LOW),sd((n,W,I),LOW)],
        scratch_shapes=[V((W,I),F),V((C,I),F),V((W,I),F),V((1,W),F),V((m,m),F),V((m,m),F)]+[kinds[name] for name in FSLOT]*2,
        compiler_params=pltpu.CompilerParams(vmem_limit_bytes=48*1024*1024),
    )(x,x,own)

SLOT=("BASE","DX2","X2","RG1","G1","RPG2","DS2Q","KK","YB","GB","DB","SB","M2B","RED","S2E","S1B","X2Q","DZQ","DZ1Q","DKQ","DQ","KST","QST","T0","RP","PG1","R")

def slot_shapes(C,W,I):
    m=C*CH
    V=pltpu.VMEM
    wide,pair,tall=V((m,I),F),V((CH,W),F),V((m,W),LOW)
    kinds=dict(BASE=wide,DX2=wide,X2=V((m,I),LOW),RG1=wide,G1=wide,RPG2=wide,DS2Q=pair,KK=V((m,m),LOW),YB=pair,GB=pair,DB=pair,SB=pair,M2B=pair,
        RED=V((4*CH,W),F),S2E=tall,S1B=V((m,I),LOW),X2Q=V((m,I),LOW),DZQ=tall,DZ1Q=V((m,I),LOW),DKQ=V((m,W),F),DQ=V((CH,W),LOW),KST=tall,QST=tall,
        T0=pair,RP=pair,PG1=wide,R=V((CH,CH),F))
    return [kinds[name] for name in SLOT]

def bwd_pre(C,H,ins,own_ref,S,TRI,BLKT,gam,bet,dgam_ref,dbet_ref,factor):
    x_ref,do_ref,z1_ref,p_ref,zc_ref,z1q_ref,zq_ref,us_ref,w1s_ref=ins
    W=C*H
    m16=lane_masks(C,H,B); m128=lane_masks(C,H,CH)
    ones=ones_of(C,H)
    g2=gam*gam
    K=x_ref[0,:CH,W:2*W]
    Kst=expand(C,K,m16); Qst=expand(C,x_ref[0,:CH,:W],m16)
    S["KST"][...]=Kst; S["QST"][...]=Qst
    R=rates(C,x_ref,own_ref,H)
    S["R"][...]=R
    RP=pair_cols(C,H,R,m128)
    S["RP"][...]=RP
    dO=do_ref[...].astype(F)
    zq=zq_ref[...]; sq=lax.rsqrt(nn(zq*zq,ones)+EPS); yq=zq*sq
    dyq=dO*gam
    rq=nn(jnp.concatenate([dyq,dyq*yq],0),ones)
    dzq=sq*(dyq-rq[:CH]-yq*rq[CH:])
    dzqb=expand(C,dzq.astype(LOW),m16)
    S["DZQ"][...]=dzqb
    dgam_ref[...]=dgam_ref[...]+factor*jnp.sum(dO*yq,0,keepdims=True)
    dbet_ref[...]=dbet_ref[...]+factor*jnp.sum(dO,0,keepdims=True)
    yield
    zc=zc_ref[...]
    s=lax.rsqrt(nn(zc*zc,ones)+EPS)
    y=zc*s
    t0=bet+K.astype(F)-x_ref[0,:CH,2*W:].astype(F)
    G=y*g2+t0*gam
    red=nn(jnp.concatenate([G,G*y,g2*y,g2*y*y],0),ones)
    m1=red[:CH]; m2=red[CH:2*CH]
    d2=s*(G-m1-y*m2)
    s2=expand(C,(d2*RP).astype(LOW),m16)
    S["YB"][...]=y; S["GB"][...]=G; S["DB"][...]=d2; S["SB"][...]=s; S["M2B"][...]=m2; S["RED"][...]=red; S["S2E"][...]=s2; S["T0"][...]=t0
    yield
    x2,g1,gg2=gelu3(z1_ref[...]); x2=x2.astype(LOW)
    P=p_ref[...]
    RS=stack_col(C,R)
    rg1=RS*g1
    s1=(P*rg1).astype(LOW)
    S["X2"][...]=x2; S["G1"][...]=g1; S["RG1"][...]=rg1; S["RPG2"][...]=RS*(P*gg2); S["PG1"][...]=P*g1; S["S1B"][...]=s1
    yield
    x2q,g1q=gelu2(z1q_ref[...]); x2q=x2q.astype(LOW)
    S["X2Q"][...]=x2q
    A2=((nt(x2q,S["X2"][...])+1.0)*TRI[...]).astype(LOW)
    dA2=(nt(dzqb,s2)*TRI[...]).astype(LOW)
    yield
    dx2q=nn(dzqb,us_ref[0,0])-nn(dA2,S["X2"][...])
    S["DX2"][...]=-tn(dA2,x2q)
    S["DS2Q"][...]=-collapse(C,tn(A2,dzqb),m16)
    dz1qb=(dx2q*g1q).astype(LOW)
    S["DZ1Q"][...]=dz1qb
    yield
    A1=((nt(Qst,Kst)+1.0)*TRI[...]).astype(LOW)
    dA1=(nt(dz1qb,S["S1B"][...])*TRI[...]).astype(LOW)
    S["KK"][...]=((nt(Kst,Kst)+1.0)*BLKT[...]).astype(LOW)
    yield
    S["DQ"][...]=(dO+collapse(C,nt(dz1qb,w1s_ref[0])-nn(dA1,Kst),m16)).astype(LOW)
    S["DKQ"][...]=tn(dA1,Qst)
    S["BASE"][...]=-tn(A1,dz1qb)
    yield

def bwd_steps(C,H,S,us_ref,u,w1,H1,h1,HU,h2,BLK,gam,bet,dgam_ref,dbet_ref,DZ1,DS1,DS2,DG,dx_ref,db_ref,o,side):
    W=C*H; SB=B*C
    m16=lane_masks(C,H,B); m128=lane_masks(C,H,CH)
    ones=ones_of(C,H); sums=sums_of(C)
    g2=gam*gam
    Kst=S["KST"][...]
    h1b=H1[...].astype(LOW)
    S["BASE"][...]=S["BASE"][...]-nn(Kst,h1b)-tile_rows(C,h1[...],NB)
    dk=nt(S["S1B"][...],h1b)+S["DKQ"][...]
    g2m=nn(jnp.broadcast_to(g2,(8,W)),ones)[0:1]
    hu=HU[...]; hh2=h2[...]
    for j in reversed(range(NB)):
        sl=slice(B*j,B*j+B); st=slice(SB*j,SB*j+SB)
        ub=us_ref[u,j]
        rr=S["RP"][sl]
        hub=hu.astype(LOW)
        x2j=S["X2"][st]
        ds1=S["BASE"][st]
        if j<NB-1: ds1=ds1-nn(S["KK"][st,SB*j+SB:],DZ1[SB*j+SB:])
        ds2=S["DS2Q"][sl]-collapse(C,nt(x2j,hub),m16)-hh2
        dx2=S["DX2"][st]-nn(S["S2E"][st],hub)
        dPb=(ds1*S["RG1"][st]).astype(LOW)
        e=rr*ds2+collapse(C,nt(dPb,ub),m16)
        s=S["SB"][sl]; m2=S["M2B"][sl]; y=S["YB"][sl]; g_=S["GB"][sl]; d2=S["DB"][sl]
        m1=S["RED"][sl]; gy=S["RED"][2*CH+B*j:2*CH+B*j+B]; gyy=S["RED"][3*CH+B*j:3*CH+B*j+B]
        ge=g2*e
        mm=nn(jnp.concatenate([e,e*y,e*d2,ge,ge*y],0),ones)
        a=mm[0:B]; b=mm[B:2*B]; cc=mm[2*B:3*B]; mge=mm[3*B:4*B]; mgey=mm[4*B:]
        dG=s*(e-a-y*b)
        mdY=s*(mge-a*g2m-b*gy-m2*a-b*m1)
        mdYY=s*(mgey-a*gy-b*gyy-2.0*b*m2)
        dZc=s*(g2*dG-s*(m2*e+g_*b)-mdY-y*(cc+mdYY))
        dZcb=expand(C,dZc.astype(LOW),m16)
        dx2=dx2+nn(dZcb,ub)
        dz1=(dx2*S["G1"][st]+ds1*S["RPG2"][st]).astype(LOW)
        DZ1[st]=dz1
        DS1[st]=ds1; DS2[sl]=ds2; DG[sl]=dG
        hu=hu+tn(jnp.concatenate([expand(C,d2.astype(LOW),m16),dZcb],0),jnp.concatenate([dPb,x2j],0))
        hh2=hh2+jnp.sum(dZc,0,keepdims=True)
        next(side,None)
    dz1=DZ1[...]
    M=(nt(dz1,S["S1B"][...])*BLK[...]).astype(LOW)
    dG=DG[...]; dGg=dG*gam
    dk=collapse(C,nt(dz1,w1)-dk-nn(M,Kst)-tn(M,Kst),m16)+dGg
    dx_ref[o,:CH,:W]=S["DQ"][...]
    dx_ref[o,:CH,W:2*W]=dk.astype(LOW)
    dx_ref[o,:CH,2*W:]=(-dGg).astype(LOW)
    dr1=jnp.sum(DS1[...]*S["PG1"][...],-1,keepdims=True)
    dr2=DS2[...]*S["DB"][...]
    lane=lax.broadcasted_iota(jnp.int32,(CH,CH),1)
    dr=jnp.zeros((CH,CH),F)
    for c in range(C):
        rows=[dr1[B*(C*j+c):B*(C*j+c)+B] for j in range(NB)]
        col=jnp.concatenate(rows,0)+jnp.sum(jnp.where(m128[c],dr2,0.0),-1,keepdims=True)
        dr=jnp.where(lane==c,col,dr)
    R=S["R"][...]
    dr=dr*R*(1.0-R*(H/RATE_SCALE))
    db_ref[...]=db_ref[...]+jnp.sum(dr,0,keepdims=True)
    dr=dr.T.astype(LOW)
    extra=dx_ref.shape[1]-CH
    dx_ref[o,CH:,:]=jnp.zeros((extra,3*W),LOW)
    dx_ref[o,CH:,:CH]=dr[:extra]
    dgam_ref[...]=dgam_ref[...]+jnp.sum(dG*(2*S["YB"][...]*gam+S["T0"][...]),0,keepdims=True)
    dbet_ref[...]=dbet_ref[...]+jnp.sum(dGg,0,keepdims=True)
    dz1qb=S["DZ1Q"][...]
    H1[...]=H1[...]+tn(Kst,dz1)+tn(S["QST"][...],dz1qb)
    h1[...]=h1[...]+nn(sums,dz1)+nn(sums,dz1qb)
    HU[...]=hu+tn(S["DZQ"][...],S["X2Q"][...])
    h2[...]=hh2+jnp.sum(collapse(C,S["DZQ"][...].astype(F),m16),0,keepdims=True)

def bwd_kernel(C,H,steps,*refs):
    first,near,far=refs[:9],refs[9:18],refs[18:27]
    us_ref,w1_ref,own_ref,dx_ref,H1,h1,HU,h2,dgam_ref,dbet_ref,db_ref,TRI,BLK,BLKT,DZ1,DS1,DS2,DG=refs[27:45]
    k=len(SLOT)
    even=dict(zip(SLOT,refs[45:45+k])); odd=dict(zip(SLOT,refs[45+k:]))
    gam=pair_row(C,H,own_ref,1); bet=pair_row(C,H,own_ref,2)
    @pl.when(pl.program_id(0)==0)
    def _():
        for ref in (H1,h1,HU,h2,dgam_ref,dbet_ref,db_ref): ref[...]=jnp.zeros_like(ref)
        fill_masks(C,TRI,BLK,BLKT)
        for _ in bwd_pre(C,H,first,own_ref,even,TRI,BLKT,gam,bet,dgam_ref,dbet_ref,1.0): pass
    more=jnp.where(pl.program_id(0)<steps-1,1.0,0.0)
    side=bwd_pre(C,H,near,own_ref,odd,TRI,BLKT,gam,bet,dgam_ref,dbet_ref,1.0)
    bwd_steps(C,H,even,us_ref,1,w1_ref[1],H1,h1,HU,h2,BLK,gam,bet,dgam_ref,dbet_ref,DZ1,DS1,DS2,DG,dx_ref,db_ref,1,side)
    side=bwd_pre(C,H,far,own_ref,even,TRI,BLKT,gam,bet,dgam_ref,dbet_ref,more)
    bwd_steps(C,H,odd,us_ref,0,w1_ref[0],H1,h1,HU,h2,BLK,gam,bet,dgam_ref,dbet_ref,DZ1,DS1,DS2,DG,dx_ref,db_ref,0,side)

def bwd_scan(x,own,do,z1,p,zc,z1q,zq,us,w1s):
    n,tall,W=x.shape
    W//=3
    C=own.shape[0]; I=own.shape[2]; H=W//C
    full=lambda *s: pl.BlockSpec(s,lambda i:(0,)*len(s))
    sd=jax.ShapeDtypeStruct
    V=pltpu.VMEM
    m=C*CH
    def chunk(at):
        rows=lambda k,w: pl.BlockSpec((k,w),lambda i:(at(i),0))
        return [pl.BlockSpec((1,tall,3*W),lambda i:(at(i),0,0)),rows(CH,W),rows(m,I),rows(m,I),rows(CH,W),rows(m,I),rows(CH,W),
            pl.BlockSpec((1,1,W,I),lambda i:(at(i),0,0,0)),pl.BlockSpec((1,W,I),lambda i:(at(i),0,0))]
    ins=(x,do,z1,p,zc,z1q,zq,us,w1s)
    return pl.pallas_call(partial(bwd_kernel,C,H,n//2),grid=(n//2,),
        in_specs=chunk(lambda i:n-1)+chunk(lambda i:n-2-2*i)+chunk(lambda i:jnp.maximum(n-3-2*i,0))+[
            pl.BlockSpec((2,NB,W,I),lambda i:(n//2-1-i,0,0,0)),pl.BlockSpec((2,W,I),lambda i:(n//2-1-i,0,0)),full(*own.shape)],
        out_specs=[pl.BlockSpec((2,tall,3*W),lambda i:(n//2-1-i,0,0)),full(W,I),full(C,I),full(W,I),full(1,W),full(1,W),full(1,W),full(1,CH)],
        out_shape=[sd((n,tall,3*W),LOW),sd((W,I),F),sd((C,I),F),sd((W,I),F),sd((1,W),F),sd((1,W),F),sd((1,W),F),sd((1,CH),F)],
        scratch_shapes=[V((m,m),F),V((m,m),F),V((m,m),F),V((m,I),LOW),V((m,I),F),V((CH,W),F),V((CH,W),F)]+slot_shapes(C,W,I)*2,
        compiler_params=pltpu.CompilerParams(vmem_limit_bytes=48*1024*1024),
        cost_estimate=pl.CostEstimate(flops=1000,bytes_accessed=1000,transcendentals=0),
    )(*ins,*ins,*ins,us,w1s,own)

RATE_SCALE = 0.25
NORM_EPS = 1e-05


def smooth_act(value):
    return 0.5 * value * (1.0 + jnp.tanh(C0 * (value + C1 * value * value * value)))


def root_norm(value, gain):
    return value * lax.rsqrt(jnp.mean(value * value, -1, keepdims=True) + NORM_EPS) * gain


def layer_norm(value, gain, bias):
    centre = value - jnp.mean(value, -1, keepdims=True)
    return centre * lax.rsqrt(jnp.mean(centre * centre, -1, keepdims=True) + NORM_EPS) * gain + bias


def gated_branch(mixed, gate_pre, gain, bias):
    return layer_norm(mixed, gain, bias) * smooth_act(gate_pre)


def swish_product(gate_val, linear_val):
    return jax.nn.silu(gate_val) * linear_val


def matmul(left, right):
    return jnp.dot(left, right, preferred_element_type=F)


def flip(array, axis, mask):
    peers = lax.axis_size(axis)
    return lax.ppermute(array, axis, [(i, i ^ mask) for i in range(peers)])


def masks_of(axis):
    masks = []
    while 1 << len(masks) < lax.axis_size(axis):
        masks.append(1 << len(masks))
    return masks


def side(axis, mask):
    return (lax.axis_index(axis) // mask) % 2


def gather_near(array, axis):
    for mask in reversed(masks_of(axis)):
        array = jnp.concatenate([array, flip(array, axis, mask)], 0)
    return array


def scatter_once(array, axis, mask):
    half = array.shape[0] // 2
    return array[:half].astype(F) + flip(array[half:].astype(LOW), axis, mask).astype(F)


def scatter_near(array, axis):
    for mask in masks_of(axis):
        array = scatter_once(array, axis, mask)
    return array


def halve(array, axis, mask, dim):
    bit = side(axis, mask)
    mine = lax.dynamic_index_in_dim(array, bit, dim, keepdims=False)
    other = lax.dynamic_index_in_dim(array, 1 - bit, dim, keepdims=False)
    return mine.astype(F) + flip(other.astype(LOW), axis, mask).astype(F)


def double(array, axis, mask):
    got = flip(array, axis, mask)
    upper = side(axis, mask) == 1
    return jnp.stack([jnp.where(upper, got, array), jnp.where(upper, array, got)])


def params_kernel(f_ref, s_ref, fb_ref, sb_ref, g_ref, b_ref, r_ref, o_ref):
    heads, head, inner = f_ref.shape
    for i in range(heads):
        o_ref[i, :head] = f_ref[i]
        o_ref[i, head : 2 * head] = s_ref[i]
        o_ref[i, 2 * head :] = jnp.zeros((8, inner), F)
        o_ref[i, 2 * head : 2 * head + 1] = fb_ref[i : i + 1]
        small = [ref[i : i + 1] for ref in (sb_ref, g_ref, b_ref)]
        small.append(jnp.broadcast_to(r_ref[:, i : i + 1], (1, inner - 3 * head)))
        o_ref[i, 2 * head + 1 : 2 * head + 2] = jnp.concatenate(small, 1)


def pack_params(first_weight, *others):
    heads, head, inner = first_weight.shape
    return pl.pallas_call(
        params_kernel,
        in_specs=[pl.BlockSpec(memory_space=pltpu.VMEM)] * 7,
        out_specs=pl.BlockSpec(memory_space=pltpu.VMEM),
        out_shape=jax.ShapeDtypeStruct((heads, 2 * head + 8, inner), F),
    )(first_weight, *others)


def project_kernel(each, blocks, x_ref, g_ref, wq_ref, wk_ref, wv_ref, wr_ref, wg_ref, s_ref, n_ref, p_ref, LT):
    step = pl.program_id(0)
    rows, width = x_ref.shape
    span = wq_ref.shape[1]

    @pl.when(step == 0)
    def _():
        x = x_ref[...].astype(F)
        scale = lax.rsqrt(jnp.sum(x * x, -1, keepdims=True) * (1.0 / width) + NORM_EPS)
        n_ref[...] = (x * scale * g_ref[...][None]).astype(LOW)
        LT[...] = jnp.zeros_like(LT)
        LT[: wr_ref.shape[0]] = nt(wr_ref[...], n_ref[...]).astype(LOW).astype(F)

    normed = n_ref[...]
    extra = s_ref.shape[1] - rows
    s_ref[0, rows:, :] = jnp.zeros((extra, 3 * span), LOW)

    @pl.when(step < blocks)
    def _():
        for i, w_ref in enumerate((wq_ref, wk_ref, wv_ref)):
            s_ref[0, :rows, span * i : span * i + span] = nn(normed, w_ref[...]).astype(LOW)
        r = lax.broadcasted_iota(jnp.int32, (extra, rows), 0)
        c = lax.broadcasted_iota(jnp.int32, (extra, rows), 1)
        pick = jnp.where((r < each) & (c == step * each + r), 1.0, 0.0)
        s_ref[0, rows:, :rows] = nn(pick, LT[...]).astype(LOW)
        p_ref[...] = nn(normed, wg_ref[...])

    @pl.when(step >= blocks)
    def _():
        s_ref[0, :rows, :] = jnp.zeros((rows, 3 * span), LOW)


def project(x, gain, wq, wk, wv, wr, wg, seqs, each, extra):
    rows, width = x.shape
    span = each * (width // wr.shape[0])
    blocks = width // span
    column = pl.BlockSpec((width, span), lambda s: (0, jnp.minimum(s, blocks - 1)))
    full = lambda *shape: pl.BlockSpec(shape, lambda s: (0,) * len(shape))
    sd = jax.ShapeDtypeStruct
    return pl.pallas_call(
        partial(project_kernel, each, blocks),
        grid=(seqs,),
        in_specs=[full(rows, width), full(width), column, column, column, full(*wr.shape), column],
        out_specs=[
            pl.BlockSpec((1, rows + extra, 3 * span), lambda s: (s, 0, 0)),
            full(rows, width),
            pl.BlockSpec((rows, span), lambda s: (0, jnp.minimum(s, blocks - 1))),
        ],
        out_shape=[sd((seqs, rows + extra, 3 * span), LOW), sd((rows, width), LOW), sd((rows, width), F)],
        scratch_shapes=[pltpu.VMEM((128, 128), F)],
        compiler_params=pltpu.CompilerParams(vmem_limit_bytes=60 * 1024 * 1024),
    )(x, gain, wq, wk, wv, wr, wg)


def tokens_kernel(each, blocks, x_ref, g_ref, m_ref, b_ref, d_ref, wq_ref, wk_ref, wv_ref, wr_ref, wg_ref, o_ref, ACC, LG):
    step = pl.program_id(0)
    rows, width = x_ref.shape
    span = wq_ref.shape[1]
    extra = b_ref.shape[1] - rows

    @pl.when(step == 0)
    def _():
        ACC[...] = jnp.zeros_like(ACC)
        LG[...] = jnp.zeros_like(LG)

    @pl.when(step < blocks)
    def _():
        total = nt(d_ref[...], wg_ref[...])
        for i, w_ref in enumerate((wq_ref, wk_ref, wv_ref)):
            total = total + nt(b_ref[0, :rows, span * i : span * i + span], w_ref[...])
        ACC[...] = ACC[...] + total
        r = lax.broadcasted_iota(jnp.int32, (rows, extra), 0)
        c = lax.broadcasted_iota(jnp.int32, (rows, extra), 1)
        place = jnp.where((c < each) & (r == step * each + c), 1.0, 0.0)
        LG[...] = LG[...] + nn(place, b_ref[0, rows:, :rows])

    @pl.when(step == pl.num_programs(0) - 1)
    def _():
        heads = wr_ref.shape[0]
        x = x_ref[...].astype(F)
        scale = lax.rsqrt(jnp.sum(x * x, -1, keepdims=True) * (1.0 / width) + NORM_EPS)
        grad = (ACC[...] + nn(LG[...].T[:, :heads], wr_ref[...])) * g_ref[...][None]
        along = jnp.sum(x * grad, -1, keepdims=True) * (1.0 / width)
        o_ref[...] = m_ref[...] + scale * (grad - x * (scale * scale * along))


def tokens_back(x, gain, middle_grad, back, gate_low, wq, wk, wv, wr, wg, each):
    rows, width = x.shape
    seqs, tall, lanes = back.shape
    span = lanes // 3
    blocks = width // span
    column = pl.BlockSpec((width, span), lambda s: (0, jnp.minimum(s, blocks - 1)))
    full = lambda *shape: pl.BlockSpec(shape, lambda s: (0,) * len(shape))
    return pl.pallas_call(
        partial(tokens_kernel, each, blocks),
        grid=(blocks,),
        in_specs=[
            full(rows, width), full(width), full(rows, width),
            pl.BlockSpec((1, tall, lanes), lambda s: (s, 0, 0)),
            pl.BlockSpec((rows, span), lambda s: (0, s)),
            column, column, column, full(*wr.shape), column,
        ],
        out_specs=full(rows, width),
        out_shape=jax.ShapeDtypeStruct((rows, width), F),
        scratch_shapes=[pltpu.VMEM((rows, width), F), pltpu.VMEM((128, 128), F)],
        compiler_params=pltpu.CompilerParams(vmem_limit_bytes=16 * 1024 * 1024),
    )(x, gain, middle_grad, back, gate_low, wq, wk, wv, wr, wg)


def feed_kernel(a_ref, b_ref, c_ref, g_ref, l_ref, d_ref):
    unit = g_ref.shape[1]
    g_ref[...] = a_ref[0, :unit].astype(F).T
    l_ref[...] = b_ref[0, :unit].astype(F).T
    half = unit // 2
    for i in range(2):
        d_ref[half * i : half * i + half] = c_ref[i, unit : unit + half].astype(F)


def feed_outputs(fed, inner_units):
    seqs, tall, width = fed.shape
    steps = seqs // 2
    unit = inner_units // steps
    sd = jax.ShapeDtypeStruct
    return pl.pallas_call(
        feed_kernel,
        grid=(steps,),
        in_specs=[
            pl.BlockSpec((1, tall, width), lambda i: (i, 0, 0)),
            pl.BlockSpec((1, tall, width), lambda i: (i + steps, 0, 0)),
            pl.BlockSpec((2, tall, width), lambda i: (i, 0, 0)),
        ],
        out_specs=[
            pl.BlockSpec((width, unit), lambda i: (0, i)),
            pl.BlockSpec((width, unit), lambda i: (0, i)),
            pl.BlockSpec((unit, width), lambda i: (i, 0)),
        ],
        out_shape=[sd((width, inner_units), F)] * 2 + [sd((inner_units, width), F)],
        compiler_params=pltpu.CompilerParams(vmem_limit_bytes=16 * 1024 * 1024),
    )(fed, fed, fed)


def swapped(array):
    seqs = lax.axis_size("seq")
    array = array.reshape(seqs, -1, array.shape[-1])
    return lax.all_to_all(array, "seq", split_axis=0, concat_axis=0, tiled=True)


def summed(parts):
    return jnp.sum(parts.astype(F), 0).astype(LOW)


def share_rows(every_normed, back_sent, state_g, vectors, fed_parts, early, aside, heads, local_heads, head, weights_in):
    seqs, tps = lax.axis_size("seq"), lax.axis_size("tp")
    width = every_normed.shape[1]
    lanes = back_sent.shape[2]
    rows = every_normed.shape[0] // seqs
    span = lanes // 3
    each = span // head
    first_g, first_bias_g, second_g, second_bias_g, gain_g, shift_g, bias_g = state_g
    inner = first_g.shape[1]
    fed = lax.all_gather(summed(fed_parts), "seq", axis=0, tiled=False)
    early = lax.all_gather(summed(swapped(early)), "seq", axis=0, tiled=True)
    for mask in reversed(masks_of("tp")):
        early = double(early, "tp", mask)
    early = early.reshape(2, width, width).astype(F)
    back = lax.all_to_all(back_sent, "seq", split_axis=0, concat_axis=0, tiled=True)
    qkv_g = back_sent[:, :rows].reshape(seqs * rows, lanes)
    logit_g = back_sent[:, rows : rows + each, :rows].transpose(1, 0, 2).reshape(each, seqs * rows)
    columns = jnp.einsum("ld,le->de", every_normed, qkv_g, preferred_element_type=F)
    rate_column = jnp.einsum("el,ld->ed", logit_g, every_normed, preferred_element_type=F)
    first_g = first_g.reshape(each, head, inner)
    second_g = second_g.reshape(each, head, inner)
    second_g = second_g - jnp.mean(second_g, 1, keepdims=True)
    second_bias_g, gain_g, shift_g = [a.reshape(each, head) for a in (second_bias_g, gain_g, shift_g)]
    second_bias_g = second_bias_g - jnp.mean(second_bias_g, 1, keepdims=True)
    bias_g = bias_g[0, :each]
    tail = jnp.concatenate(
        [second_bias_g, gain_g, shift_g, jnp.pad(bias_g[:, None], ((0, 0), (0, inner - 3 * head - 1)))], -1
    )
    states = jnp.concatenate(
        [
            jnp.stack([first_g, second_g], 1),
            jnp.stack([first_bias_g, tail], 1)[:, :, None],
            jnp.zeros((each, 2, 7, inner), F),
        ],
        2,
    )
    state_rows = states.size // lanes // tps
    rate_rows = rate_column.size // lanes // tps
    vectors = jnp.concatenate([vectors, jnp.zeros_like(vectors[:1])], 0)
    vector_rows = vectors.size // lanes // tps
    rest = jnp.concatenate(
        [rate_column.reshape(tps, rate_rows, lanes), vectors.reshape(tps, vector_rows, lanes)], 1
    )
    late = jnp.concatenate(
        [
            columns.reshape(tps, width // tps, lanes),
            states.reshape(tps, state_rows, lanes),
            jnp.pad(rest, ((0, 0), (0, 16 - rate_rows - vector_rows), (0, 0))),
        ],
        1,
    )
    late = lax.psum_scatter(late.astype(LOW), "tp", scatter_dimension=0, tiled=True)
    late = lax.all_gather(late, ("seq", "tp"), axis=0, tiled=True).reshape((seqs, tps) + late.shape[1:])
    weights = late[:, :, : width // tps].reshape(seqs, tps, width // tps, 3, span)
    weights = weights.transpose(3, 1, 2, 0, 4).reshape(3, width, seqs * span)[:, :, :width].astype(F)
    states = late[:, :, width // tps : width // tps + state_rows].reshape(seqs * each, 2, head + 8, inner)[:heads]
    states = lax.dynamic_slice_in_dim(states, lax.axis_index("tp") * local_heads, local_heads, 0).astype(F)
    rest = late[:, :, width // tps + state_rows :]
    rate_weight_grad = rest[:, :, :rate_rows].reshape(seqs * each, width)[:heads].T.astype(F)
    vectors = rest[:, :, rate_rows : rate_rows + vector_rows].reshape(seqs, 4, width)
    vectors = jnp.sum(vectors.astype(F), 0)
    grads = (weights[0], weights[1], weights[2], early[1])
    norm_gain_grad = jnp.sum(sum(g * w.astype(F) for g, w in zip(grads, weights_in)), -1)
    head_w = (states[:, 0, :head], jnp.swapaxes(states[:, 1, :head], 1, 2))
    return weights, head_w, states[:, :, head], rate_weight_grad, vectors, fed, back, early, aside, norm_gain_grad


def pack_kernel(head, me_ref, n_ref, x_ref, w_ref, wb_ref, u_ref, ub_ref, g_ref, s_ref, r_ref, v_ref, keep_ref, sent_ref, COL, UC, SMALL):
    seqs, _, lanes = x_ref.shape
    rows = n_ref.shape[0] // seqs
    width = n_ref.shape[1]
    here = width // 4
    normed = n_ref[...]
    COL[...] = tn(normed, x_ref[:, :rows].reshape(seqs * rows, lanes))
    rate = jnp.zeros((16, width), F)
    for s in range(seqs):
        logit = x_ref[s, rows : rows + 16, :rows]
        rate = rate + nn(logit, n_ref[rows * s : rows * s + rows])
    SMALL[...] = jnp.zeros_like(SMALL)
    for c in range(2):
        lane = slice(head * c, head * c + head)
        u = u_ref[lane]
        UC[lane] = u - jnp.sum(u, 0, keepdims=True) * (1.0 / head)
        ub = ub_ref[:, lane]
        ub = ub - jnp.sum(ub, 1, keepdims=True) * (1.0 / head)
        for i in range(2):
            SMALL[2 * c, i : i + 1] = wb_ref[c : c + 1, 128 * i : 128 * i + 128]
        SMALL[2 * c + 1, 0:1] = jnp.concatenate([ub, g_ref[:, lane]], 1)
        SMALL[2 * c + 1, 1:2] = jnp.concatenate([s_ref[:, lane], jnp.broadcast_to(r_ref[:, c : c + 1], (1, head))], 1)
    for t in range(4):
        for i in range(3):
            at = (t % 2) * 384 + 128 * i
            SMALL[t, 2 + i : 3 + i] = rate[t // 2 : t // 2 + 1, at : at + 128]
        for i in range(5):
            k = 5 * t + i
            if k < 18:
                SMALL[t, 5 + i : 6 + i] = v_ref[k // 6 : k // 6 + 1, (k % 6) * 128 : (k % 6) * 128 + 128]
    for place, o in enumerate((0, 2, 1, 3)):
        out = (keep_ref, sent_ref)[place // 2].at[place % 2]
        t = me_ref[0] ^ o
        out[:here] = COL[pl.ds(pl.multiple_of(t * here, 16), here)].astype(LOW)
        for n in range(9):
            c, k, half = n // 4, (n // 2) % 2, n % 2
            if n < 8:
                tile = (w_ref, UC)[k][pl.ds(pl.multiple_of(head * c + 16 * t, 16), 16), 128 * half : 128 * half + 128]
            else:
                tile = SMALL[t]
            row, lane = here + 16 * (n // 3), 128 * (n % 3)
            out[row : row + 16, lane : lane + 128] = tile.astype(LOW)


def last_kernel(seqs, each, heads, local_heads, me_ref, *refs):
    ours = lax.rem(pl.program_id(0), 2) == lax.rem(me_ref[0], 2)

    @pl.when(ours)
    def _():
        last_part(seqs, each, heads, local_heads, me_ref, refs[0], refs[1], *refs[4:])

    @pl.when(jnp.logical_not(ours))
    def _():
        last_part(seqs, each, heads, local_heads, me_ref, refs[2], refs[3], *refs[4:])


def last_part(seqs, each, heads, local_heads, me_ref, a_ref, b_ref, wq_ref, wk_ref, wv_ref, wg_ref,
              q_ref, k_ref, v_ref, n_ref, f_ref, s_ref, r_ref, out_ref, gate_ref, gate_n_ref, ST):
    t = pl.program_id(0)
    cut = a_ref.shape[2]
    lanes = a_ref.shape[3]
    span = lanes // 3
    below = q_ref.shape[0] - cut

    def spot(s):
        return s % 2, ((s >> 1) & 1) * 2 + (s >> 2)

    for s in range(seqs):
        if s * each >= heads:
            continue
        x, q = spot(s)
        for i, o_ref in enumerate((q_ref, k_ref, v_ref)):
            o_ref[:cut, span * s : span * s + span] = a_ref[0, 4 * x + q, :, span * i : span * i + span].astype(F)
            o_ref[cut:, span * s : span * s + span] = b_ref[x, 0, q, :below, span * i : span * i + span].astype(F)
    total = q_ref[...] * wq_ref[...].astype(F)
    for o_ref, w_ref in ((k_ref, wk_ref), (v_ref, wv_ref)):
        total = total + o_ref[...] * w_ref[...].astype(F)
    n_ref[...] = jnp.sum(total, -1, keepdims=True)

    def tile(x, q, n):
        row, lane = below + 16 * (n // 3), 128 * (n % 3)
        return b_ref[x, 0, q, row : row + 16, lane : lane + 128].astype(F)

    for i in range(local_heads):
        h = me_ref[0] * local_heads + i
        s = h // each
        upper = lax.rem(h, each) == 1
        x = lax.rem(s, 2)
        q = lax.rem(s // 2, 2) * 2 + s // 4
        for k in range(2):
            for j in range(2):
                ST[i, k, pl.ds(pl.multiple_of(16 * t, 16), 16), 128 * j : 128 * j + 128] = jnp.where(
                    upper, tile(x, q, 4 + k * 2 + j), tile(x, q, k * 2 + j)
                )
    for s in range(seqs):
        r_ref[0, s] = tile(*spot(s), 8)

    first = below + 48
    tall = out_ref.shape[0] // seqs

    def square(o_ref):
        for s in range(seqs):
            x, q = spot(s)
            for i in range(2):
                row = first + tall * i
                o_ref[tall * s : tall * s + tall, lanes * i : lanes * i + lanes] = b_ref[x, 0, q, row : row + tall].astype(F)

    @pl.when(t == 3)
    def _():
        for i in range(local_heads):
            f_ref[i] = ST[i, 0]
            s_ref[i] = ST[i, 1]

    @pl.when(t % 2 == 0)
    def _():
        square(out_ref)

    @pl.when(t % 2 == 1)
    def _():
        square(gate_ref)
        gate_n_ref[...] = jnp.sum(gate_ref[...] * wg_ref[...].astype(F), -1, keepdims=True)


def share_tiles(every_normed, back_sent, state_g, vectors, fed_parts, early, aside, heads, local_heads, head, weights_in):
    seqs, tps = lax.axis_size("seq"), lax.axis_size("tp")
    width = every_normed.shape[1]
    lanes = back_sent.shape[2]
    each = 2
    inner = state_g[0].shape[1]
    here = width // tps
    share = here + 48
    me = lax.axis_index("tp").astype(jnp.int32).reshape(1)
    sd = jax.ShapeDtypeStruct
    late, late_sent = pl.pallas_call(
        partial(pack_kernel, head),
        in_specs=[pl.BlockSpec(memory_space=pltpu.SMEM)] + [pl.BlockSpec(memory_space=pltpu.VMEM)] * 10,
        out_specs=[pl.BlockSpec(memory_space=pltpu.VMEM)] * 2,
        out_shape=[sd((2, share, lanes), LOW)] * 2,
        scratch_shapes=[
            pltpu.VMEM((width, lanes), F),
            pltpu.VMEM((each * head, inner), F),
            pltpu.VMEM((4, 16, 128), F),
        ],
        compiler_params=pltpu.CompilerParams(vmem_limit_bytes=20 * 1024 * 1024),
    )(me, every_normed, back_sent, *state_g, vectors)
    late = late.astype(F) + flip(late_sent, "tp", 1).astype(F)
    late = scatter_once(late, "tp", 2).astype(LOW)[0]
    early = summed(swapped(early))
    late = jnp.concatenate([late, early[:, :lanes], early[:, lanes:]], 0)
    share = late.shape[0]
    late = double(late, "seq", 4)
    late, fed = lax.optimization_barrier((late, summed(fed_parts)))
    fed = lax.all_gather(fed, "seq", axis=0, tiled=False)
    late = double(late, "seq", 2)
    back = lax.all_to_all(back_sent, "seq", split_axis=0, concat_axis=0, tiled=True)
    cut = 160
    part_a, part_b = late[:, :, :cut], late[:, :, cut:]
    part_a, part_b = double(part_a, "seq", 1), double(part_b, "tp", 2)
    part_a, part_b = double(part_a, "tp", 2), double(part_b, "seq", 1)
    part_a, part_b, fed, back, aside = lax.optimization_barrier((part_a, part_b, fed, back, aside))
    part_a = part_a.reshape(2, seqs, cut, lanes)
    part_b = part_b.reshape(2, 2, seqs // 2, share - cut, lanes)
    got_a, got_b = flip(part_a, "tp", 1), flip(part_b, "tp", 1)
    a_spec = pl.BlockSpec((1, seqs, cut, lanes), lambda t: (t // 2, 0, 0, 0))
    b_spec = pl.BlockSpec((2, 1, seqs // 2, share - cut, lanes), lambda t: (0, t // 2, 0, 0, 0))
    square = pl.BlockSpec((here, width), lambda t: (t, 0))
    taller = pl.BlockSpec((2 * here, width), lambda t: (t // 2, 0))
    *weights, norm_gain_grad, head_f, head_s, small, out_g, gate_g, gate_n = pl.pallas_call(
        partial(last_kernel, seqs, each, heads, local_heads),
        grid=(tps,),
        in_specs=[
            pl.BlockSpec(memory_space=pltpu.SMEM),
            a_spec, b_spec, a_spec, b_spec, square, square, square, taller,
        ],
        out_specs=[
            square, square, square,
            pl.BlockSpec((here, 1), lambda t: (t, 0)),
            pl.BlockSpec((local_heads, head, inner), lambda t: (0, 0, 0)),
            pl.BlockSpec((local_heads, head, inner), lambda t: (0, 0, 0)),
            pl.BlockSpec((1, seqs, 16, 128), lambda t: (t, 0, 0, 0)),
            taller, taller,
            pl.BlockSpec((2 * here, 1), lambda t: (t // 2, 0)),
        ],
        out_shape=[sd((width, width), F)] * 3
        + [sd((width, 1), F), sd((local_heads, head, inner), F), sd((local_heads, head, inner), F)]
        + [sd((tps, seqs, 16, 128), F)]
        + [sd((width, width), F)] * 2
        + [sd((width, 1), F)],
        scratch_shapes=[pltpu.VMEM((local_heads, 2, head, inner), F)],
        compiler_params=pltpu.CompilerParams(vmem_limit_bytes=48 * 1024 * 1024),
    )(me, part_a, part_b, got_a, got_b, *weights_in)
    norm_gain_grad = norm_gain_grad + gate_n
    head_t = small[:, :, :2].transpose(1, 0, 2, 3).reshape(seqs * each, 2, inner)
    head_t = lax.dynamic_slice_in_dim(head_t, me[0] * local_heads, local_heads, 0)
    rate_weight_grad = small[:, :, 2:5].transpose(1, 0, 2, 3).reshape(seqs * each, width)[:heads].T
    vectors = jnp.sum(small[:, :, 5:10], 1).reshape(-1)[: 3 * width].reshape(3, width)
    return weights, (head_f, jnp.swapaxes(head_s, 1, 2)), head_t, rate_weight_grad, vectors, fed, back, (out_g, gate_g), aside, norm_gain_grad[:, 0]


def on_device(
    tokens, norm_gain, query_weight, key_weight, value_weight, rate_weight, rate_bias,
    first_weight, first_bias, second_weight, second_bias, inner_gain, inner_bias,
    branch_gate, output_weight, post_gain, post_bias, feed_gain, feed_gate, feed_linear,
    feed_down, cotangent,
):
    seqs = lax.axis_size("seq")
    rank = lax.axis_index("seq")
    heads = rate_weight.shape[1]
    local_heads, head, inner = first_weight.shape
    rows = tokens.shape[1]
    width = tokens.shape[2]
    each = -(-heads // seqs)
    span = each * head
    length = seqs * rows
    extra = -(-each // 16) * 16

    def to_chains(array):
        padded = jnp.pad(array, ((0, 0), (0, seqs * span - array.shape[1])))
        return padded.reshape(rows, seqs, span).transpose(1, 0, 2)

    def from_chains(array):
        return array.transpose(1, 0, 2).reshape(rows, seqs * span)[:, :width]

    def swap(array):
        return lax.all_to_all(array, "seq", split_axis=0, concat_axis=0, tiled=True)

    packed = pack_params(
        first_weight, jnp.swapaxes(second_weight, 1, 2), first_bias, second_bias, inner_gain, inner_bias, rate_bias[None]
    )
    every = lax.all_gather(packed, "tp", axis=0, tiled=True)
    own = lax.dynamic_slice_in_dim(every, jnp.minimum(rank * each, heads - each), each, 0)

    residual = tokens[0].astype(F)
    normed_val, norm_pull = jax.vjp(root_norm, residual, norm_gain)
    down_grad = cotangent[0]
    grad_out = down_grad.astype(F)
    every_grad = gather_near(down_grad, "tp")
    if span % 128 == 0 and width % span == 0 and rows == 128:
        sent, normed, gate_pre = project(
            tokens[0], norm_gain, query_weight, key_weight, value_weight, rate_weight.T, branch_gate, seqs, each, extra
        )
    else:
        normed = normed_val.astype(LOW)
        query_tok = matmul(normed, query_weight).astype(LOW)
        keys_tok = matmul(normed, key_weight).astype(LOW)
        values_tok = matmul(normed, value_weight).astype(LOW)
        logits_tok = matmul(normed, rate_weight).astype(LOW)
        gate_pre = matmul(normed, branch_gate)
        logit_rows = jnp.pad(logits_tok.T, ((0, seqs * each - heads), (0, 0))).reshape(seqs, each, rows)
        logit_rows = jnp.pad(logit_rows, ((0, 0), (0, extra - each), (0, 3 * span - rows)))
        sent = [to_chains(query_tok), to_chains(keys_tok), to_chains(values_tok)]
        sent = jnp.concatenate([jnp.concatenate(sent, -1), logit_rows], 1)
    got = swap(sent)

    every_normed = lax.all_gather(normed, "seq", axis=0, tiled=True)
    outs, *kept = fwd_scan(got, own)
    outs, every_normed, every_grad = lax.optimization_barrier((outs, every_normed, every_grad))
    mixed_tok = from_chains(swap(outs.reshape(seqs, rows, span))).astype(F)

    branch_val, branch_pull = jax.vjp(gated_branch, mixed_tok, gate_pre, post_gain, post_bias)
    branch_in = branch_val.astype(LOW)
    middle = residual + matmul(branch_in, output_weight)
    feed_val, feed_pull = jax.vjp(root_norm, middle, feed_gain)
    feed_in = feed_val.astype(LOW)
    every_in = gather_near(feed_in, "tp")
    gate_val = matmul(every_in, feed_gate)
    linear_val = matmul(every_in, feed_linear)
    act_val, act_pull = jax.vjp(swish_product, gate_val, linear_val)
    hidden = act_val.astype(LOW)

    hidden_grad = jnp.einsum("td,fd->tf", every_grad, feed_down, preferred_element_type=F)
    gate_grad, linear_grad = act_pull(hidden_grad)
    gate_low = gate_grad.astype(LOW)
    linear_low = linear_grad.astype(LOW)
    input_part = jnp.einsum("tf,df->td", gate_low, feed_gate, preferred_element_type=F) + jnp.einsum(
        "tf,df->td", linear_low, feed_linear, preferred_element_type=F
    )
    feed_down_grad = jnp.einsum("tf,td->fd", hidden, every_grad, preferred_element_type=F)
    both_low = jnp.concatenate([gate_low, linear_low], 1)
    feed_both_grad = jnp.einsum("tf,td->fd", both_low, every_in, preferred_element_type=F)
    fed_parts = jnp.concatenate(
        [
            feed_both_grad.astype(LOW).reshape(seqs, -1, width),
            feed_down_grad.astype(LOW).reshape(seqs, -1, width),
        ],
        1,
    )
    feed_in_grad = input_part
    for mask in masks_of("tp"):
        half = feed_in_grad.shape[0] // 2
        arrived = flip(feed_in_grad[half:].astype(LOW), "tp", mask)
        if mask == masks_of("tp")[-1]:
            arrived, fed_parts = lax.optimization_barrier((arrived, fed_parts))
        feed_in_grad = feed_in_grad[:half].astype(F) + arrived.astype(F)
    middle_part, feed_gain_grad = feed_pull(feed_in_grad)
    middle_grad = grad_out + middle_part
    out_low = middle_grad.astype(LOW)
    branch_grad = jnp.einsum("te,de->td", out_low, output_weight, preferred_element_type=F)
    mixed_grad, gate_pre_grad, post_gain_grad, post_bias_grad = branch_pull(branch_grad)
    out_grad_c = swap(to_chains(mixed_grad.astype(LOW))).reshape(length, span)

    second_part = matmul(hidden, feed_down).astype(LOW)
    second_part, out_grad_c = lax.optimization_barrier((second_part, out_grad_c))
    second_out = scatter_near(second_part, "tp")
    result = (middle + second_out).astype(LOW)[None]

    gate_low_pre = gate_pre_grad.astype(LOW)
    out_low, gate_low_pre, out_grad_c = lax.optimization_barrier((out_low, gate_low_pre, out_grad_c))
    tps = lax.axis_size("tp")
    lefts = jnp.stack([branch_in, normed])
    rights = jnp.stack([out_low, gate_low_pre])
    part_rows = 2 * width // tps
    orders = [0]
    for mask in reversed(masks_of("tp")):
        orders = orders + [o + mask for o in orders]
    parts = []
    for o in orders:
        owner = lax.axis_index("tp") ^ o
        which, place = owner % 2, owner // 2
        left = lax.dynamic_slice(lefts, (which, 0, place * part_rows), (1, rows, part_rows))
        right = lax.dynamic_index_in_dim(rights, which, 0, keepdims=True)
        parts.append((left, right))
    half = tps // 2

    def products(chosen):
        left = jnp.concatenate([p[0] for p in chosen], 0)
        right = jnp.concatenate([p[1] for p in chosen], 0)
        return jnp.einsum("jtd,jte->jde", left, right, preferred_element_type=F)

    early_sent = products(parts[half:]).astype(LOW)
    early = products(parts[:half]) + flip(early_sent, "tp", 1).astype(F)
    fed_parts, early, out_grad_c = lax.optimization_barrier((fed_parts, early.astype(LOW), out_grad_c))
    fed_parts = swap(fed_parts)
    for mask in masks_of("tp")[1:]:
        early = scatter_once(early, "tp", mask)

    back_sent, *state_g = bwd_scan(got, own, out_grad_c, *kept)
    early, fed_parts, back_sent = lax.optimization_barrier((early.astype(LOW), fed_parts, back_sent))
    vectors = jnp.stack([post_gain_grad, post_bias_grad, feed_gain_grad])
    share = share_tiles if each == 2 and tps == 4 and seqs == 8 else share_rows
    weights, head_w, head_t, rate_weight_grad, vectors, fed, back, early, result, norm_gain_grad = share(
        every_normed, back_sent, state_g, vectors, fed_parts, early, result, heads, local_heads, head,
        (query_weight, key_weight, value_weight, branch_gate),
    )
    if span % 128 == 0 and width % span == 0 and rows == 128:
        tokens_grad = tokens_back(
            tokens[0], norm_gain, middle_grad, back, gate_low_pre,
            query_weight, key_weight, value_weight, rate_weight.T, branch_gate, each,
        )[None]
    else:
        query_low = from_chains(back[:, :rows, :span])
        keys_low = from_chains(back[:, :rows, span : 2 * span])
        values_low = from_chains(back[:, :rows, 2 * span :])
        logit_low = back[:, rows : rows + each, :rows].reshape(seqs * each, rows)[:heads].T

        normed_grad = (
            jnp.einsum("te,de->td", query_low, query_weight, preferred_element_type=F)
            + jnp.einsum("te,de->td", keys_low, key_weight, preferred_element_type=F)
            + jnp.einsum("te,de->td", values_low, value_weight, preferred_element_type=F)
            + jnp.einsum("te,de->td", logit_low, rate_weight, preferred_element_type=F)
            + jnp.einsum("te,de->td", gate_low_pre, branch_gate, preferred_element_type=F)
        )
        residual_part, unused = norm_pull(normed_grad)
        tokens_grad = (middle_grad + residual_part)[None]
    inner_units = feed_gate.shape[1]
    if 2 * inner_units // seqs % 128 == 0:
        fed_grads = feed_outputs(fed, inner_units)
    else:
        both = fed[:, : 2 * inner_units // seqs].reshape(2, inner_units, width).astype(F)
        down = fed[:, 2 * inner_units // seqs : 3 * inner_units // seqs].reshape(inner_units, width).astype(F)
        fed_grads = (both[0].T, both[1].T, down)
    norm_gain_grad = norm_gain_grad + jnp.sum(rate_weight_grad * rate_weight.astype(F), -1)
    norm_gain_grad = norm_gain_grad / norm_gain
    tail_sum = head_t[:, 1]
    return (
        result,
        tokens_grad,
        norm_gain_grad,
        weights[0],
        weights[1],
        weights[2],
        rate_weight_grad,
        tail_sum[:, 3 * head],
        head_w[0],
        head_t[:, 0],
        head_w[1],
        tail_sum[:, :head],
        tail_sum[:, head : 2 * head],
        tail_sum[:, 2 * head : 3 * head],
        early[1],
        early[0],
        vectors[0],
        vectors[1],
        vectors[2],
        *fed_grads,
    )


def solution(mesh):
    in_specs = (
        P("tp", "seq", None),
        P(),
        P(),
        P(),
        P(),
        P(),
        P("tp"),
        P("tp", None, None),
        P("tp", None),
        P("tp", None, None),
        P("tp", None),
        P("tp", None),
        P("tp", None),
        P(),
        P(),
        P(),
        P(),
        P(),
        P(None, "tp"),
        P(None, "tp"),
        P("tp", None),
        P("tp", "seq", None),
    )
    out_specs = (
        P("tp", "seq", None),
        P("tp", "seq", None),
        P(),
        P(),
        P(),
        P(),
        P(),
        P("tp"),
        P("tp", None, None),
        P("tp", None),
        P("tp", None, None),
        P("tp", None),
        P("tp", None),
        P("tp", None),
        P(),
        P(),
        P(),
        P(),
        P(),
        P(None, "tp"),
        P(None, "tp"),
        P("tp", None),
    )
    return jax.shard_map(
        on_device, mesh=mesh, in_specs=in_specs, out_specs=out_specs, check_vma=False
    )
```
